128 devices in a mesh: fsdp: 16 (over y_hi, x, core), tp: 8 (over y_lo, z).
Axes of the slice: x: 4, y: 4 (y_hi: 2, y_lo: 2; y = y_hi * 2 + y_lo), z: 4, core: 2. Of those that a mesh axis runs over, the one named last changes fastest.
Arguments:
- tokens: bfloat16 [12288, 3584], P('fsdp', 'tp'), may hold values from -6 to 6
- gate_master: float32 [3584, 9216], P('fsdp', 'tp'), may hold values from -0.09375 to 0.09375
- up_master: float32 [3584, 9216], P('fsdp', 'tp'), may hold values from -0.09375 to 0.09375
- down_master: float32 [9216, 3584], P('fsdp', 'tp'), may hold values from -0.0625 to 0.0625
Outputs:
- mixed: bfloat16 [12288, 3584], P('fsdp', 'tp')
- log_amax: float32 [3, 28, 72], replicated
The draws below stay inside these ranges and needn't reach their ends.
All inputs are finite; a program needn't handle non-finite values.
Results may differ from the reference program's by a relative error of at most 0.0071.
Values may be sent and summed in bfloat16 or wider, within the bound.
No kernel may reach another device: no remote copies, remote signals or barrier semaphores. Data moves between devices by JAX's collectives and lax.ppermute only.
A program may use at most 192 MiB of HBM per device.

```python
import jax
import jax.numpy as jnp
from jax import lax

D = 3584
FF = 9216
BLOCK = 128
TOKENS = 12288


def block_levels(key, extent, split, low, top_value):
    def one(dim, blocks):
        heights = jax.random.uniform(jax.random.fold_in(jax.random.fold_in(key, 6), dim), (blocks,), jnp.float32, low / len(split), top_value / len(split))
        return jnp.repeat(jnp.exp(heights), extent[dim] // blocks).reshape((-1,) + (1,) * (len(extent) - dim - 1))

    gain = one(*split[0])
    for cut in split[1:]:
        gain = gain * one(*cut)
    return gain


def bell_draw(stream_key, shape, deviation, limit, cuts=(), kind=jnp.bfloat16):
    array = jax.random.normal(stream_key, shape, jnp.float32) * deviation
    if len(cuts) > 0:
        array = block_levels(stream_key, shape, cuts, -0.22, 0.18) * array
    return jnp.clip(array, min=-limit, max=limit).astype(kind)


def setup_inputs(seed: int = 0) -> dict:
    keys = jax.random.split(jax.random.key(seed), 5)
    return {
        "tokens": bell_draw(keys[0], (TOKENS, D), 1.0, 6.0, ((0, 16), (1, 8))),
        "gate_master": bell_draw(keys[1], (D, FF), D ** -0.5, 0.09375, ((0, 16), (1, 8)), jnp.float32),
        "up_master": bell_draw(keys[2], (D, FF), D ** -0.5, 0.09375, ((0, 16), (1, 8)), jnp.float32),
        "down_master": bell_draw(keys[3], (FF, D), FF ** -0.5, 0.0625, ((0, 16), (1, 8)), jnp.float32),
    }


FP8_MAX = 448.0
EPS = 1e-6
SMALLEST_NORMAL = 2.0 ** -6


def snapped(value):
    magnitude = jnp.abs(value)
    exponent = jnp.floor(jnp.log2(jnp.maximum(magnitude, SMALLEST_NORMAL)))
    step_size = jnp.exp2(exponent - 3.0)
    return jnp.sign(value) * step_size * jnp.floor(magnitude / step_size + 0.5)


def block_amax(master):
    height, breadth = master.shape
    blocks = jnp.abs(master).reshape(height // BLOCK, BLOCK, breadth // BLOCK, BLOCK)
    return jnp.max(blocks, axis=(1, 3))


def rollout(master):
    amax = block_amax(master)
    scale = (amax + EPS) / FP8_MAX
    spread_scale = jnp.repeat(jnp.repeat(scale, BLOCK, axis=0), BLOCK, axis=1)
    coded = snapped(master / spread_scale).astype(jnp.bfloat16)
    coded = lax.optimization_barrier(coded)
    return (coded.astype(jnp.float32) * spread_scale).astype(jnp.bfloat16), amax


def reference(tokens, gate_master, up_master, down_master):
    gate_weight, gate_amax = rollout(gate_master)
    up_weight, up_amax = rollout(up_master)
    down_weight, down_amax = rollout(down_master)
    log_amax = jnp.stack([jnp.log(gate_amax + EPS), jnp.log(up_amax + EPS), jnp.log(down_amax + EPS).T])
    gate = jnp.dot(tokens, gate_weight, preferred_element_type=jnp.float32)
    up = jnp.dot(tokens, up_weight, preferred_element_type=jnp.float32)
    hidden = (jax.nn.silu(gate) * up).astype(jnp.bfloat16)
    mixed = jnp.dot(hidden, down_weight, preferred_element_type=jnp.float32).astype(jnp.bfloat16)
    return mixed, log_amax
```

```python
import functools

import jax
import jax.numpy as jnp
from jax import lax
from jax.experimental import pallas as pl
from jax.experimental.layout import Layout, with_layout_constraint
from jax.experimental.pallas import tpu as pltpu
from jax.sharding import PartitionSpec as P

D = 3584
FF = 9216
BLOCK = 128

FP8_MAX = 448.0
EPS = 1e-06
SMALLEST_NORMAL = 2.0 ** (-6)
AXES = ("fsdp", "tp")
VMEM_LIMIT = 56 * 1024 * 1024
TILE = 384


def snapped(value):
    magnitude = jnp.abs(value)
    exponent = jnp.floor(jnp.log2(jnp.maximum(magnitude, SMALLEST_NORMAL)))
    step_size = jnp.exp2(exponent - 3.0)
    return jnp.sign(value) * step_size * jnp.floor(magnitude / step_size + 0.5)


def place(y, x, core, z):
    y, x, z = y % 4, x % 4, z % 4
    return (((y // 2) * 4 + x) * 2 + core) * 8 + (y % 2) * 4 + z


def send(array, target):
    pairs = [
        (place(y, x, core, z), place(*target(y, x, core, z)))
        for y in range(4)
        for x in range(4)
        for core in range(2)
        for z in range(4)
    ]
    return lax.ppermute(array, AXES, pairs)


def x_up(y, x, core, z):
    return y, x + 1, core, z


def x_down(y, x, core, z):
    return y, x - 1, core, z


def y_far(y, x, core, z):
    return y + 2, x, core, z


def other_core(y, x, core, z):
    return y, x, 1 - core, z


def to_ff_group(y, x, core, z):
    y_hi, y_lo = y // 2, y % 2
    return (y_lo ^ y_hi) * 2 + y_hi, z - x, core, x


def to_chunk(dy, dx):
    def target(y, x, core, z):
        y_hi, y_lo = y // 2, y % 2
        return y_hi * 2 + (y_lo ^ y_hi ^ dy), x, core, z + x + dx

    return target


def block_maxima(local, row_start, column_start, rows, columns):
    height, breadth = local.shape
    span_rows = (height - 1) // BLOCK + 2
    span_columns = (breadth - 1) // BLOCK + 2
    magnitude = jnp.abs(local)
    which_row = (row_start % BLOCK + jnp.arange(height, dtype=jnp.int32)) // BLOCK
    by_row = jnp.stack(
        [
            jnp.max(jnp.where((which_row == k)[:, None], magnitude, 0.0), axis=0)
            for k in range(span_rows)
        ]
    )
    which_column = (column_start % BLOCK + jnp.arange(breadth, dtype=jnp.int32)) // BLOCK
    pick = which_column[None, :] == jnp.arange(span_columns, dtype=jnp.int32)[:, None]
    part = jnp.max(jnp.where(pick[None], by_row[:, None, :], 0.0), axis=2)
    table = jnp.zeros((rows // BLOCK + span_rows, columns // BLOCK + span_columns), jnp.float32)
    return lax.dynamic_update_slice(table, part, (row_start // BLOCK, column_start // BLOCK))


def spread(scales, row_start, height, column_start, breadth):
    span_rows = (height - 1) // BLOCK + 2
    span_columns = (breadth - 1) // BLOCK + 2
    near = lax.dynamic_slice(
        scales, (row_start // BLOCK, column_start // BLOCK), (span_rows, span_columns)
    )
    which_row = (row_start % BLOCK + jnp.arange(height, dtype=jnp.int32)) // BLOCK
    which_column = (column_start % BLOCK + jnp.arange(breadth, dtype=jnp.int32)) // BLOCK
    wide = jnp.zeros((span_rows, breadth), jnp.float32)
    for k in range(span_columns):
        wide = jnp.where((which_column == k)[None, :], near[:, k : k + 1], wide)
    full = jnp.zeros((height, breadth), jnp.float32)
    for k in range(span_rows):
        full = jnp.where((which_row == k)[:, None], wide[k : k + 1, :], full)
    return full


def rollout(master, table, row_start, column_start):
    height, breadth = master.shape
    scale = spread((table + EPS) / FP8_MAX, row_start, height, column_start, breadth)
    return (snapped(master / scale) * scale).astype(jnp.bfloat16)


ORDER = ((0, 0), (1, 0), (0, -1), (0, 1), (1, -1), (1, 1), (0, 2), (1, 2))


def gathered(own):
    far = send(own, y_far)
    own_l, own_r = send(own, x_up), send(own, x_down)
    far_l, far_r = send(far, x_up), send(far, x_down)
    own_ll = send(own_l, x_up)
    far_rr = send(far_r, x_down)
    pairs = [
        jnp.stack(pair)
        for pair in ((own, far), (own_l, own_r), (far_l, far_r), (own_ll, far_rr))
    ]
    return [(pair, send(pair, other_core)) for pair in pairs]


def merge(scratch, core, mine, theirs):
    half = mine.shape[0]
    scratch[:half] = jnp.where(core == 0, mine, theirs)
    scratch[half:] = jnp.where(core == 0, theirs, mine)


def token_kernel(pairs, has_before, has_gate, info, tokens, *refs):
    refs = list(refs)
    before = refs.pop(0) if has_before else None
    gate = refs.pop(0) if has_gate else None
    *blocks, out, scratch = refs
    for n in range(len(pairs)):
        for k in range(2):
            merge(scratch.at[2 * n + k], info[8], blocks[2 * n][k], blocks[2 * n + 1][k])

    @pl.loop(0, tokens.shape[1] // TILE)
    def _(m):
        rows = pl.ds(pl.multiple_of(m * TILE, TILE), TILE)
        total = before[rows, :] if has_before else None
        for n, pair in enumerate(pairs):
            for k in range(2):
                product = jnp.dot(
                    tokens[info[2 * pair + k], rows, :],
                    scratch[2 * n + k],
                    preferred_element_type=jnp.float32,
                )
                total = product if total is None else total + product
        if has_gate:
            value = gate[rows, :]
            total = value / (1.0 + jnp.exp(-value)) * total
        out[rows, :] = total.astype(out.dtype)


def vmem(n):
    return [pl.BlockSpec(memory_space=pltpu.VMEM)] * n


def token_sum(info, tokens, pairs, blocks, before=None, gate=None):
    rows, columns = tokens.shape[1], blocks[0].shape[2]
    depth = blocks[0].shape[1] * 2
    operands = [tokens] + [a for a in (before, gate) if a is not None] + list(blocks)
    return pl.pallas_call(
        functools.partial(token_kernel, pairs, before is not None, gate is not None),
        out_shape=jax.ShapeDtypeStruct(
            (rows, columns), jnp.float32 if gate is None else jnp.bfloat16
        ),
        in_specs=[pl.BlockSpec(memory_space=pltpu.SMEM)] + vmem(len(operands)),
        out_specs=pl.BlockSpec(memory_space=pltpu.VMEM),
        scratch_shapes=[pltpu.VMEM((2 * len(pairs), depth, columns), jnp.bfloat16)],
        compiler_params=pltpu.CompilerParams(vmem_limit_bytes=VMEM_LIMIT),
        cost_estimate=pl.CostEstimate(
            flops=2 * rows * columns * depth * 2 * len(pairs),
            bytes_accessed=rows * columns * 8,
            transcendentals=0,
        ),
    )(info, *operands)


def down_kernel(info, hidden, mine, theirs, out_a, out_b):
    for k, out in enumerate((out_a, out_b)):
        low = jnp.where(info[8] == 0, mine[k], theirs[k])
        high = jnp.where(info[8] == 0, theirs[k], mine[k])
        out[...] = lax.dot_general(
            jnp.concatenate([low, high], axis=1),
            hidden[...],
            (((1,), (1,)), ((), ())),
            preferred_element_type=jnp.float32,
        ).astype(out.dtype)


def down_terms(info, hidden, mine, theirs):
    rows, depth = hidden.shape
    columns = mine.shape[1]
    shape = jax.ShapeDtypeStruct((columns, rows), jnp.bfloat16)
    return pl.pallas_call(
        down_kernel,
        out_shape=(shape, shape),
        in_specs=[pl.BlockSpec(memory_space=pltpu.SMEM)] + vmem(3),
        out_specs=vmem(2),
        compiler_params=pltpu.CompilerParams(vmem_limit_bytes=VMEM_LIMIT),
        cost_estimate=pl.CostEstimate(
            flops=4 * rows * columns * depth, bytes_accessed=rows * columns * 4, transcendentals=0
        ),
    )(info, hidden, mine, theirs)


def on_device(tokens, gate_master, up_master, down_master):
    fsdp_place = lax.axis_index("fsdp")
    tp_place = lax.axis_index("tp")
    gate_height, gate_breadth = gate_master.shape
    down_height, down_breadth = down_master.shape
    gate_at = (fsdp_place * gate_height, tp_place * gate_breadth)
    down_at = (fsdp_place * down_height, tp_place * down_breadth)

    by_rows = Layout(major_to_minor=(0, 1))
    whole = lax.all_gather(with_layout_constraint(tokens, by_rows), "tp")

    tables = [
        block_maxima(gate_master, *gate_at, D, FF),
        block_maxima(up_master, *gate_at, D, FF),
        block_maxima(down_master, *down_at, FF, D),
    ]
    rows = D // BLOCK + 12
    columns = FF // BLOCK + 16
    pad = lambda a: jnp.pad(a, ((0, rows - a.shape[0]), (0, columns - a.shape[1])))
    table = jnp.concatenate([pad(tables[0]), pad(tables[1]), pad(tables[2].T)])

    def step(table, target):
        return jnp.maximum(table, send(table, target))

    table = step(table, other_core)
    table = step(table, lambda y, x, core, z: (y, x ^ 1, core, z))
    gate_weight = rollout(gate_master, table[:rows], *gate_at)
    up_weight = rollout(up_master, table[rows : 2 * rows], *gate_at)
    table = step(table, lambda y, x, core, z: (y, x, core, z ^ 1))
    down_weight = rollout(down_master, table[2 * rows :].T, *down_at)
    down_block = send(down_weight.T, to_ff_group)
    table = step(table, lambda y, x, core, z: (y, x ^ 2, core, z))
    table = step(table, y_far)
    table = step(table, lambda y, x, core, z: (y ^ 1, x, core, z))
    table = step(table, lambda y, x, core, z: (y, x, core, z ^ 2))
    log_amax = jnp.log(
        jnp.stack([table[k * rows : k * rows + D // BLOCK, : FF // BLOCK] for k in range(3)]) + EPS
    )

    core = fsdp_place % 2
    y_hi, x = fsdp_place // 8, (fsdp_place // 2) % 4
    info = jnp.stack([(y_hi ^ dy) * 4 + (x + dx + 4) % 4 for dy, dx in ORDER] + [core])

    gate_blocks = gathered(gate_weight)
    up_blocks = gathered(up_weight)
    down_blocks = gathered(down_block)

    def flat(blocks):
        return [block for pair in blocks for block in pair]

    gate = token_sum(info, whole, (0, 1, 2, 3), flat(gate_blocks))
    up = token_sum(info, whole, (0, 1, 2), flat(up_blocks[:3]))
    hidden = token_sum(info, whole, (3,), flat(up_blocks[3:]), up, gate)

    total = 0.0
    for n, (mine, theirs) in enumerate(down_blocks):
        for k, term in enumerate(down_terms(info, hidden, mine, theirs)):
            total += send(term, to_chunk(*ORDER[2 * n + k])).astype(jnp.float32)
    return total.astype(jnp.bfloat16).T, log_amax


def solution(mesh):
    return jax.shard_map(
        on_device,
        mesh=mesh,
        in_specs=(P("fsdp", "tp"), P("fsdp", "tp"), P("fsdp", "tp"), P("fsdp", "tp")),
        out_specs=(P("fsdp", "tp"), P()),
        check_vma=False,
    )
```

```python
import functools

import jax
import jax.numpy as jnp
from jax import lax
from jax.experimental import pallas as pl
from jax.experimental.pallas import tpu as pltpu
from jax.sharding import PartitionSpec as P

D = 3584
FF = 9216
BLOCK = 128

FP8_MAX = 448.0
EPS = 1e-06
SMALLEST_NORMAL = 2.0 ** (-6)
AXES = ("fsdp", "tp")
VMEM_LIMIT = 48 * 1024 * 1024
TILE = 256
WIDE = 512


def snapped(value):
    magnitude = jnp.abs(value)
    exponent = jnp.floor(jnp.log2(jnp.maximum(magnitude, SMALLEST_NORMAL)))
    step_size = jnp.exp2(exponent - 3.0)
    return jnp.sign(value) * step_size * jnp.floor(magnitude / step_size + 0.5)


def place(y, x, core, z):
    y, x, z = y % 4, x % 4, z % 4
    return (((y // 2) * 4 + x) * 2 + core) * 8 + (y % 2) * 4 + z


def send(array, target):
    pairs = [
        (place(y, x, core, z), place(*target(y, x, core, z)))
        for y in range(4)
        for x in range(4)
        for core in range(2)
        for z in range(4)
    ]
    return lax.ppermute(array, AXES, pairs)


def x_up(y, x, core, z):
    return y, x + 1, core, z


def x_down(y, x, core, z):
    return y, x - 1, core, z


def z_up(y, x, core, z):
    return y, x, core, z + 1


def z_down(y, x, core, z):
    return y, x, core, z - 1


def y_near(y, x, core, z):
    return y ^ 1, x, core, z


def y_far(y, x, core, z):
    return y + 2, x, core, z


def other_core(y, x, core, z):
    return y, x, 1 - core, z


def to_ff_group(y, x, core, z):
    y_hi, y_lo = y // 2, y % 2
    return (y_lo ^ y_hi) * 2 + y_hi, z - x, core, x


def to_chunk(dy, dx):
    def target(y, x, core, z):
        y_hi, y_lo = y // 2, y % 2
        return y_hi * 2 + (y_lo ^ y_hi ^ dy), x, core, z + x + dx

    return target


def block_maxima(local, row_start, column_start, rows, columns):
    height, breadth = local.shape
    span_rows = (height - 1) // BLOCK + 2
    span_columns = (breadth - 1) // BLOCK + 2
    magnitude = jnp.abs(local)
    which_row = (row_start % BLOCK + jnp.arange(height, dtype=jnp.int32)) // BLOCK
    by_row = jnp.stack(
        [
            jnp.max(jnp.where((which_row == k)[:, None], magnitude, 0.0), axis=0)
            for k in range(span_rows)
        ]
    )
    which_column = (column_start % BLOCK + jnp.arange(breadth, dtype=jnp.int32)) // BLOCK
    pick = which_column[None, :] == jnp.arange(span_columns, dtype=jnp.int32)[:, None]
    part = jnp.max(jnp.where(pick[None], by_row[:, None, :], 0.0), axis=2)
    table = jnp.zeros((rows // BLOCK + span_rows, columns // BLOCK + span_columns), jnp.float32)
    return lax.dynamic_update_slice(table, part, (row_start // BLOCK, column_start // BLOCK))


def spread(scales, row_start, height, column_start, breadth):
    span_rows = (height - 1) // BLOCK + 2
    span_columns = (breadth - 1) // BLOCK + 2
    near = lax.dynamic_slice(
        scales, (row_start // BLOCK, column_start // BLOCK), (span_rows, span_columns)
    )
    which_row = (row_start % BLOCK + jnp.arange(height, dtype=jnp.int32)) // BLOCK
    which_column = (column_start % BLOCK + jnp.arange(breadth, dtype=jnp.int32)) // BLOCK
    wide = jnp.zeros((span_rows, breadth), jnp.float32)
    for k in range(span_columns):
        wide = jnp.where((which_column == k)[None, :], near[:, k : k + 1], wide)
    full = jnp.zeros((height, breadth), jnp.float32)
    for k in range(span_rows):
        full = jnp.where((which_row == k)[:, None], wide[k : k + 1, :], full)
    return full


def rollout(master, table, row_start, column_start):
    height, breadth = master.shape
    scale = spread((table + EPS) / FP8_MAX, row_start, height, column_start, breadth)
    return (snapped(master / scale) * scale).astype(jnp.bfloat16)


ORDER = ((0, 0), (1, 0), (0, -1), (0, 1), (1, -1), (1, 1), (0, 2), (1, 2))


def after(array, *others):
    return lax.optimization_barrier((array, *others))[0]


def ring(own, across, up, down, others=(), between=lambda n, blocks: ()):
    far = send(own, across)
    own_l, own_r = send(own, up), send(own, down)
    far = after(far, own_l, own_r, *others)
    far_l, far_r = send(far, up), send(far, down)
    others = between(0, [own, far, own_l, own_r])
    own_l, far_r = after(own_l, far_l, *others), after(far_r, far_l, *others)
    own_ll, far_rr = send(own_l, up), send(far_r, down)
    between(1, [far_l, far_r])
    return [own, far, own_l, own_r, far_l, far_r, own_ll, far_rr]


TOKEN_ORDER = ((0, 0), (1, 0), (0, -1), (1, -1), (0, 1), (1, 1), (0, 2), (1, 2))


def token_ring(own):
    pair = jnp.stack([own, send(own, y_near)])
    left, right = send(pair, z_up), send(pair, z_down)
    own_ll, near_rr = send(left[0], z_up), send(right[1], z_down)
    return jnp.concatenate([pair, left, right, own_ll[None], near_rr[None]])


def token_kernel(count, has_before, last, info, *refs):
    tokens, refs = refs[:count], list(refs[count:])
    before = refs.pop(0) if has_before else None
    blocks, (out, scratch, sems) = refs[: 2 * count], refs[2 * count :]
    half = blocks[0].shape[0]

    @pl.when(pl.program_id(0) == 0)
    def _():
        copies = []
        for n in range(count):
            for side in range(2):
                place = info[8] if side == 0 else 1 - info[8]
                rows = pl.ds(pl.multiple_of(n * WIDE + place * half, 16), half)
                copies.append(
                    pltpu.make_async_copy(
                        blocks[2 * n + side], scratch.at[rows, :], sems.at[2 * n + side]
                    )
                )
        for copy in copies:
            copy.start()
        for n in range(count):
            pad = WIDE - 2 * half
            scratch[n * WIDE + 2 * half : (n + 1) * WIDE, :] = jnp.zeros(
                (pad, scratch.shape[1]), scratch.dtype
            )
        for copy in copies:
            copy.wait()

    rows = jnp.concatenate([token[...] for token in tokens], axis=1)
    total = jnp.dot(rows, scratch[...], preferred_element_type=jnp.float32)
    if has_before:
        total += before[...]
    if last:
        middle = total.shape[1] // 2
        gate = total[:, :middle]
        total = gate / (1.0 + jnp.exp(-gate)) * total[:, middle:]
    out[...] = total.astype(out.dtype)


def token_sum(info, tokens, first, blocks, before=None, last=False):
    rows, columns = tokens.shape[1], blocks[0].shape[1]
    count = len(blocks) // 2
    width = columns // 2 if last else columns

    def token_block(n):
        return pl.BlockSpec((None, TILE, WIDE), lambda m, info: (info[first + n], m, 0))

    def tile(width):
        return pl.BlockSpec((TILE, width), lambda m, info: (m, 0))

    return pl.pallas_call(
        functools.partial(token_kernel, count, before is not None, last),
        out_shape=jax.ShapeDtypeStruct((rows, width), jnp.bfloat16 if last else jnp.float32),
        grid_spec=pltpu.PrefetchScalarGridSpec(
            num_scalar_prefetch=1,
            grid=(rows // TILE,),
            in_specs=[token_block(n) for n in range(count)]
            + ([] if before is None else [tile(columns)])
            + [pl.BlockSpec(memory_space=pl.ANY)] * (2 * count),
            out_specs=tile(width),
            scratch_shapes=[
                pltpu.VMEM((count * WIDE, columns), jnp.bfloat16),
                pltpu.SemaphoreType.DMA((2 * count,)),
            ],
        ),
        compiler_params=pltpu.CompilerParams(vmem_limit_bytes=VMEM_LIMIT),
        cost_estimate=pl.CostEstimate(
            flops=2 * rows * columns * count * WIDE,
            bytes_accessed=rows * columns * 8,
            transcendentals=0,
        ),
    )(info, *([tokens] * count), *([] if before is None else [before]), *blocks)


def vmem(n):
    return [pl.BlockSpec(memory_space=pltpu.VMEM)] * n


def down_kernel(info, hidden, *refs):
    blocks, outs = refs[: 2 * len(refs) // 3], refs[2 * len(refs) // 3 :]
    for n, out in enumerate(outs):
        mine, theirs = blocks[2 * n][...], blocks[2 * n + 1][...]
        low = jnp.where(info[8] == 0, mine, theirs)
        high = jnp.where(info[8] == 0, theirs, mine)
        out[...] = lax.dot_general(
            jnp.concatenate([low, high], axis=1),
            hidden[...],
            (((1,), (1,)), ((), ())),
            preferred_element_type=jnp.float32,
        ).astype(out.dtype)


def down_terms(info, hidden, blocks):
    rows, depth = hidden.shape
    columns = blocks[0].shape[0]
    count = len(blocks) // 2
    return pl.pallas_call(
        down_kernel,
        out_shape=[jax.ShapeDtypeStruct((columns, rows), jnp.bfloat16)] * count,
        in_specs=[pl.BlockSpec(memory_space=pltpu.SMEM)] + vmem(1 + len(blocks)),
        out_specs=vmem(count),
        compiler_params=pltpu.CompilerParams(vmem_limit_bytes=VMEM_LIMIT),
        cost_estimate=pl.CostEstimate(
            flops=2 * count * rows * columns * depth,
            bytes_accessed=rows * columns * 4,
            transcendentals=0,
        ),
    )(info, hidden, *blocks)


def on_device(tokens, gate_master, up_master, down_master):
    fsdp_place = lax.axis_index("fsdp")
    tp_place = lax.axis_index("tp")
    core = fsdp_place % 2
    y_hi, x = fsdp_place // 8, (fsdp_place // 2) % 4
    y_lo, z = tp_place // 4, tp_place % 4
    chips = [(y_hi ^ dy, (x + dx + 4) % 4) for dy, dx in ORDER]
    gate_height, gate_breadth = gate_master.shape
    down_height, down_breadth = down_master.shape
    gate_at = (fsdp_place * gate_height, tp_place * gate_breadth)
    down_at = (fsdp_place * down_height, tp_place * down_breadth)

    tables = [
        block_maxima(gate_master, *gate_at, D, FF),
        block_maxima(up_master, *gate_at, D, FF),
        block_maxima(down_master, *down_at, FF, D),
    ]
    rows = D // BLOCK + 12
    columns = FF // BLOCK + 56
    pad = lambda a: jnp.pad(a, ((0, rows - a.shape[0]), (0, columns - a.shape[1])))
    table = jnp.concatenate([pad(tables[0]), pad(tables[1]), pad(tables[2].T)])

    def step(table, target):
        return jnp.maximum(table, send(table, target))

    padded = jnp.pad(after(tokens, table), ((0, 0), (0, WIDE - tokens.shape[1])))
    table = step(table, other_core)
    table, padded = lax.optimization_barrier((table, padded))
    relative = token_ring(padded)
    down_table = step(table, lambda y, x, core, z: (y, x, core, z ^ 1))
    table = step(table, lambda y, x, core, z: (y, x ^ 1, core, z))
    gate_up = jnp.concatenate(
        [
            rollout(gate_master, table[:rows], *gate_at),
            rollout(up_master, table[rows : 2 * rows], *gate_at),
        ],
        axis=1,
    )
    gate_up, down_table = lax.optimization_barrier((gate_up, down_table))
    pairs = []

    def swap(n, blocks):
        others = [send(block, other_core) for block in blocks]
        for block, other in zip(blocks, others):
            pairs.extend((block, other))
        return others

    blocks = ring(gate_up, y_far, x_up, x_down, (), swap)
    swap(2, blocks[6:])
    down_table = after(down_table, *blocks[:4])
    down_weight = rollout(down_master, down_table[2 * rows :].T, *down_at)
    down_block = send(after(down_weight.T, blocks[4]), to_ff_group)

    table = jnp.maximum(table, down_table)
    every = jnp.max(lax.all_gather(table, "fsdp"), axis=0)
    every = jnp.max(lax.all_gather(every, "tp"), axis=0)
    log_amax = jnp.log(
        jnp.stack([every[k * rows : k * rows + D // BLOCK, : FF // BLOCK] for k in range(3)]) + EPS
    )

    order = [TOKEN_ORDER.index((dy, dx)) for dy in range(2) for dx in (0, 1, 2, -1)]
    by_offset = jnp.array(order, jnp.int32)
    info = jnp.stack(
        [by_offset[(chip_y ^ y_lo) * 4 + (chip_x - z + 4) % 4] for chip_y, chip_x in chips] + [core]
    )

    early = token_sum(info, relative, 0, pairs[:12])
    down_block, early = lax.optimization_barrier((down_block, early))
    down_block = after(down_block, blocks[6], blocks[7])
    hidden = token_sum(info, relative, 6, pairs[12:], early, last=True)
    down_blocks = ring(down_block, y_far, x_up, x_down, (hidden,))

    def both(blocks):
        return [b for block in blocks for b in (block, send(block, other_core))]

    total = 0.0
    for n in range(0, 8, 2):
        terms = down_terms(info, hidden, both(down_blocks[n : n + 2]))
        for k in range(2):
            total += send(terms[k], to_chunk(*ORDER[n + k])).astype(jnp.float32)
    return total.astype(jnp.bfloat16).T, log_amax


def solution(mesh):
    return jax.shard_map(
        on_device,
        mesh=mesh,
        in_specs=(P("fsdp", "tp"), P("fsdp", "tp"), P("fsdp", "tp"), P("fsdp", "tp")),
        out_specs=(P("fsdp", "tp"), P()),
        check_vma=False,
    )
```

```python
import functools

import jax
import jax.numpy as jnp
from jax import lax
from jax.experimental import pallas as pl
from jax.experimental.pallas import tpu as pltpu
from jax.sharding import PartitionSpec as P

D = 3584
FF = 9216
BLOCK = 128

FP8_MAX = 448.0
EPS = 1e-06
SMALLEST_NORMAL = 2.0 ** (-6)
AXES = ("fsdp", "tp")
VMEM_LIMIT = 48 * 1024 * 1024
TILE = 256
HALF = 256


def snapped(value):
    magnitude = jnp.abs(value)
    exponent = jnp.floor(jnp.log2(jnp.maximum(magnitude, SMALLEST_NORMAL)))
    step_size = jnp.exp2(exponent - 3.0)
    return jnp.sign(value) * step_size * jnp.floor(magnitude / step_size + 0.5)


def place(y, x, core, z):
    y, x, z = y % 4, x % 4, z % 4
    return (((y // 2) * 4 + x) * 2 + core) * 8 + (y % 2) * 4 + z


def send(array, target):
    pairs = [
        (place(y, x, core, z), place(*target(y, x, core, z)))
        for y in range(4)
        for x in range(4)
        for core in range(2)
        for z in range(4)
    ]
    return lax.ppermute(array, AXES, pairs)


def x_up(y, x, core, z):
    return y, x + 1, core, z


def x_down(y, x, core, z):
    return y, x - 1, core, z


def z_up(y, x, core, z):
    return y, x, core, z + 1


def z_down(y, x, core, z):
    return y, x, core, z - 1


def y_near(y, x, core, z):
    return y ^ 1, x, core, z


def y_far(y, x, core, z):
    return y + 2, x, core, z


def other_core(y, x, core, z):
    return y, x, 1 - core, z


def to_ff_group(y, x, core, z):
    y_hi, y_lo = y // 2, y % 2
    return (y_lo ^ y_hi) * 2 + y_hi, z - x, core, x


def to_chunk(dy, dx):
    def target(y, x, core, z):
        y_hi, y_lo = y // 2, y % 2
        return y_hi * 2 + (y_lo ^ y_hi ^ dy), x, core, z + x + dx

    return target


def block_maxima(local, row_start, column_start, rows, columns):
    height, breadth = local.shape
    span_rows = (height - 1) // BLOCK + 2
    span_columns = (breadth - 1) // BLOCK + 2
    magnitude = jnp.abs(local)
    which_row = (row_start % BLOCK + jnp.arange(height, dtype=jnp.int32)) // BLOCK
    by_row = jnp.stack(
        [
            jnp.max(jnp.where((which_row == k)[:, None], magnitude, 0.0), axis=0)
            for k in range(span_rows)
        ]
    )
    which_column = (column_start % BLOCK + jnp.arange(breadth, dtype=jnp.int32)) // BLOCK
    pick = which_column[None, :] == jnp.arange(span_columns, dtype=jnp.int32)[:, None]
    part = jnp.max(jnp.where(pick[None], by_row[:, None, :], 0.0), axis=2)
    table = jnp.zeros((rows // BLOCK + span_rows, columns // BLOCK + span_columns), jnp.float32)
    return lax.dynamic_update_slice(table, part, (row_start // BLOCK, column_start // BLOCK))


def spread(scales, row_start, height, column_start, breadth):
    span_rows = (height - 1) // BLOCK + 2
    span_columns = (breadth - 1) // BLOCK + 2
    near = lax.dynamic_slice(
        scales, (row_start // BLOCK, column_start // BLOCK), (span_rows, span_columns)
    )
    which_row = (row_start % BLOCK + jnp.arange(height, dtype=jnp.int32)) // BLOCK
    which_column = (column_start % BLOCK + jnp.arange(breadth, dtype=jnp.int32)) // BLOCK
    wide = jnp.zeros((span_rows, breadth), jnp.float32)
    for k in range(span_columns):
        wide = jnp.where((which_column == k)[None, :], near[:, k : k + 1], wide)
    full = jnp.zeros((height, breadth), jnp.float32)
    for k in range(span_rows):
        full = jnp.where((which_row == k)[:, None], wide[k : k + 1, :], full)
    return full


def rollout(master, table, row_start, column_start):
    height, breadth = master.shape
    scale = spread((table + EPS) / FP8_MAX, row_start, height, column_start, breadth)
    return (snapped(master / scale) * scale).astype(jnp.bfloat16)


ORDER = ((0, 0), (1, 0), (0, -1), (0, 1), (1, -1), (1, 1), (0, 2), (1, 2))


def after(array, *others):
    return lax.optimization_barrier((array, *others))[0]


def ring(own, far, up, down, others=(), between=lambda blocks: ()):
    own_l, own_r = send(own, up), send(own, down)
    far = after(far, own_l, own_r, *others)
    far_l, far_r = send(far, up), send(far, down)
    others = between([own, far, own_l, own_r])
    own_l, far_r = after(own_l, far_l, *others), after(far_r, far_l, *others)
    own_ll, far_rr = send(own_l, up), send(far_r, down)
    return [own, far, own_l, own_r, far_l, far_r, own_ll, far_rr]


TOKEN_ORDER = ((0, 0), (1, 0), (0, -1), (1, -1), (0, 1), (1, 1), (0, 2), (1, 2))


def token_ring(own, near):
    pair = jnp.stack([own, near])
    left, right = send(pair, z_up), send(pair, z_down)
    own_ll, near_rr = send(left[0], z_up), send(right[1], z_down)
    return jnp.concatenate([pair, left, right, own_ll[None], near_rr[None]])


def token_kernel(count, has_before, last, info, *refs):
    tokens, refs = refs[:count], list(refs[count:])
    before = refs.pop(0) if has_before else None
    blocks, (out, scratch, sems) = refs[:count], refs[count:]
    height = blocks[0].shape[0]

    @pl.when(pl.program_id(0) == 0)
    def _():
        copies = [
            pltpu.make_async_copy(
                block, scratch.at[pl.ds(n * HALF, height), :], sems.at[n]
            )
            for n, block in enumerate(blocks)
        ]
        for copy in copies:
            copy.start()
        for n in range(count):
            scratch[n * HALF + height : (n + 1) * HALF, :] = jnp.zeros(
                (HALF - height, scratch.shape[1]), scratch.dtype
            )
        for copy in copies:
            copy.wait()

    rows = jnp.concatenate([token[...] for token in tokens], axis=1)
    total = jnp.dot(rows, scratch[...], preferred_element_type=jnp.float32)
    if has_before:
        total += before[...]
    if last:
        middle = total.shape[1] // 2
        gate = total[:, :middle]
        total = gate / (1.0 + jnp.exp(-gate)) * total[:, middle:]
    out[...] = total.astype(out.dtype)


def token_sum(info, tokens, first, blocks, before=None, last=False):
    rows, columns = tokens.shape[1], blocks[0].shape[1]
    count = len(blocks)
    width = columns // 2 if last else columns

    def token_block(n):
        side = n % 2
        return pl.BlockSpec(
            (None, TILE, HALF),
            lambda m, info: (info[first + n // 2], m, 1 - info[8] if side else info[8]),
        )

    def tile(width):
        return pl.BlockSpec((TILE, width), lambda m, info: (m, 0))

    return pl.pallas_call(
        functools.partial(token_kernel, count, before is not None, last),
        out_shape=jax.ShapeDtypeStruct((rows, width), jnp.bfloat16 if last else jnp.float32),
        grid_spec=pltpu.PrefetchScalarGridSpec(
            num_scalar_prefetch=1,
            grid=(rows // TILE,),
            in_specs=[token_block(n) for n in range(count)]
            + ([] if before is None else [tile(columns)])
            + [pl.BlockSpec(memory_space=pl.ANY)] * count,
            out_specs=tile(width),
            scratch_shapes=[
                pltpu.VMEM((count * HALF, columns), jnp.bfloat16),
                pltpu.SemaphoreType.DMA((count,)),
            ],
        ),
        compiler_params=pltpu.CompilerParams(vmem_limit_bytes=VMEM_LIMIT),
        cost_estimate=pl.CostEstimate(
            flops=2 * rows * columns * count * HALF,
            bytes_accessed=rows * columns * 8,
            transcendentals=0,
        ),
    )(info, *([tokens] * count), *([] if before is None else [before]), *blocks)


def vmem(n):
    return [pl.BlockSpec(memory_space=pltpu.VMEM)] * n


def down_kernel(info, hidden, *refs):
    blocks, outs = refs[: 2 * len(refs) // 3], refs[2 * len(refs) // 3 :]
    for n, out in enumerate(outs):
        mine, theirs = blocks[2 * n][...], blocks[2 * n + 1][...]
        low = jnp.where(info[8] == 0, mine, theirs)
        high = jnp.where(info[8] == 0, theirs, mine)
        out[...] = lax.dot_general(
            jnp.concatenate([low, high], axis=1),
            hidden[...],
            (((1,), (1,)), ((), ())),
            preferred_element_type=jnp.float32,
        ).astype(out.dtype)


def down_terms(info, hidden, blocks):
    rows, depth = hidden.shape
    columns = blocks[0].shape[0]
    count = len(blocks) // 2
    return pl.pallas_call(
        down_kernel,
        out_shape=[jax.ShapeDtypeStruct((columns, rows), jnp.bfloat16)] * count,
        in_specs=[pl.BlockSpec(memory_space=pltpu.SMEM)] + vmem(1 + len(blocks)),
        out_specs=vmem(count),
        compiler_params=pltpu.CompilerParams(vmem_limit_bytes=VMEM_LIMIT),
        cost_estimate=pl.CostEstimate(
            flops=2 * count * rows * columns * depth,
            bytes_accessed=rows * columns * 4,
            transcendentals=0,
        ),
    )(info, hidden, *blocks)


def on_device(tokens, gate_master, up_master, down_master):
    fsdp_place = lax.axis_index("fsdp")
    tp_place = lax.axis_index("tp")
    core = fsdp_place % 2
    y_hi, x = fsdp_place // 8, (fsdp_place // 2) % 4
    y_lo, z = tp_place // 4, tp_place % 4
    chips = [(y_hi ^ dy, (x + dx + 4) % 4) for dy, dx in ORDER]
    gate_height, gate_breadth = gate_master.shape
    down_height, down_breadth = down_master.shape
    gate_at = (fsdp_place * gate_height, tp_place * gate_breadth)
    down_at = (fsdp_place * down_height, tp_place * down_breadth)

    half = tokens.shape[1] // 2
    padded = jnp.concatenate(
        [jnp.pad(tokens[:, k * half : (k + 1) * half], ((0, 0), (0, HALF - half))) for k in range(2)],
        axis=1,
    )
    near = send(padded, y_near)
    gate_master, up_master, down_master, padded = lax.optimization_barrier(
        (gate_master, up_master, down_master, padded)
    )

    tables = [
        block_maxima(gate_master, *gate_at, D, FF),
        block_maxima(up_master, *gate_at, D, FF),
        block_maxima(down_master, *down_at, FF, D),
    ]
    rows = D // BLOCK + 12
    columns = FF // BLOCK + 56
    pad = lambda a: jnp.pad(a, ((0, rows - a.shape[0]), (0, columns - a.shape[1])))
    spare = jnp.zeros((8, columns), jnp.float32)
    table = jnp.concatenate([pad(tables[0]), pad(tables[1]), pad(tables[2].T), spare])

    def step(table, target):
        return jnp.maximum(table, send(table, target))

    table = step(table, other_core)
    down_table = step(table, lambda y, x, core, z: (y, x, core, z ^ 1))
    table = step(table, lambda y, x, core, z: (y, x ^ 1, core, z))
    gate_up = jnp.concatenate(
        [
            rollout(gate_master, table[:rows], *gate_at),
            rollout(up_master, table[rows : 2 * rows], *gate_at),
        ],
        axis=1,
    )
    gate_up, down_table, near, padded = lax.optimization_barrier(
        (gate_up, down_table, near, padded)
    )
    relative = token_ring(padded, near)
    pairs = []

    def swap(blocks):
        others = [send(block, other_core) for block in blocks]
        for block, other in zip(blocks, others):
            pairs.extend((block, other))
        return others

    blocks = ring(gate_up, send(gate_up, y_far), x_up, x_down, (), swap)
    swap(blocks[4:6])

    table = jnp.maximum(table, down_table)
    every = jnp.max(lax.all_gather(table, "fsdp"), axis=0)
    order = [TOKEN_ORDER.index((dy, dx)) for dy in range(2) for dx in (0, 1, 2, -1)]
    by_offset = jnp.array(order, jnp.int32)
    info = jnp.stack(
        [by_offset[(chip_y ^ y_lo) * 4 + (chip_x - z + 4) % 4] for chip_y, chip_x in chips] + [core]
    )

    relative, every = lax.optimization_barrier((relative, every))
    early = token_sum(info, relative, 0, pairs)

    def both(blocks):
        return [b for block in blocks for b in (block, send(block, other_core))]

    down_table = after(down_table, *blocks[:4])
    down_weight = rollout(down_master, down_table[2 * rows : 3 * rows].T, *down_at)
    down_block = send(after(down_weight.T, blocks[4], blocks[5]), to_ff_group)
    down_far = send(down_block, y_far)
    down_pairs = [both([down_block, down_far])]
    down_block, early, own_ll, far_rr = lax.optimization_barrier(
        (down_block, early, blocks[6], blocks[7])
    )
    pairs = both([own_ll, far_rr])
    early = after(early, *down_pairs[0])
    hidden = token_sum(info, relative, 6, pairs, early, last=True)
    down_blocks = ring(down_block, down_far, x_up, x_down, (hidden,))
    down_pairs += [both(down_blocks[n : n + 2]) for n in (2, 4, 6)]

    every = jnp.pad(every, ((0, every.shape[0]), (0, 0)))
    every = jnp.max(lax.all_gather(every, "tp"), axis=0)
    log_amax = jnp.log(
        jnp.stack([every[k * rows : k * rows + D // BLOCK, : FF // BLOCK] for k in range(3)]) + EPS
    )

    total = 0.0
    for n in range(0, 8, 2):
        terms = down_terms(info, hidden, down_pairs[n // 2])
        for k in range(2):
            total += send(terms[k], to_chunk(*ORDER[n + k])).astype(jnp.float32)
    return total.astype(jnp.bfloat16).T, log_amax


def solution(mesh):
    return jax.shard_map(
        on_device,
        mesh=mesh,
        in_specs=(P("fsdp", "tp"), P("fsdp", "tp"), P("fsdp", "tp"), P("fsdp", "tp")),
        out_specs=(P("fsdp", "tp"), P()),
        check_vma=False,
    )
```

```python
import functools

import jax
import jax.numpy as jnp
from jax import lax
from jax.experimental import pallas as pl
from jax.experimental.pallas import tpu as pltpu
from jax.sharding import PartitionSpec as P

D = 3584
FF = 9216
BLOCK = 128

FP8_MAX = 448.0
EPS = 1e-06
SMALLEST_NORMAL = 2.0 ** (-6)
AXES = ("fsdp", "tp")
VMEM_LIMIT = 48 * 1024 * 1024
TILE = 256
HALF = 256


def snapped(value):
    magnitude = jnp.abs(value)
    exponent = jnp.floor(jnp.log2(jnp.maximum(magnitude, SMALLEST_NORMAL)))
    step_size = jnp.exp2(exponent - 3.0)
    return jnp.sign(value) * step_size * jnp.floor(magnitude / step_size + 0.5)


def place(y, x, core, z):
    y, x, z = y % 4, x % 4, z % 4
    return (((y // 2) * 4 + x) * 2 + core) * 8 + (y % 2) * 4 + z


def send(array, target):
    pairs = [
        (place(y, x, core, z), place(*target(y, x, core, z)))
        for y in range(4)
        for x in range(4)
        for core in range(2)
        for z in range(4)
    ]
    return lax.ppermute(array, AXES, pairs)


def x_up(y, x, core, z):
    return y, x + 1, core, z


def x_down(y, x, core, z):
    return y, x - 1, core, z


def z_up(y, x, core, z):
    return y, x, core, z + 1


def z_down(y, x, core, z):
    return y, x, core, z - 1


def y_near(y, x, core, z):
    return y ^ 1, x, core, z


def y_far(y, x, core, z):
    return y + 2, x, core, z


def other_core(y, x, core, z):
    return y, x, 1 - core, z


def to_ff_group(y, x, core, z):
    y_hi, y_lo = y // 2, y % 2
    across = y_lo ^ y_hi
    return across * 2 + y_hi, z - x - 2 * across, core, x


def to_chunk(dy, dx):
    def target(y, x, core, z):
        y_hi, y_lo = y // 2, y % 2
        across = y_hi ^ dy
        return y_hi * 2 + (y_lo ^ across), x, core, z + x + dx + 2 * across

    return target


def block_maxima(local, row_start, column_start, rows, columns):
    height, breadth = local.shape
    span_rows = (height - 1) // BLOCK + 2
    span_columns = (breadth - 1) // BLOCK + 2
    magnitude = jnp.abs(local)
    which_row = (row_start % BLOCK + jnp.arange(height, dtype=jnp.int32)) // BLOCK
    by_row = jnp.stack(
        [
            jnp.max(jnp.where((which_row == k)[:, None], magnitude, 0.0), axis=0)
            for k in range(span_rows)
        ]
    )
    which_column = (column_start % BLOCK + jnp.arange(breadth, dtype=jnp.int32)) // BLOCK
    pick = which_column[None, :] == jnp.arange(span_columns, dtype=jnp.int32)[:, None]
    part = jnp.max(jnp.where(pick[None], by_row[:, None, :], 0.0), axis=2)
    table = jnp.zeros((rows // BLOCK + span_rows, columns // BLOCK + span_columns), jnp.float32)
    return lax.dynamic_update_slice(table, part, (row_start // BLOCK, column_start // BLOCK))


def spread(scales, row_start, height, column_start, breadth):
    span_rows = (height - 1) // BLOCK + 2
    span_columns = (breadth - 1) // BLOCK + 2
    near = lax.dynamic_slice(
        scales, (row_start // BLOCK, column_start // BLOCK), (span_rows, span_columns)
    )
    which_row = (row_start % BLOCK + jnp.arange(height, dtype=jnp.int32)) // BLOCK
    which_column = (column_start % BLOCK + jnp.arange(breadth, dtype=jnp.int32)) // BLOCK
    wide = jnp.zeros((span_rows, breadth), jnp.float32)
    for k in range(span_columns):
        wide = jnp.where((which_column == k)[None, :], near[:, k : k + 1], wide)
    full = jnp.zeros((height, breadth), jnp.float32)
    for k in range(span_rows):
        full = jnp.where((which_row == k)[:, None], wide[k : k + 1, :], full)
    return full


def rollout(master, table, row_start, column_start):
    height, breadth = master.shape
    scale = spread((table + EPS) / FP8_MAX, row_start, height, column_start, breadth)
    return (snapped(master / scale) * scale).astype(jnp.bfloat16)


ORDER = ((0, 0), (1, 0), (0, -1), (0, 1), (1, -1), (1, 1), (0, 2), (1, 2))


def after(array, *others):
    return lax.optimization_barrier((array, *others))[0]


def ring(own, far, up, down, between):
    own_l, own_r = send(own, up), send(own, down)
    far = after(far, own_l, own_r)
    far_l, far_r = send(far, up), send(far, down)
    others = between([own, far, own_l, own_r])
    own_l, far_r = after(own_l, far_l, *others), after(far_r, far_l, *others)
    own_ll, far_rr = send(own_l, up), send(far_r, down)
    return [own, far, own_l, own_r, far_l, far_r, own_ll, far_rr]


TOKEN_ORDER = ((0, 0), (1, 0), (0, -1), (1, -1), (0, 1), (1, 1), (0, 2), (1, 2))


def token_ring(pair):
    left, right = send(pair, z_up), send(pair, z_down)
    return [pair, left, right, send(left[0], z_up)[None], send(right[1], z_down)[None]]


def token_kernel(count, has_before, last, info, *refs):
    tokens, refs = refs[:5], list(refs[5:])
    before = refs.pop(0) if has_before else None
    blocks, (out, wide, scratch, wide_sems, sems) = refs[:count], refs[count:]
    height = blocks[0].shape[0]
    pieces = [ref.at[k] for ref in tokens for k in range(ref.shape[0])]

    def block_copy(n):
        rows = pl.ds(n * HALF, height)
        return pltpu.make_async_copy(blocks[n], scratch.at[rows, :], sems.at[n])

    def token_copy(n, piece=0):
        return pltpu.make_async_copy(pieces[piece], wide.at[n], wide_sems.at[n])

    def rows_of(m, n):
        start = pl.multiple_of(m * TILE, TILE)
        low, high = wide[n, pl.ds(start, TILE), :HALF], wide[n, pl.ds(start, TILE), HALF:]
        swapped = info[8] == 1
        return jnp.where(swapped, high, low), jnp.where(swapped, low, high)

    def finish(total):
        if has_before:
            total += before[...]
        if last:
            middle = total.shape[1] // 2
            gate = total[:, :middle]
            total = gate / (1.0 + jnp.exp(-gate)) * total[:, middle:]
        out[...] = total.astype(out.dtype)

    m = pl.program_id(0)

    @pl.when(m == 0)
    def _():
        for n in range(count // 2):
            for piece in range(len(pieces)):

                @pl.when(info[n] == piece)
                def _():
                    token_copy(n, piece).start()

            block_copy(2 * n).start()
            block_copy(2 * n + 1).start()
        for n in range(count):
            scratch[n * HALF + height : (n + 1) * HALF, :] = jnp.zeros(
                (HALF - height, scratch.shape[1]), scratch.dtype
            )
        for n in range(count // 2):
            token_copy(n).wait()
            block_copy(2 * n).wait()
            block_copy(2 * n + 1).wait()

    rows = jnp.concatenate([part for n in range(count // 2) for part in rows_of(m, n)], axis=1)
    finish(jnp.dot(rows, scratch[...], preferred_element_type=jnp.float32))


def token_sum(info, tokens, first, blocks, before=None, last=False):
    rows, columns = tokens[0].shape[1], blocks[0].shape[1]
    count = len(blocks)
    width = columns // 2 if last else columns

    def tile(width):
        return pl.BlockSpec((TILE, width), lambda m, info: (m, 0))

    if first:
        info = jnp.concatenate([info[first:8], info[:first], info[8:]])
    return pl.pallas_call(
        functools.partial(token_kernel, count, before is not None, last),
        out_shape=jax.ShapeDtypeStruct((rows, width), jnp.bfloat16 if last else jnp.float32),
        grid_spec=pltpu.PrefetchScalarGridSpec(
            num_scalar_prefetch=1,
            grid=(rows // TILE,),
            in_specs=[pl.BlockSpec(memory_space=pl.ANY)] * 5
            + ([] if before is None else [tile(columns)])
            + [pl.BlockSpec(memory_space=pl.ANY)] * count,
            out_specs=tile(width),
            scratch_shapes=[
                pltpu.VMEM((count // 2, rows, 2 * HALF), jnp.bfloat16),
                pltpu.VMEM((count * HALF, columns), jnp.bfloat16),
                pltpu.SemaphoreType.DMA((count // 2,)),
                pltpu.SemaphoreType.DMA((count,)),
            ],
        ),
        compiler_params=pltpu.CompilerParams(vmem_limit_bytes=VMEM_LIMIT),
        cost_estimate=pl.CostEstimate(
            flops=2 * rows * columns * count * HALF,
            bytes_accessed=rows * columns * 8,
            transcendentals=0,
        ),
    )(info, *tokens, *([] if before is None else [before]), *blocks)


def vmem(n):
    return [pl.BlockSpec(memory_space=pltpu.VMEM)] * n


def down_kernel(info, hidden, *refs):
    blocks, outs = refs[: 2 * len(refs) // 3], refs[2 * len(refs) // 3 :]
    for n, out in enumerate(outs):
        mine, theirs = blocks[2 * n][...], blocks[2 * n + 1][...]
        low = jnp.where(info[8] == 0, mine, theirs)
        high = jnp.where(info[8] == 0, theirs, mine)
        out[...] = lax.dot_general(
            jnp.concatenate([low, high], axis=1),
            hidden[...],
            (((1,), (1,)), ((), ())),
            preferred_element_type=jnp.float32,
        ).astype(out.dtype)


def down_terms(info, hidden, blocks):
    rows, depth = hidden.shape
    columns = blocks[0].shape[0]
    count = len(blocks) // 2
    return pl.pallas_call(
        down_kernel,
        out_shape=[jax.ShapeDtypeStruct((columns, rows), jnp.bfloat16)] * count,
        in_specs=[pl.BlockSpec(memory_space=pltpu.SMEM)] + vmem(1 + len(blocks)),
        out_specs=vmem(count),
        compiler_params=pltpu.CompilerParams(vmem_limit_bytes=VMEM_LIMIT),
        cost_estimate=pl.CostEstimate(
            flops=2 * count * rows * columns * depth,
            bytes_accessed=rows * columns * 4,
            transcendentals=0,
        ),
    )(info, hidden, *blocks)


def on_device(tokens, gate_master, up_master, down_master):
    fsdp_place = lax.axis_index("fsdp")
    tp_place = lax.axis_index("tp")
    core = fsdp_place % 2
    y_hi, x = fsdp_place // 8, (fsdp_place // 2) % 4
    y_lo, z = tp_place // 4, tp_place % 4
    chips = [(y_hi ^ dy, (x + dx + 4) % 4) for dy, dx in ORDER]
    gate_height, gate_breadth = gate_master.shape
    down_height, down_breadth = down_master.shape
    gate_at = (fsdp_place * gate_height, tp_place * gate_breadth)
    down_at = (fsdp_place * down_height, tp_place * down_breadth)

    half = tokens.shape[1] // 2
    padded = jnp.concatenate(
        [jnp.pad(tokens[:, k * half : (k + 1) * half], ((0, 0), (0, HALF - half))) for k in range(2)],
        axis=1,
    )
    near = send(padded, y_near)
    gate_master, up_master, down_master, padded = lax.optimization_barrier(
        (gate_master, up_master, down_master, padded)
    )

    tables = [
        block_maxima(gate_master, *gate_at, D, FF),
        block_maxima(up_master, *gate_at, D, FF),
        block_maxima(down_master, *down_at, FF, D),
    ]
    rows = D // BLOCK + 12
    columns = FF // BLOCK + 56
    pad = lambda a: jnp.pad(a, ((0, rows - a.shape[0]), (0, columns - a.shape[1])))
    table = jnp.concatenate([pad(tables[0]), pad(tables[1]), pad(tables[2].T)])

    def step(table, target):
        return jnp.maximum(table, send(table, target))

    table = step(table, other_core)
    table = step(table, lambda y, x, core, z: (y, x ^ 1, core, z))
    gate_up = jnp.concatenate(
        [
            rollout(gate_master, table[:rows], *gate_at),
            rollout(up_master, table[rows : 2 * rows], *gate_at),
        ],
        axis=1,
    )
    every = step(table, lambda y, x, core, z: (y, x, core, z ^ 1))
    pair = jnp.stack([padded, near])
    gate_up, pair, every = lax.optimization_barrier((gate_up, pair, every))
    down_table = every
    relative = token_ring(pair)
    pairs = []

    def swap(blocks):
        nonlocal every
        if len(blocks) == 4:
            every = step(after(every, *blocks), y_near)
        others = [send(block, other_core) for block in blocks]
        for block, other in zip(blocks, others):
            pairs.extend((block, other))
        return others + [every]

    blocks = ring(gate_up, send(gate_up, y_far), x_up, x_down, swap)
    swap(blocks[4:6])

    order = [TOKEN_ORDER.index((dy, dx)) for dy in range(2) for dx in (0, 1, 2, -1)]
    by_offset = jnp.array(order, jnp.int32)
    info = jnp.stack(
        [by_offset[(chip_y ^ y_lo) * 4 + (chip_x - z + 4) % 4] for chip_y, chip_x in chips] + [core]
    )

    ready = after(every, relative[3], relative[4], blocks[4], blocks[5])
    early = token_sum(info, relative, 0, pairs)
    every = step(ready, lambda y, x, core, z: (y, x, core, z ^ 2))

    def both(blocks):
        return [b for block in blocks for b in (block, send(block, other_core))]

    down_table = after(down_table, *blocks[:4])
    down_weight = rollout(down_master, down_table[2 * rows : 3 * rows].T, *down_at)
    down_block = send(after(down_weight.T, blocks[4], blocks[5]), to_ff_group)
    down_far = send(down_block, y_far)
    down_pairs = [both([down_block, down_far])]
    down_block, early, own_ll, far_rr, every = lax.optimization_barrier(
        (down_block, early, blocks[6], blocks[7], every)
    )
    pairs = both([own_ll, far_rr])
    every = step(after(every, *down_pairs[0]), y_far)
    early = after(early, *down_pairs[0])
    hidden = token_sum(info, relative, 6, pairs, early, last=True)
    def sums(n, pair):
        terms = down_terms(info, hidden, pair)
        return terms, [send(term, to_chunk(*ORDER[n + k])) for k, term in enumerate(terms)]

    own_l, own_r = send(down_block, x_up), send(down_block, x_down)
    own_l, own_r, down_far, hidden = lax.optimization_barrier((own_l, own_r, down_far, hidden))
    _, parts = sums(0, down_pairs[0])
    far_l, far_r = send(down_far, x_up), send(down_far, x_down)
    terms, more = sums(2, both([own_l, own_r]))
    own_l, far_r, *_ = lax.optimization_barrier((own_l, far_r, far_l, *terms, *parts))
    own_ll, far_rr = send(own_l, x_up), send(far_r, x_down)
    parts += more
    parts += sums(4, both([far_l, far_r]))[1]
    parts += sums(6, both([own_ll, far_rr]))[1]
    every = step(after(every, own_ll, far_rr), lambda y, x, core, z: (y, x ^ 2, core, z))
    log_amax = jnp.log(
        jnp.stack([every[k * rows : k * rows + D // BLOCK, : FF // BLOCK] for k in range(3)]) + EPS
    )
    total = sum(part.astype(jnp.float32) for part in parts)
    return total.astype(jnp.bfloat16).T, log_amax


def solution(mesh):
    return jax.shard_map(
        on_device,
        mesh=mesh,
        in_specs=(P("fsdp", "tp"), P("fsdp", "tp"), P("fsdp", "tp"), P("fsdp", "tp")),
        out_specs=(P("fsdp", "tp"), P()),
        check_vma=False,
    )
```

```python
import functools

import jax
import jax.numpy as jnp
from jax import lax
from jax.experimental import pallas as pl
from jax.experimental.pallas import tpu as pltpu
from jax.sharding import PartitionSpec as P

D = 3584
FF = 9216
BLOCK = 128

FP8_MAX = 448.0
EPS = 1e-06
SMALLEST_NORMAL = 2.0 ** (-6)
AXES = ("fsdp", "tp")
VMEM_LIMIT = 60 * 1024 * 1024
TILE = 256
HALF = 256
FREE = pl.CostEstimate(flops=0, bytes_accessed=0, transcendentals=0)


def snapped(value):
    magnitude = jnp.abs(value)
    exponent = jnp.floor(jnp.log2(jnp.maximum(magnitude, SMALLEST_NORMAL)))
    step_size = jnp.exp2(exponent - 3.0)
    return jnp.sign(value) * step_size * jnp.floor(magnitude / step_size + 0.5)


def place(y, x, core, z):
    y, x, z = y % 4, x % 4, z % 4
    return (((y // 2) * 4 + x) * 2 + core) * 8 + (y % 2) * 4 + z


def send(array, target):
    pairs = [
        (place(y, x, core, z), place(*target(y, x, core, z)))
        for y in range(4)
        for x in range(4)
        for core in range(2)
        for z in range(4)
    ]
    return lax.ppermute(array, AXES, pairs)


def x_up(y, x, core, z):
    return y, x + 1, core, z


def x_down(y, x, core, z):
    return y, x - 1, core, z


def z_up(y, x, core, z):
    return y, x, core, z + 1


def z_down(y, x, core, z):
    return y, x, core, z - 1


def y_near(y, x, core, z):
    return y ^ 1, x, core, z


def y_far(y, x, core, z):
    return y + 2, x, core, z


def other_core(y, x, core, z):
    return y, x, 1 - core, z


def to_ff_group(y, x, core, z):
    y_hi, y_lo = y // 2, y % 2
    across = y_lo ^ y_hi
    return across * 2 + y_hi, z - x - 2 * across, core, x


def to_chunk(dy, dx):
    def target(y, x, core, z):
        y_hi, y_lo = y // 2, y % 2
        across = y_hi ^ dy
        return y_hi * 2 + (y_lo ^ across), x, core, z + x + dx + 2 * across

    return target


def block_maxima(local, row_start, column_start, rows, columns):
    height, breadth = local.shape
    span_rows = (height - 1) // BLOCK + 2
    span_columns = (breadth - 1) // BLOCK + 2
    magnitude = jnp.abs(local)
    which_row = (row_start % BLOCK + jnp.arange(height, dtype=jnp.int32)) // BLOCK
    by_row = jnp.stack(
        [
            jnp.max(jnp.where((which_row == k)[:, None], magnitude, 0.0), axis=0)
            for k in range(span_rows)
        ]
    )
    which_column = (column_start % BLOCK + jnp.arange(breadth, dtype=jnp.int32)) // BLOCK
    pick = which_column[None, :] == jnp.arange(span_columns, dtype=jnp.int32)[:, None]
    part = jnp.max(jnp.where(pick[None], by_row[:, None, :], 0.0), axis=2)
    table = jnp.zeros((rows // BLOCK + span_rows, columns // BLOCK + span_columns), jnp.float32)
    return lax.dynamic_update_slice(table, part, (row_start // BLOCK, column_start // BLOCK))


def spread(scales, row_start, height, column_start, breadth):
    span_rows = (height - 1) // BLOCK + 2
    span_columns = (breadth - 1) // BLOCK + 2
    near = lax.dynamic_slice(
        scales, (row_start // BLOCK, column_start // BLOCK), (span_rows, span_columns)
    )
    which_row = (row_start % BLOCK + jnp.arange(height, dtype=jnp.int32)) // BLOCK
    which_column = (column_start % BLOCK + jnp.arange(breadth, dtype=jnp.int32)) // BLOCK
    wide = jnp.zeros((span_rows, breadth), jnp.float32)
    for k in range(span_columns):
        wide = jnp.where((which_column == k)[None, :], near[:, k : k + 1], wide)
    full = jnp.zeros((height, breadth), jnp.float32)
    for k in range(span_rows):
        full = jnp.where((which_row == k)[:, None], wide[k : k + 1, :], full)
    return full


def rollout(master, table, row_start, column_start):
    height, breadth = master.shape
    scale = spread((table + EPS) / FP8_MAX, row_start, height, column_start, breadth)
    return (snapped(master / scale) * scale).astype(jnp.bfloat16)


ORDER = ((0, 0), (1, 0), (0, -1), (0, 1), (1, -1), (1, 1), (0, 2), (1, 2))


def after(array, *others):
    return lax.optimization_barrier((array, *others))[0]


def ring(own, far, up, down, others, between):
    own_l, own_r = send(own, up), send(own, down)
    far = after(far, own_l, own_r, *others)
    far_l, far_r = send(far, up), send(far, down)
    others = between([own, far, own_l, own_r])
    own_l, far_r = after(own_l, far_l, *others), after(far_r, far_l, *others)
    own_ll, far_rr = send(own_l, up), send(far_r, down)
    return [own, far, own_l, own_r, far_l, far_r, own_ll, far_rr]


def token_kernel(count, first, has_before, last, info, *refs):
    pieces, refs = refs[:8], list(refs[8:])
    before = refs.pop(0) if has_before else None
    blocks, (out, wide, scratch, wide_sems, sems) = refs[:count], refs[count:]
    blocks = [blocks[n // 4 * 2 + n % 2].at[n // 2 % 2] for n in range(2 * count)]
    count = len(blocks)
    height = blocks[0].shape[0]

    def block_copy(n):
        rows = pl.ds(n * HALF, height)
        return pltpu.make_async_copy(blocks[n], scratch.at[rows, :], sems.at[n])

    def token_copy(n, piece=0):
        return pltpu.make_async_copy(pieces[piece], wide.at[n], wide_sems.at[n])

    def rows_of(m, n):
        start = pl.multiple_of(m * TILE, TILE)
        low, high = wide[n, pl.ds(start, TILE), :HALF], wide[n, pl.ds(start, TILE), HALF:]
        swapped = info[8] == 1
        return jnp.where(swapped, high, low), jnp.where(swapped, low, high)

    def finish(total):
        if has_before:
            total += before[...]
        if last:
            middle = total.shape[1] // 2
            gate = total[:, :middle]
            total = gate / (1.0 + jnp.exp(-gate)) * total[:, middle:]
        out[...] = total.astype(out.dtype)

    m = pl.program_id(0)

    @pl.when(m == 0)
    def _():
        for n in range(count // 2):
            for piece in range(len(pieces)):

                @pl.when(info[first + n] == piece)
                def _():
                    token_copy(n, piece).start()

            block_copy(2 * n).start()
            block_copy(2 * n + 1).start()
        for n in range(count):
            scratch[n * HALF + height : (n + 1) * HALF, :] = jnp.zeros(
                (HALF - height, scratch.shape[1]), scratch.dtype
            )
        for n in range(count // 2):
            token_copy(n).wait()
            block_copy(2 * n).wait()
            block_copy(2 * n + 1).wait()

    rows = jnp.concatenate([part for n in range(count // 2) for part in rows_of(m, n)], axis=1)
    finish(jnp.dot(rows, scratch[...], preferred_element_type=jnp.float32))


def token_sum(info, tokens, first, blocks, before=None, last=False):
    rows, columns = tokens[0].shape[0], blocks[0].shape[2]
    count = 2 * len(blocks)
    width = columns // 2 if last else columns

    def tile(width):
        return pl.BlockSpec((TILE, width), lambda m, info: (m, 0))

    return pl.pallas_call(
        functools.partial(token_kernel, len(blocks), first, before is not None, last),
        out_shape=jax.ShapeDtypeStruct((rows, width), jnp.bfloat16 if last else jnp.float32),
        grid_spec=pltpu.PrefetchScalarGridSpec(
            num_scalar_prefetch=1,
            grid=(rows // TILE,),
            in_specs=[pl.BlockSpec(memory_space=pl.ANY)] * 8
            + ([] if before is None else [tile(columns)])
            + [pl.BlockSpec(memory_space=pl.ANY)] * len(blocks),
            out_specs=tile(width),
            scratch_shapes=[
                pltpu.VMEM((count // 2, rows, 2 * HALF), jnp.bfloat16),
                pltpu.VMEM((count * HALF, columns), jnp.bfloat16),
                pltpu.SemaphoreType.DMA((count // 2,)),
                pltpu.SemaphoreType.DMA((count,)),
            ],
        ),
        compiler_params=pltpu.CompilerParams(vmem_limit_bytes=VMEM_LIMIT),
        cost_estimate=FREE,
    )(info, *tokens, *([] if before is None else [before]), *blocks)


def vmem(n):
    return [pl.BlockSpec(memory_space=pltpu.VMEM)] * n


DOWN_ORDER = ((0, 0), (1, 0), (0, -1), (1, -1), (0, 1), (1, 1), (0, 2), (1, 2))


def down_kernel(info, hidden, mine, theirs, *outs):
    for n, out in enumerate(outs):
        low = jnp.where(info[8] == 0, mine[n], theirs[n])
        high = jnp.where(info[8] == 0, theirs[n], mine[n])
        out[...] = lax.dot_general(
            jnp.concatenate([low, high], axis=1),
            hidden[...],
            (((1,), (1,)), ((), ())),
            preferred_element_type=jnp.float32,
        ).astype(out.dtype)


def down_terms(info, hidden, mine, theirs):
    rows, depth = hidden.shape
    count, columns, _ = mine.shape
    return pl.pallas_call(
        down_kernel,
        out_shape=[jax.ShapeDtypeStruct((columns, rows), jnp.bfloat16)] * count,
        in_specs=[pl.BlockSpec(memory_space=pltpu.SMEM)] + vmem(3),
        out_specs=vmem(count),
        compiler_params=pltpu.CompilerParams(vmem_limit_bytes=VMEM_LIMIT),
        cost_estimate=FREE,
    )(info, hidden, mine, theirs)


def on_device(tokens, gate_master, up_master, down_master):
    fsdp_place = lax.axis_index("fsdp")
    tp_place = lax.axis_index("tp")
    core = fsdp_place % 2
    y_hi, x = fsdp_place // 8, (fsdp_place // 2) % 4
    y_lo, z = tp_place // 4, tp_place % 4
    gate_height, gate_breadth = gate_master.shape
    down_height, down_breadth = down_master.shape
    gate_at = (fsdp_place * gate_height, tp_place * gate_breadth)
    down_at = (fsdp_place * down_height, tp_place * down_breadth)

    half = tokens.shape[1] // 2
    padded = jnp.concatenate(
        [jnp.pad(tokens[:, k * half : (k + 1) * half], ((0, 0), (0, HALF - half))) for k in range(2)],
        axis=1,
    )
    near = send(padded, y_near)
    tokens_l, tokens_r = send(padded, z_up), send(padded, z_down)
    gate_master, up_master, down_master, padded = lax.optimization_barrier(
        (gate_master, up_master, down_master, padded)
    )

    tables = [
        block_maxima(gate_master, *gate_at, D, FF),
        block_maxima(up_master, *gate_at, D, FF),
        block_maxima(down_master, *down_at, FF, D),
    ]
    rows = D // BLOCK + 12
    columns = FF // BLOCK + 56
    pad = lambda a: jnp.pad(a, ((0, rows - a.shape[0]), (0, columns - a.shape[1])))
    table = jnp.concatenate([pad(tables[0]), pad(tables[1]), pad(tables[2].T)])

    def step(table, target):
        return jnp.maximum(table, send(table, target))

    table = step(table, other_core)
    table = step(table, lambda y, x, core, z: (y, x ^ 1, core, z))
    gate_up = jnp.concatenate(
        [
            rollout(gate_master, table[:rows], *gate_at),
            rollout(up_master, table[rows : 2 * rows], *gate_at),
        ],
        axis=1,
    )
    every = step(table, lambda y, x, core, z: (y, x, core, z ^ 1))
    gate_up, near, tokens_l, tokens_r, every = lax.optimization_barrier(
        (gate_up, near, tokens_l, tokens_r, every)
    )
    down_table = every
    near_l, near_r = send(near, z_up), send(near, z_down)
    tokens_l, near_r = after(tokens_l, near_l), after(near_r, near_l)
    tokens_ll, near_rr = send(tokens_l, z_up), send(near_r, z_down)
    pieces = [padded, near, tokens_l, tokens_r, near_l, near_r, tokens_ll, near_rr]
    down_weight = rollout(down_master, down_table[2 * rows : 3 * rows].T, *down_at)
    pairs = []

    def swap(blocks):
        for n in range(0, len(blocks), 2):
            pair = jnp.stack(blocks[n : n + 2])
            pairs.extend((pair, send(pair, other_core)))

    down_block = send(after(down_weight.T, near_l, near_r), to_ff_group)
    down_far = send(down_block, y_far)

    def between(blocks):
        swap(blocks)
        return [pairs[1], pairs[3], down_far]

    blocks = ring(
        gate_up, send(gate_up, y_far), x_up, x_down, (tokens_ll, near_rr, down_block), between
    )
    every = step(after(every, *blocks[:4]), y_near)
    swap(blocks[4:6])

    steps = jnp.array([dy + 4 * (dx % 4) for dy, dx in ORDER] + [0] * 8, jnp.int32)
    chip_y, chip_x = (steps % 4) ^ (y_hi ^ y_lo), (steps // 4 + x - z + 4) % 4
    info = jnp.where(
        chip_x == 0,
        chip_y,
        jnp.where(chip_x == 2, 6 + chip_y, 2 + 2 * chip_y + jnp.where(chip_x == 1, 1, 0)),
    )
    info = jnp.where(jnp.arange(16) == 8, core, info)

    down_pair = jnp.stack([down_block, down_far])
    down_theirs = send(after(down_pair, blocks[4], blocks[5]), other_core)

    early = token_sum(info, pieces, 0, [after(pairs[0], down_theirs)] + pairs[1:])
    early, own_ll, far_rr = lax.optimization_barrier((early, blocks[6], blocks[7]))
    every = step(after(every, early), lambda y, x, core, z: (y, x, core, z ^ 2))
    down_pair = after(down_pair, own_ll)
    left, right = send(down_pair, x_up), send(down_pair, x_down)
    last = jnp.stack([own_ll, far_rr])
    last = [last, send(last, other_core)]
    hidden = token_sum(info, pieces, 6, last, early, last=True)

    def sums(n, mine, theirs, *before):
        terms = down_terms(info, hidden, mine, theirs)
        return [
            send(after(term, *before), to_chunk(*DOWN_ORDER[n + k])) for k, term in enumerate(terms)
        ], terms

    parts, terms = sums(0, down_pair, down_theirs)
    left, right = after(left, *terms), after(right, *terms)
    rest = jnp.stack([send(left[0], x_up), send(right[1], x_down)])
    parts += sums(2, left, send(left, other_core))[0]
    rest = after(rest, *parts[:2])
    parts += sums(4, right, send(right, other_core), *parts[:2])[0]
    more, terms = sums(6, rest, send(rest, other_core), *parts[2:4])
    parts += more
    every = step(after(every, *terms), y_far)
    every = step(every, lambda y, x, core, z: (y, x ^ 2, core, z))
    log_amax = jnp.log(
        jnp.stack([every[k * rows : k * rows + D // BLOCK, : FF // BLOCK] for k in range(3)]) + EPS
    )
    total = sum(part.astype(jnp.float32) for part in parts)
    return total.astype(jnp.bfloat16).T, log_amax


def solution(mesh):
    return jax.shard_map(
        on_device,
        mesh=mesh,
        in_specs=(P("fsdp", "tp"), P("fsdp", "tp"), P("fsdp", "tp"), P("fsdp", "tp")),
        out_specs=(P("fsdp", "tp"), P()),
        check_vma=False,
    )
```

```python
import functools

import jax
import jax.numpy as jnp
from jax import lax
from jax.experimental import pallas as pl
from jax.experimental.pallas import tpu as pltpu
from jax.sharding import PartitionSpec as P

D = 3584
FF = 9216
BLOCK = 128

FP8_MAX = 448.0
EPS = 1e-06
SMALLEST_NORMAL = 2.0 ** (-6)
AXES = ("fsdp", "tp")
VMEM_LIMIT = 60 * 1024 * 1024
TILE = 256
HALF = 256
FREE = pl.CostEstimate(flops=0, bytes_accessed=0, transcendentals=0)


def snapped(value):
    magnitude = jnp.abs(value)
    exponent = jnp.floor(jnp.log2(jnp.maximum(magnitude, SMALLEST_NORMAL)))
    step_size = jnp.exp2(exponent - 3.0)
    return jnp.sign(value) * step_size * jnp.floor(magnitude / step_size + 0.5)


def place(y, x, core, z):
    y, x, z = y % 4, x % 4, z % 4
    return (((y // 2) * 4 + x) * 2 + core) * 8 + (y % 2) * 4 + z


def send(array, target):
    pairs = [
        (place(y, x, core, z), place(*target(y, x, core, z)))
        for y in range(4)
        for x in range(4)
        for core in range(2)
        for z in range(4)
    ]
    return lax.ppermute(array, AXES, pairs)


def x_up(y, x, core, z):
    return y, x + 1, core, z


def x_down(y, x, core, z):
    return y, x - 1, core, z


def z_up(y, x, core, z):
    return y, x, core, z + 1


def z_down(y, x, core, z):
    return y, x, core, z - 1


def y_near(y, x, core, z):
    return y ^ 1, x, core, z


def y_far(y, x, core, z):
    return y + 2, x, core, z


def other_core(y, x, core, z):
    return y, x, 1 - core, z


def to_ff_group(y, x, core, z):
    y_hi, y_lo = y // 2, y % 2
    across = y_lo ^ y_hi
    return across * 2 + y_hi, z - x - 2 * across, core, x


def to_chunk(dy, dx):
    def target(y, x, core, z):
        y_hi, y_lo = y // 2, y % 2
        across = y_hi ^ dy
        return y_hi * 2 + (y_lo ^ across), x, core, z + x + dx + 2 * across

    return target


def block_maxima(local, row_start, column_start, rows, columns):
    height, breadth = local.shape
    span_rows = (height - 1) // BLOCK + 2
    span_columns = (breadth - 1) // BLOCK + 2
    magnitude = jnp.abs(local)
    which_row = (row_start % BLOCK + jnp.arange(height, dtype=jnp.int32)) // BLOCK
    by_row = jnp.stack(
        [
            jnp.max(jnp.where((which_row == k)[:, None], magnitude, 0.0), axis=0)
            for k in range(span_rows)
        ]
    )
    which_column = (column_start % BLOCK + jnp.arange(breadth, dtype=jnp.int32)) // BLOCK
    pick = which_column[None, :] == jnp.arange(span_columns, dtype=jnp.int32)[:, None]
    part = jnp.max(jnp.where(pick[None], by_row[:, None, :], 0.0), axis=2)
    table = jnp.zeros((rows // BLOCK + span_rows, columns // BLOCK + span_columns), jnp.float32)
    return lax.dynamic_update_slice(table, part, (row_start // BLOCK, column_start // BLOCK))


def spread(scales, row_start, height, column_start, breadth):
    span_rows = (height - 1) // BLOCK + 2
    span_columns = (breadth - 1) // BLOCK + 2
    near = lax.dynamic_slice(
        scales, (row_start // BLOCK, column_start // BLOCK), (span_rows, span_columns)
    )
    which_row = (row_start % BLOCK + jnp.arange(height, dtype=jnp.int32)) // BLOCK
    which_column = (column_start % BLOCK + jnp.arange(breadth, dtype=jnp.int32)) // BLOCK
    wide = jnp.zeros((span_rows, breadth), jnp.float32)
    for k in range(span_columns):
        wide = jnp.where((which_column == k)[None, :], near[:, k : k + 1], wide)
    full = jnp.zeros((height, breadth), jnp.float32)
    for k in range(span_rows):
        full = jnp.where((which_row == k)[:, None], wide[k : k + 1, :], full)
    return full


def rollout(master, table, row_start, column_start):
    height, breadth = master.shape
    scale = spread((table + EPS) / FP8_MAX, row_start, height, column_start, breadth)
    return (snapped(master / scale) * scale).astype(jnp.bfloat16)


ORDER = ((0, 0), (1, 0), (0, -1), (0, 1), (1, -1), (1, 1), (0, 2), (1, 2))


def after(array, *others):
    return lax.optimization_barrier((array, *others))[0]


def ring(own, far, up, down, others, between):
    own_l, own_r = send(own, up), send(own, down)
    far = after(far, own_l, own_r, *others)
    far_l, far_r = send(far, up), send(far, down)
    others = between([own, far, own_l, own_r])
    own_l, far_r = after(own_l, far_l, *others), after(far_r, far_l, *others)
    own_ll, far_rr = send(own_l, up), send(far_r, down)
    return [own, far, own_l, own_r, far_l, far_r, own_ll, far_rr]


def token_kernel(count, first, has_before, last, info, *refs):
    pieces, refs = refs[:8], list(refs[8:])
    before = refs.pop(0) if has_before else None
    blocks, (out, wide, scratch, wide_sems, sems) = refs[:count], refs[count:]
    blocks = [blocks[n // 4 * 2 + n % 2].at[n // 2 % 2] for n in range(2 * count)]
    count = len(blocks)
    height = blocks[0].shape[0]

    def block_copy(n):
        rows = pl.ds(n * HALF, height)
        return pltpu.make_async_copy(blocks[n], scratch.at[rows, :], sems.at[n])

    def token_copy(n, piece=0):
        return pltpu.make_async_copy(pieces[piece], wide.at[n], wide_sems.at[n])

    def rows_of(m, n):
        start = pl.multiple_of(m * TILE, TILE)
        low, high = wide[n, pl.ds(start, TILE), :HALF], wide[n, pl.ds(start, TILE), HALF:]
        swapped = info[8] == 1
        return jnp.where(swapped, high, low), jnp.where(swapped, low, high)

    def finish(total):
        if has_before:
            total += before[...]
        if last:
            middle = total.shape[1] // 2
            gate = total[:, :middle]
            total = gate / (1.0 + jnp.exp(-gate)) * total[:, middle:]
        out[...] = total.astype(out.dtype)

    m = pl.program_id(0)

    @pl.when(m == 0)
    def _():
        for n in range(count // 2):
            for piece in range(len(pieces)):

                @pl.when(info[first + n] == piece)
                def _():
                    token_copy(n, piece).start()

            block_copy(2 * n).start()
            block_copy(2 * n + 1).start()
        for n in range(count):
            scratch[n * HALF + height : (n + 1) * HALF, :] = jnp.zeros(
                (HALF - height, scratch.shape[1]), scratch.dtype
            )
        for n in range(count // 2):
            token_copy(n).wait()
            block_copy(2 * n).wait()
            block_copy(2 * n + 1).wait()

    rows = jnp.concatenate([part for n in range(count // 2) for part in rows_of(m, n)], axis=1)
    finish(jnp.dot(rows, scratch[...], preferred_element_type=jnp.float32))


def token_sum(info, tokens, first, blocks, before=None, last=False):
    rows, columns = tokens[0].shape[0], blocks[0].shape[2]
    count = 2 * len(blocks)
    width = columns // 2 if last else columns

    def tile(width):
        return pl.BlockSpec((TILE, width), lambda m, info: (m, 0))

    return pl.pallas_call(
        functools.partial(token_kernel, len(blocks), first, before is not None, last),
        out_shape=jax.ShapeDtypeStruct((rows, width), jnp.bfloat16 if last else jnp.float32),
        grid_spec=pltpu.PrefetchScalarGridSpec(
            num_scalar_prefetch=1,
            grid=(rows // TILE,),
            in_specs=[pl.BlockSpec(memory_space=pl.ANY)] * 8
            + ([] if before is None else [tile(columns)])
            + [pl.BlockSpec(memory_space=pl.ANY)] * len(blocks),
            out_specs=tile(width),
            scratch_shapes=[
                pltpu.VMEM((count // 2, rows, 2 * HALF), jnp.bfloat16),
                pltpu.VMEM((count * HALF, columns), jnp.bfloat16),
                pltpu.SemaphoreType.DMA((count // 2,)),
                pltpu.SemaphoreType.DMA((count,)),
            ],
        ),
        compiler_params=pltpu.CompilerParams(vmem_limit_bytes=VMEM_LIMIT),
        cost_estimate=FREE,
    )(info, *tokens, *([] if before is None else [before]), *blocks)


def vmem(n):
    return [pl.BlockSpec(memory_space=pltpu.VMEM)] * n


def down_kernel(info, hidden, mine, theirs, *outs):
    for n, out in enumerate(outs):
        low = jnp.where(info[8] == 0, mine[n], theirs[n])
        high = jnp.where(info[8] == 0, theirs[n], mine[n])
        out[...] = lax.dot_general(
            jnp.concatenate([low, high], axis=1),
            hidden[...],
            (((1,), (1,)), ((), ())),
            preferred_element_type=jnp.float32,
        ).astype(out.dtype)


def down_terms(info, hidden, mine, theirs):
    rows, depth = hidden.shape
    count, columns, _ = mine.shape
    return pl.pallas_call(
        down_kernel,
        out_shape=[jax.ShapeDtypeStruct((columns, rows), jnp.bfloat16)] * count,
        in_specs=[pl.BlockSpec(memory_space=pltpu.SMEM)] + vmem(3),
        out_specs=vmem(count),
        compiler_params=pltpu.CompilerParams(vmem_limit_bytes=VMEM_LIMIT // 3),
        cost_estimate=FREE,
    )(info, hidden, mine, theirs)


def on_device(tokens, gate_master, up_master, down_master):
    fsdp_place = lax.axis_index("fsdp")
    tp_place = lax.axis_index("tp")
    core = fsdp_place % 2
    y_hi, x = fsdp_place // 8, (fsdp_place // 2) % 4
    y_lo, z = tp_place // 4, tp_place % 4
    gate_height, gate_breadth = gate_master.shape
    down_height, down_breadth = down_master.shape
    gate_at = (fsdp_place * gate_height, tp_place * gate_breadth)
    down_at = (fsdp_place * down_height, tp_place * down_breadth)

    half = tokens.shape[1] // 2
    padded = jnp.concatenate(
        [jnp.pad(tokens[:, k * half : (k + 1) * half], ((0, 0), (0, HALF - half))) for k in range(2)],
        axis=1,
    )
    near = send(padded, y_near)
    tokens_l, tokens_r = send(padded, z_up), send(padded, z_down)
    gate_master, up_master, down_master, padded = lax.optimization_barrier(
        (gate_master, up_master, down_master, padded)
    )

    tables = [
        block_maxima(gate_master, *gate_at, D, FF),
        block_maxima(up_master, *gate_at, D, FF),
        block_maxima(down_master, *down_at, FF, D),
    ]
    rows = D // BLOCK + 12
    columns = FF // BLOCK + 56
    pad = lambda a: jnp.pad(a, ((0, rows - a.shape[0]), (0, columns - a.shape[1])))
    table = jnp.concatenate([pad(tables[0]), pad(tables[1]), pad(tables[2].T)])

    def step(table, target):
        return jnp.maximum(table, send(table, target))

    table = step(table, other_core)
    table = step(table, lambda y, x, core, z: (y, x ^ 1, core, z))
    gate_up = jnp.concatenate(
        [
            rollout(gate_master, table[:rows], *gate_at),
            rollout(up_master, table[rows : 2 * rows], *gate_at),
        ],
        axis=1,
    )
    every = step(table, lambda y, x, core, z: (y, x, core, z ^ 1))
    gate_up, near, tokens_l, tokens_r, every = lax.optimization_barrier(
        (gate_up, near, tokens_l, tokens_r, every)
    )
    down_table = every
    near_l, near_r = send(near, z_up), send(near, z_down)
    tokens_l, near_r = after(tokens_l, near_l), after(near_r, near_l)
    tokens_ll, near_rr = send(tokens_l, z_up), send(near_r, z_down)
    pieces = [padded, near, tokens_l, tokens_r, near_l, near_r, tokens_ll, near_rr]
    down_weight = rollout(down_master, down_table[2 * rows : 3 * rows].T, *down_at)
    pairs = []

    def swap(blocks, *before):
        blocks = [after(block, *before) for block in blocks]
        for n in range(0, len(blocks), 2):
            pair = jnp.stack(blocks[n : n + 2])
            pairs.extend((pair, send(pair, other_core)))

    down_block = send(after(down_weight.T, near_l, near_r), to_ff_group)
    down_far = send(down_block, y_far)
    every = step(after(every, near_l, near_r), y_near)

    def between(blocks):
        swap(blocks[:2], tokens_ll, near_rr)
        return [pairs[1], down_far]

    far = send(gate_up, y_far)
    blocks = ring(gate_up, far, x_up, x_down, (near_l, near_r, down_block, every), between)
    swap(blocks[2:4], blocks[4], blocks[5])
    swap(blocks[4:6])
    every = step(after(every, *blocks[4:6]), lambda y, x, core, z: (y, x, core, z ^ 2))

    steps = jnp.array([dy + 4 * (dx % 4) for dy, dx in ORDER] + [0] * 8, jnp.int32)
    chip_y, chip_x = (steps % 4) ^ (y_hi ^ y_lo), (steps // 4 + x - z + 4) % 4
    info = jnp.where(
        chip_x == 0,
        chip_y,
        jnp.where(chip_x == 2, 6 + chip_y, 2 + 2 * chip_y + jnp.where(chip_x == 1, 1, 0)),
    )
    info = jnp.where(jnp.arange(16) == 8, core, info)

    pairs[0], every = lax.optimization_barrier((pairs[0], every))
    early = token_sum(info, pieces, 0, pairs)
    early, own_ll, far_rr = lax.optimization_barrier((early, blocks[6], blocks[7]))
    every = step(after(every, early), y_far)
    last = jnp.stack([own_ll, far_rr])
    last = [last, send(last, other_core)]
    down_block = after(down_block, own_ll)
    own_l, own_r = send(down_block, x_up), send(down_block, x_down)
    down_pair = jnp.stack([down_block, down_far])
    down_theirs = send(down_pair, other_core)
    hidden = token_sum(info, pieces, 6, last, after(early, down_theirs, every), last=True)

    parts = []

    def sums(mine):
        mine = jnp.stack(mine)
        theirs = send(mine, other_core) if parts else down_theirs
        terms = down_terms(info, hidden, mine, theirs)
        for term in terms:
            parts.append(send(term, to_chunk(*ORDER[len(parts)])))
        return terms

    terms = sums([down_block, down_far])
    far = after(down_far, own_l, own_r)
    far_l, far_r = send(far, x_up), send(far, x_down)
    terms = sums([after(own_l, *terms), own_r])
    terms = sums([far_l, after(far_r, *terms)])
    own_l, far_r = after(own_l, far_l, *parts[:2]), after(far_r, far_l, *parts[:2])
    terms = sums([after(send(own_l, x_up), *parts[2:4]), send(far_r, x_down)])
    every = step(after(every, *terms), lambda y, x, core, z: (y, x ^ 2, core, z))
    log_amax = jnp.log(
        jnp.stack([every[k * rows : k * rows + D // BLOCK, : FF // BLOCK] for k in range(3)]) + EPS
    )
    total = sum(part.astype(jnp.float32) for part in parts)
    return total.astype(jnp.bfloat16).T, log_amax


def solution(mesh):
    return jax.shard_map(
        on_device,
        mesh=mesh,
        in_specs=(P("fsdp", "tp"), P("fsdp", "tp"), P("fsdp", "tp"), P("fsdp", "tp")),
        out_specs=(P("fsdp", "tp"), P()),
        check_vma=False,
    )
```

```python
import functools

import jax
import jax.numpy as jnp
from jax import lax
from jax.experimental import pallas as pl
from jax.experimental.pallas import tpu as pltpu
from jax.sharding import PartitionSpec as P

D = 3584
FF = 9216
BLOCK = 128

FP8_MAX = 448.0
EPS = 1e-06
SMALLEST_NORMAL = 2.0 ** (-6)
AXES = ("fsdp", "tp")
VMEM_LIMIT = 60 * 1024 * 1024
TILE = 256
HALF = 256
FREE = pl.CostEstimate(flops=0, bytes_accessed=0, transcendentals=0)


def snapped(value):
    magnitude = jnp.abs(value)
    exponent = jnp.floor(jnp.log2(jnp.maximum(magnitude, SMALLEST_NORMAL)))
    step_size = jnp.exp2(exponent - 3.0)
    return jnp.sign(value) * step_size * jnp.floor(magnitude / step_size + 0.5)


def place(y, x, core, z):
    y, x, z = y % 4, x % 4, z % 4
    return (((y // 2) * 4 + x) * 2 + core) * 8 + (y % 2) * 4 + z


def send(array, target):
    pairs = [
        (place(y, x, core, z), place(*target(y, x, core, z)))
        for y in range(4)
        for x in range(4)
        for core in range(2)
        for z in range(4)
    ]
    return lax.ppermute(array, AXES, pairs)


def x_up(y, x, core, z):
    return y, x + 1, core, z


def x_down(y, x, core, z):
    return y, x - 1, core, z


def z_up(y, x, core, z):
    return y, x, core, z + 1


def z_down(y, x, core, z):
    return y, x, core, z - 1


def y_near(y, x, core, z):
    return y ^ 1, x, core, z


def y_far(y, x, core, z):
    return y + 2, x, core, z


def other_core(y, x, core, z):
    return y, x, 1 - core, z


def to_ff_group(y, x, core, z):
    y_hi, y_lo = y // 2, y % 2
    across = y_lo ^ y_hi
    return across * 2 + y_hi, z - x - 2 * across, core, x


def to_chunk(dy, dx):
    def target(y, x, core, z):
        y_hi, y_lo = y // 2, y % 2
        across = y_hi ^ dy
        return y_hi * 2 + (y_lo ^ across), x, core, z + x + dx + 2 * across

    return target


def block_maxima(local, row_start, column_start, rows, columns):
    height, breadth = local.shape
    span_rows = (height - 1) // BLOCK + 2
    span_columns = (breadth - 1) // BLOCK + 2
    magnitude = jnp.abs(local)
    which_row = (row_start % BLOCK + jnp.arange(height, dtype=jnp.int32)) // BLOCK
    by_row = jnp.stack(
        [
            jnp.max(jnp.where((which_row == k)[:, None], magnitude, 0.0), axis=0)
            for k in range(span_rows)
        ]
    )
    which_column = (column_start % BLOCK + jnp.arange(breadth, dtype=jnp.int32)) // BLOCK
    pick = which_column[None, :] == jnp.arange(span_columns, dtype=jnp.int32)[:, None]
    part = jnp.max(jnp.where(pick[None], by_row[:, None, :], 0.0), axis=2)
    table = jnp.zeros((rows // BLOCK + span_rows, columns // BLOCK + span_columns), jnp.float32)
    return lax.dynamic_update_slice(table, part, (row_start // BLOCK, column_start // BLOCK))


def spread(scales, row_start, height, column_start, breadth):
    span_rows = (height - 1) // BLOCK + 2
    span_columns = (breadth - 1) // BLOCK + 2
    near = lax.dynamic_slice(
        scales, (row_start // BLOCK, column_start // BLOCK), (span_rows, span_columns)
    )
    which_row = (row_start % BLOCK + jnp.arange(height, dtype=jnp.int32)) // BLOCK
    which_column = (column_start % BLOCK + jnp.arange(breadth, dtype=jnp.int32)) // BLOCK
    wide = jnp.zeros((span_rows, breadth), jnp.float32)
    for k in range(span_columns):
        wide = jnp.where((which_column == k)[None, :], near[:, k : k + 1], wide)
    full = jnp.zeros((height, breadth), jnp.float32)
    for k in range(span_rows):
        full = jnp.where((which_row == k)[:, None], wide[k : k + 1, :], full)
    return full


def rollout(master, table, row_start, column_start):
    height, breadth = master.shape
    scale = spread((table + EPS) / FP8_MAX, row_start, height, column_start, breadth)
    return (snapped(master / scale) * scale).astype(jnp.bfloat16)


ORDER = ((0, 0), (1, 0), (0, -1), (0, 1), (1, -1), (1, 1), (0, 2), (1, 2))


def after(array, *others):
    return lax.optimization_barrier((array, *others))[0]


def ring(own, far, up, down, others, between):
    own_l, own_r = send(own, up), send(own, down)
    far = after(far, own_l, own_r, *others)
    far_l, far_r = send(far, up), send(far, down)
    others = between([own, far, own_l, own_r])
    own_l, far_r = after(own_l, far_l, *others), after(far_r, far_l, *others)
    own_ll, far_rr = send(own_l, up), send(far_r, down)
    return [own, far, own_l, own_r, far_l, far_r, own_ll, far_rr]


def token_kernel(count, first, has_before, last, info, *refs):
    pieces, refs = refs[:8], list(refs[8:])
    before = refs.pop(0) if has_before else None
    blocks, (out, wide, scratch, wide_sems, sems) = refs[:count], refs[count:]
    blocks = [blocks[n // 4 * 2 + n % 2].at[n // 2 % 2] for n in range(2 * count)]
    count = len(blocks)
    height = blocks[0].shape[0]

    def block_copy(n):
        rows = pl.ds(n * HALF, height)
        return pltpu.make_async_copy(blocks[n], scratch.at[rows, :], sems.at[n])

    def token_copy(n, piece=0):
        return pltpu.make_async_copy(pieces[piece], wide.at[n], wide_sems.at[n])

    def rows_of(m, n):
        start = pl.multiple_of(m * TILE, TILE)
        low, high = wide[n, pl.ds(start, TILE), :HALF], wide[n, pl.ds(start, TILE), HALF:]
        swapped = info[8] == 1
        return jnp.where(swapped, high, low), jnp.where(swapped, low, high)

    def finish(total):
        if has_before:
            total += before[...]
        if last:
            middle = total.shape[1] // 2
            gate = total[:, :middle]
            total = gate / (1.0 + jnp.exp(-gate)) * total[:, middle:]
        out[...] = total.astype(out.dtype)

    m = pl.program_id(0)

    @pl.when(m == 0)
    def _():
        for n in range(count // 2):
            for piece in range(len(pieces)):

                @pl.when(info[first + n] == piece)
                def _():
                    token_copy(n, piece).start()

            block_copy(2 * n).start()
            block_copy(2 * n + 1).start()
        for n in range(count):
            scratch[n * HALF + height : (n + 1) * HALF, :] = jnp.zeros(
                (HALF - height, scratch.shape[1]), scratch.dtype
            )
        for n in range(count // 2):
            token_copy(n).wait()
            block_copy(2 * n).wait()
            block_copy(2 * n + 1).wait()

    rows = jnp.concatenate([part for n in range(count // 2) for part in rows_of(m, n)], axis=1)
    finish(jnp.dot(rows, scratch[...], preferred_element_type=jnp.float32))


def token_sum(info, tokens, first, blocks, before=None, last=False):
    rows, columns = tokens[0].shape[0], blocks[0].shape[2]
    count = 2 * len(blocks)
    width = columns // 2 if last else columns

    def tile(width):
        return pl.BlockSpec((TILE, width), lambda m, info: (m, 0))

    return pl.pallas_call(
        functools.partial(token_kernel, len(blocks), first, before is not None, last),
        out_shape=jax.ShapeDtypeStruct((rows, width), jnp.bfloat16 if last else jnp.float32),
        grid_spec=pltpu.PrefetchScalarGridSpec(
            num_scalar_prefetch=1,
            grid=(rows // TILE,),
            in_specs=[pl.BlockSpec(memory_space=pl.ANY)] * 8
            + ([] if before is None else [tile(columns)])
            + [pl.BlockSpec(memory_space=pl.ANY)] * len(blocks),
            out_specs=tile(width),
            scratch_shapes=[
                pltpu.VMEM((count // 2, rows, 2 * HALF), jnp.bfloat16),
                pltpu.VMEM((count * HALF, columns), jnp.bfloat16),
                pltpu.SemaphoreType.DMA((count // 2,)),
                pltpu.SemaphoreType.DMA((count,)),
            ],
        ),
        compiler_params=pltpu.CompilerParams(
            vmem_limit_bytes=VMEM_LIMIT // 3 if last else VMEM_LIMIT
        ),
        cost_estimate=FREE,
    )(info, *tokens, *([] if before is None else [before]), *blocks)


def vmem(n):
    return [pl.BlockSpec(memory_space=pltpu.VMEM)] * n


def down_kernel(info, hidden, mine, theirs, *outs):
    for n, out in enumerate(outs):
        low = jnp.where(info[8] == 0, mine[n], theirs[n])
        high = jnp.where(info[8] == 0, theirs[n], mine[n])
        out[...] = lax.dot_general(
            jnp.concatenate([low, high], axis=1),
            hidden[...],
            (((1,), (1,)), ((), ())),
            preferred_element_type=jnp.float32,
        ).astype(out.dtype)


def down_terms(info, hidden, mine, theirs):
    rows, depth = hidden.shape
    count, columns, _ = mine.shape
    return pl.pallas_call(
        down_kernel,
        out_shape=[jax.ShapeDtypeStruct((columns, rows), jnp.bfloat16)] * count,
        in_specs=[pl.BlockSpec(memory_space=pltpu.SMEM)] + vmem(3),
        out_specs=vmem(count),
        compiler_params=pltpu.CompilerParams(vmem_limit_bytes=VMEM_LIMIT // 3),
        cost_estimate=FREE,
    )(info, hidden, mine, theirs)


def on_device(tokens, gate_master, up_master, down_master):
    fsdp_place = lax.axis_index("fsdp")
    tp_place = lax.axis_index("tp")
    core = fsdp_place % 2
    y_hi, x = fsdp_place // 8, (fsdp_place // 2) % 4
    y_lo, z = tp_place // 4, tp_place % 4
    gate_height, gate_breadth = gate_master.shape
    down_height, down_breadth = down_master.shape
    gate_at = (fsdp_place * gate_height, tp_place * gate_breadth)
    down_at = (fsdp_place * down_height, tp_place * down_breadth)

    half = tokens.shape[1] // 2
    padded = jnp.concatenate(
        [jnp.pad(tokens[:, k * half : (k + 1) * half], ((0, 0), (0, HALF - half))) for k in range(2)],
        axis=1,
    )
    near = send(padded, y_near)
    tokens_l, tokens_r = send(padded, z_up), send(padded, z_down)
    gate_master, up_master, down_master, padded = lax.optimization_barrier(
        (gate_master, up_master, down_master, padded)
    )

    tables = [
        block_maxima(gate_master, *gate_at, D, FF),
        block_maxima(up_master, *gate_at, D, FF),
        block_maxima(down_master, *down_at, FF, D),
    ]
    rows = D // BLOCK + 12
    columns = FF // BLOCK + 56
    pad = lambda a: jnp.pad(a, ((0, rows - a.shape[0]), (0, columns - a.shape[1])))
    table = jnp.concatenate([pad(tables[0]), pad(tables[1]), pad(tables[2].T)])

    def step(table, target):
        return jnp.maximum(table, send(table, target))

    table = step(table, other_core)
    table = step(table, lambda y, x, core, z: (y, x ^ 1, core, z))
    gate_up = jnp.concatenate(
        [
            rollout(gate_master, table[:rows], *gate_at),
            rollout(up_master, table[rows : 2 * rows], *gate_at),
        ],
        axis=1,
    )
    every = step(table, lambda y, x, core, z: (y, x, core, z ^ 1))
    gate_up, every = lax.optimization_barrier((gate_up, every))
    near, tokens_l, tokens_r = lax.optimization_barrier((near, tokens_l, tokens_r))
    down_table = every
    near_l, near_r = send(near, z_up), send(near, z_down)
    tokens_l, near_r = after(tokens_l, near_l), after(near_r, near_l)
    tokens_ll, near_rr = send(tokens_l, z_up), send(near_r, z_down)
    pieces = [padded, near, tokens_l, tokens_r, near_l, near_r, tokens_ll, near_rr]
    down_weight = rollout(down_master, down_table[2 * rows : 3 * rows].T, *down_at)
    pairs = []

    def swap(blocks, *before):
        blocks = [after(block, *before) for block in blocks]
        for n in range(0, len(blocks), 2):
            pair = jnp.stack(blocks[n : n + 2])
            pairs.extend((pair, send(pair, other_core)))

    down_block = send(after(down_weight.T, near_l, near_r), to_ff_group)
    every = step(after(every, near_l, near_r), y_near)

    down_far = None

    def between(blocks):
        nonlocal down_far
        swap(blocks[:2])
        down_far = send(after(down_block, pairs[1]), y_far)
        return [pairs[1], tokens_ll, near_rr]

    far = send(gate_up, y_far)
    blocks = ring(gate_up, far, x_up, x_down, (near_l, near_r, down_block, every), between)
    swap(blocks[2:4], blocks[4], blocks[5], down_far)
    swap(blocks[4:6])

    steps = jnp.array([dy + 4 * (dx % 4) for dy, dx in ORDER] + [0] * 8, jnp.int32)
    chip_y, chip_x = (steps % 4) ^ (y_hi ^ y_lo), (steps // 4 + x - z + 4) % 4
    info = jnp.where(
        chip_x == 0,
        chip_y,
        jnp.where(chip_x == 2, 6 + chip_y, 2 + 2 * chip_y + jnp.where(chip_x == 1, 1, 0)),
    )
    info = jnp.where(jnp.arange(16) == 8, core, info)

    early = token_sum(info, pieces, 0, pairs)
    early, own_ll, far_rr = lax.optimization_barrier((early, blocks[6], blocks[7]))
    every = step(after(every, early), lambda y, x, core, z: (y, x, core, z ^ 2))
    last = jnp.stack([own_ll, far_rr])
    last = [last, send(last, other_core)]
    down_block = after(down_block, own_ll)
    own_l, own_r = send(down_block, x_up), send(down_block, x_down)
    down_pair = jnp.stack([down_block, down_far])
    down_theirs = send(down_pair, other_core)
    hidden = token_sum(info, pieces, 6, last, after(early, down_theirs, every), last=True)

    parts = []

    def sums(mine):
        mine = jnp.stack(mine)
        theirs = send(mine, other_core) if parts else down_theirs
        terms = down_terms(info, hidden, mine, theirs)
        for term in terms:
            parts.append(send(term, to_chunk(*ORDER[len(parts)])))
        return terms

    terms = sums([down_block, down_far])
    far = after(down_far, own_l, own_r)
    far_l, far_r = send(far, x_up), send(far, x_down)
    terms = sums([after(own_l, *terms), own_r])
    sums([far_l, after(far_r, *terms, *parts[:2])])
    own_l, far_r, *_ = lax.optimization_barrier((own_l, far_r, *parts[:2], *terms))
    terms = sums([after(send(own_l, x_up), *parts[2:4]), send(far_r, x_down)])
    every = step(after(every, *terms), y_far)
    every = step(every, lambda y, x, core, z: (y, x ^ 2, core, z))
    log_amax = jnp.log(
        jnp.stack([every[k * rows : k * rows + D // BLOCK, : FF // BLOCK] for k in range(3)]) + EPS
    )
    total = sum(part.astype(jnp.float32) for part in parts)
    return total.astype(jnp.bfloat16).T, log_amax


def solution(mesh):
    return jax.shard_map(
        on_device,
        mesh=mesh,
        in_specs=(P("fsdp", "tp"), P("fsdp", "tp"), P("fsdp", "tp"), P("fsdp", "tp")),
        out_specs=(P("fsdp", "tp"), P()),
        check_vma=False,
    )
```

```python
import functools

import jax
import jax.numpy as jnp
from jax import lax
from jax.experimental import pallas as pl
from jax.experimental.pallas import tpu as pltpu
from jax.sharding import PartitionSpec as P

D = 3584
FF = 9216
BLOCK = 128

FP8_MAX = 448.0
EPS = 1e-06
SMALLEST_NORMAL = 2.0 ** (-6)
AXES = ("fsdp", "tp")
VMEM_LIMIT = 60 * 1024 * 1024
TILE = 256
HALF = 256
FREE = pl.CostEstimate(flops=0, bytes_accessed=0, transcendentals=0)


def snapped(value):
    magnitude = jnp.abs(value)
    exponent = jnp.floor(jnp.log2(jnp.maximum(magnitude, SMALLEST_NORMAL)))
    step_size = jnp.exp2(exponent - 3.0)
    return jnp.sign(value) * step_size * jnp.floor(magnitude / step_size + 0.5)


def place(y, x, core, z):
    y, x, z = y % 4, x % 4, z % 4
    return (((y // 2) * 4 + x) * 2 + core) * 8 + (y % 2) * 4 + z


def send(array, target):
    pairs = [
        (place(y, x, core, z), place(*target(y, x, core, z)))
        for y in range(4)
        for x in range(4)
        for core in range(2)
        for z in range(4)
    ]
    return lax.ppermute(array, AXES, pairs)


def x_up(y, x, core, z):
    return y, x + 1, core, z


def x_down(y, x, core, z):
    return y, x - 1, core, z


def z_up(y, x, core, z):
    return y, x, core, z + 1


def z_down(y, x, core, z):
    return y, x, core, z - 1


def y_near(y, x, core, z):
    return y ^ 1, x, core, z


def y_far(y, x, core, z):
    return y + 2, x, core, z


def other_core(y, x, core, z):
    return y, x, 1 - core, z


def to_ff_group(y, x, core, z):
    y_hi, y_lo = y // 2, y % 2
    across = y_lo ^ y_hi
    return across * 2 + y_hi, z - x - 2 * across, core, x


def to_chunk(dy, dx):
    def target(y, x, core, z):
        y_hi, y_lo = y // 2, y % 2
        across = y_hi ^ dy
        return y_hi * 2 + (y_lo ^ across), x, core, z + x + dx + 2 * across

    return target


def block_maxima(local, row_start, column_start, rows, columns):
    height, breadth = local.shape
    span_rows = (height - 1) // BLOCK + 2
    span_columns = (breadth - 1) // BLOCK + 2
    magnitude = jnp.abs(local)
    which_row = (row_start % BLOCK + jnp.arange(height, dtype=jnp.int32)) // BLOCK
    by_row = jnp.stack(
        [
            jnp.max(jnp.where((which_row == k)[:, None], magnitude, 0.0), axis=0)
            for k in range(span_rows)
        ]
    )
    which_column = (column_start % BLOCK + jnp.arange(breadth, dtype=jnp.int32)) // BLOCK
    pick = which_column[None, :] == jnp.arange(span_columns, dtype=jnp.int32)[:, None]
    part = jnp.max(jnp.where(pick[None], by_row[:, None, :], 0.0), axis=2)
    table = jnp.zeros((rows // BLOCK + span_rows, columns // BLOCK + span_columns), jnp.float32)
    return lax.dynamic_update_slice(table, part, (row_start // BLOCK, column_start // BLOCK))


def spread(scales, row_start, height, column_start, breadth):
    span_rows = (height - 1) // BLOCK + 2
    span_columns = (breadth - 1) // BLOCK + 2
    near = lax.dynamic_slice(
        scales, (row_start // BLOCK, column_start // BLOCK), (span_rows, span_columns)
    )
    which_row = (row_start % BLOCK + jnp.arange(height, dtype=jnp.int32)) // BLOCK
    which_column = (column_start % BLOCK + jnp.arange(breadth, dtype=jnp.int32)) // BLOCK
    wide = jnp.zeros((span_rows, breadth), jnp.float32)
    for k in range(span_columns):
        wide = jnp.where((which_column == k)[None, :], near[:, k : k + 1], wide)
    full = jnp.zeros((height, breadth), jnp.float32)
    for k in range(span_rows):
        full = jnp.where((which_row == k)[:, None], wide[k : k + 1, :], full)
    return full


def rollout(master, table, row_start, column_start):
    height, breadth = master.shape
    scale = spread((table + EPS) / FP8_MAX, row_start, height, column_start, breadth)
    return (snapped(master / scale) * scale).astype(jnp.bfloat16)


ORDER = ((0, 0), (1, 0), (0, -1), (0, 1), (1, -1), (1, 1), (0, 2), (1, 2))


def after(array, *others):
    return lax.optimization_barrier((array, *others))[0]


def ring(own, far, up, down, others, between):
    own_l, own_r = send(own, up), send(own, down)
    far = after(far, own_l, own_r, *others)
    far_l, far_r = send(far, up), send(far, down)
    others = between([own, far, own_l, own_r])
    own_l, far_r = after(own_l, far_l, *others), after(far_r, far_l, *others)
    own_ll, far_rr = send(own_l, up), send(far_r, down)
    return [own, far, own_l, own_r, far_l, far_r, own_ll, far_rr]


def token_kernel(count, first, has_before, last, info, *refs):
    pieces, refs = refs[:8], list(refs[8:])
    before = refs.pop(0) if has_before else None
    blocks, (out, wide, scratch, wide_sems, sems) = refs[:count], refs[count:]
    blocks = [blocks[n // 4 * 2 + n % 2].at[n // 2 % 2] for n in range(2 * count)]
    count = len(blocks)
    height = blocks[0].shape[0]

    def block_copy(n):
        rows = pl.ds(n * HALF, height)
        return pltpu.make_async_copy(blocks[n], scratch.at[rows, :], sems.at[n])

    def token_copy(n, piece=0):
        return pltpu.make_async_copy(pieces[piece], wide.at[n], wide_sems.at[n])

    def rows_of(m, n):
        start = pl.multiple_of(m * TILE, TILE)
        low, high = wide[n, pl.ds(start, TILE), :HALF], wide[n, pl.ds(start, TILE), HALF:]
        swapped = info[8] == 1
        return jnp.where(swapped, high, low), jnp.where(swapped, low, high)

    def finish(total):
        if has_before:
            total += before[...]
        if last:
            middle = total.shape[1] // 2
            gate = total[:, :middle]
            total = gate / (1.0 + jnp.exp(-gate)) * total[:, middle:]
        out[...] = total.astype(out.dtype)

    m = pl.program_id(0)

    @pl.when(m == 0)
    def _():
        for n in range(count // 2):
            for piece in range(len(pieces)):

                @pl.when(info[first + n] == piece)
                def _():
                    token_copy(n, piece).start()

            block_copy(2 * n).start()
            block_copy(2 * n + 1).start()
        for n in range(count):
            scratch[n * HALF + height : (n + 1) * HALF, :] = jnp.zeros(
                (HALF - height, scratch.shape[1]), scratch.dtype
            )
        for n in range(count // 2):
            token_copy(n).wait()
            block_copy(2 * n).wait()
            block_copy(2 * n + 1).wait()

    rows = jnp.concatenate([part for n in range(count // 2) for part in rows_of(m, n)], axis=1)
    finish(jnp.dot(rows, scratch[...], preferred_element_type=jnp.float32))


def token_sum(info, tokens, first, blocks, before=None, last=False):
    rows, columns = tokens[0].shape[0], blocks[0].shape[2]
    count = 2 * len(blocks)
    width = columns // 2 if last else columns

    def tile(width):
        return pl.BlockSpec((TILE, width), lambda m, info: (m, 0))

    return pl.pallas_call(
        functools.partial(token_kernel, len(blocks), first, before is not None, last),
        out_shape=jax.ShapeDtypeStruct((rows, width), jnp.bfloat16 if last else jnp.float32),
        grid_spec=pltpu.PrefetchScalarGridSpec(
            num_scalar_prefetch=1,
            grid=(rows // TILE,),
            in_specs=[pl.BlockSpec(memory_space=pl.ANY)] * 8
            + ([] if before is None else [tile(columns)])
            + [pl.BlockSpec(memory_space=pl.ANY)] * len(blocks),
            out_specs=tile(width),
            scratch_shapes=[
                pltpu.VMEM((count // 2, rows, 2 * HALF), jnp.bfloat16),
                pltpu.VMEM((count * HALF, columns), jnp.bfloat16),
                pltpu.SemaphoreType.DMA((count // 2,)),
                pltpu.SemaphoreType.DMA((count,)),
            ],
        ),
        compiler_params=pltpu.CompilerParams(
            vmem_limit_bytes=VMEM_LIMIT // 3 if last else VMEM_LIMIT
        ),
        cost_estimate=FREE,
    )(info, *tokens, *([] if before is None else [before]), *blocks)


def vmem(n):
    return [pl.BlockSpec(memory_space=pltpu.VMEM)] * n


def down_kernel(info, hidden, mine, theirs, *outs):
    for n, out in enumerate(outs):
        low = jnp.where(info[8] == 0, mine[n], theirs[n])
        high = jnp.where(info[8] == 0, theirs[n], mine[n])
        out[...] = lax.dot_general(
            jnp.concatenate([low, high], axis=1),
            hidden[...],
            (((1,), (1,)), ((), ())),
            preferred_element_type=jnp.float32,
        ).astype(out.dtype)


def down_terms(info, hidden, mine, theirs):
    rows, depth = hidden.shape
    count, columns, _ = mine.shape
    return pl.pallas_call(
        down_kernel,
        out_shape=[jax.ShapeDtypeStruct((columns, rows), jnp.bfloat16)] * count,
        in_specs=[pl.BlockSpec(memory_space=pltpu.SMEM)] + vmem(3),
        out_specs=vmem(count),
        compiler_params=pltpu.CompilerParams(vmem_limit_bytes=VMEM_LIMIT // 3),
        cost_estimate=pl.CostEstimate(
            flops=4 * rows * columns * depth, bytes_accessed=12 * rows * columns, transcendentals=0
        ),
    )(info, hidden, mine, theirs)


def on_device(tokens, gate_master, up_master, down_master):
    fsdp_place = lax.axis_index("fsdp")
    tp_place = lax.axis_index("tp")
    core = fsdp_place % 2
    y_hi, x = fsdp_place // 8, (fsdp_place // 2) % 4
    y_lo, z = tp_place // 4, tp_place % 4
    gate_height, gate_breadth = gate_master.shape
    down_height, down_breadth = down_master.shape
    gate_at = (fsdp_place * gate_height, tp_place * gate_breadth)
    down_at = (fsdp_place * down_height, tp_place * down_breadth)

    half = tokens.shape[1] // 2
    padded = jnp.concatenate(
        [jnp.pad(tokens[:, k * half : (k + 1) * half], ((0, 0), (0, HALF - half))) for k in range(2)],
        axis=1,
    )
    near = send(padded, y_near)
    tokens_l, tokens_r = send(padded, z_up), send(padded, z_down)
    gate_master, up_master, down_master, padded = lax.optimization_barrier(
        (gate_master, up_master, down_master, padded)
    )

    tables = [
        block_maxima(gate_master, *gate_at, D, FF),
        block_maxima(up_master, *gate_at, D, FF),
        block_maxima(down_master, *down_at, FF, D),
    ]
    rows = D // BLOCK + 12
    columns = FF // BLOCK + 56
    pad = lambda a: jnp.pad(a, ((0, rows - a.shape[0]), (0, columns - a.shape[1])))
    table = jnp.concatenate([pad(tables[0]), pad(tables[1]), pad(tables[2].T)])

    def step(table, target):
        return jnp.maximum(table, send(table, target))

    table = step(table, other_core)
    table = step(table, lambda y, x, core, z: (y, x ^ 1, core, z))
    gate_up = jnp.concatenate(
        [
            rollout(gate_master, table[:rows], *gate_at),
            rollout(up_master, table[rows : 2 * rows], *gate_at),
        ],
        axis=1,
    )
    every = step(table, lambda y, x, core, z: (y, x, core, z ^ 1))
    gate_up, every = lax.optimization_barrier((gate_up, every))
    near, tokens_l, tokens_r = lax.optimization_barrier((near, tokens_l, tokens_r))
    down_table = every
    near_l, near_r = send(near, z_up), send(near, z_down)
    tokens_l, near_r = after(tokens_l, near_l), after(near_r, near_l)
    tokens_ll, near_rr = send(tokens_l, z_up), send(near_r, z_down)
    pieces = [padded, near, tokens_l, tokens_r, near_l, near_r, tokens_ll, near_rr]
    down_weight = rollout(down_master, down_table[2 * rows : 3 * rows].T, *down_at)
    pairs = []

    def swap(blocks, *before):
        blocks = [after(block, *before) for block in blocks]
        for n in range(0, len(blocks), 2):
            pair = jnp.stack(blocks[n : n + 2])
            pairs.extend((pair, send(pair, other_core)))

    down_block = send(after(down_weight.T, near_l, near_r), to_ff_group)
    every = step(after(every, near_l, near_r), y_near)

    down_far = None

    def between(blocks):
        nonlocal down_far
        swap(blocks[:2])
        down_far = send(after(down_block, pairs[1]), y_far)
        return [pairs[1], tokens_ll, near_rr]

    far = send(gate_up, y_far)
    blocks = ring(gate_up, far, x_up, x_down, (near_l, near_r, down_block, every), between)
    swap(blocks[2:4], blocks[4], blocks[5], down_far)
    swap(blocks[4:6])

    steps = jnp.array([dy + 4 * (dx % 4) for dy, dx in ORDER] + [0] * 8, jnp.int32)
    chip_y, chip_x = (steps % 4) ^ (y_hi ^ y_lo), (steps // 4 + x - z + 4) % 4
    info = jnp.where(
        chip_x == 0,
        chip_y,
        jnp.where(chip_x == 2, 6 + chip_y, 2 + 2 * chip_y + jnp.where(chip_x == 1, 1, 0)),
    )
    info = jnp.where(jnp.arange(16) == 8, core, info)

    down_pair = jnp.stack([down_block, down_far])
    down_theirs = send(down_pair, other_core)
    pairs[0] = after(pairs[0], down_theirs)
    early = token_sum(info, pieces, 0, pairs)
    early, own_ll, far_rr = lax.optimization_barrier((early, blocks[6], blocks[7]))
    every = step(after(every, early), lambda y, x, core, z: (y, x, core, z ^ 2))
    last = jnp.stack([own_ll, far_rr])
    last = [last, send(last, other_core)]
    down_block, down_far = after(down_block, own_ll), after(down_far, own_ll)
    own_l, own_r = send(down_block, x_up), send(down_block, x_down)
    far_l, far_r = send(down_far, x_up), send(down_far, x_down)
    hidden = token_sum(info, pieces, 6, last, after(early, every), last=True)

    parts = []

    def sums(mine, *before):
        mine = jnp.stack(mine) if parts else down_pair
        theirs = send(mine, other_core) if parts else down_theirs
        terms = down_terms(info, hidden, mine, theirs)
        for term in terms:
            parts.append(send(after(term, *before), to_chunk(*ORDER[len(parts)])))
        return terms

    every = step(every, y_far)
    terms = sums((), every)
    terms = sums([after(own_l, *terms), own_r])
    own_l, far_r, *_ = lax.optimization_barrier((own_l, far_r, far_l, *parts[:2], *terms))
    own_ll, far_rr = send(own_l, x_up), send(far_r, x_down)
    terms = sums([far_l, after(far_r, *terms)])
    terms = sums([own_ll, after(far_rr, *terms, *parts[2:4])])
    every = step(after(every, *terms), lambda y, x, core, z: (y, x ^ 2, core, z))
    log_amax = jnp.log(
        jnp.stack([every[k * rows : k * rows + D // BLOCK, : FF // BLOCK] for k in range(3)]) + EPS
    )
    total = sum(part.astype(jnp.float32) for part in parts)
    return total.astype(jnp.bfloat16).T, log_amax


def solution(mesh):
    return jax.shard_map(
        on_device,
        mesh=mesh,
        in_specs=(P("fsdp", "tp"), P("fsdp", "tp"), P("fsdp", "tp"), P("fsdp", "tp")),
        out_specs=(P("fsdp", "tp"), P()),
        check_vma=False,
    )
```

```python
import functools

import jax
import jax.numpy as jnp
from jax import lax
from jax.experimental import pallas as pl
from jax.experimental.pallas import tpu as pltpu
from jax.sharding import PartitionSpec as P

D = 3584
FF = 9216
BLOCK = 128

FP8_MAX = 448.0
EPS = 1e-06
SMALLEST_NORMAL = 2.0 ** (-6)
AXES = ("fsdp", "tp")
VMEM_LIMIT = 60 * 1024 * 1024
TILE = 256
HALF = 256
FREE = pl.CostEstimate(flops=0, bytes_accessed=0, transcendentals=0)


def snapped(value):
    magnitude = jnp.abs(value)
    exponent = jnp.floor(jnp.log2(jnp.maximum(magnitude, SMALLEST_NORMAL)))
    step_size = jnp.exp2(exponent - 3.0)
    return jnp.sign(value) * step_size * jnp.floor(magnitude / step_size + 0.5)


def place(y, x, core, z):
    y, x, z = y % 4, x % 4, z % 4
    return (((y // 2) * 4 + x) * 2 + core) * 8 + (y % 2) * 4 + z


def send(array, target):
    pairs = [
        (place(y, x, core, z), place(*target(y, x, core, z)))
        for y in range(4)
        for x in range(4)
        for core in range(2)
        for z in range(4)
    ]
    return lax.ppermute(array, AXES, pairs)


def x_up(y, x, core, z):
    return y, x + 1, core, z


def x_down(y, x, core, z):
    return y, x - 1, core, z


def z_up(y, x, core, z):
    return y, x, core, z + 1


def z_down(y, x, core, z):
    return y, x, core, z - 1


def y_near(y, x, core, z):
    return y ^ 1, x, core, z


def y_far(y, x, core, z):
    return y + 2, x, core, z


def other_core(y, x, core, z):
    return y, x, 1 - core, z


def to_ff_group(y, x, core, z):
    y_hi, y_lo = y // 2, y % 2
    across = y_lo ^ y_hi
    return across * 2 + y_hi, z - x - 2 * across, core, x


def to_chunk(dy, dx):
    def target(y, x, core, z):
        y_hi, y_lo = y // 2, y % 2
        across = y_hi ^ dy
        return y_hi * 2 + (y_lo ^ across), x, core, z + x + dx + 2 * across

    return target


def block_maxima(local, row_start, column_start, rows, columns):
    height, breadth = local.shape
    span_rows = (height - 1) // BLOCK + 2
    span_columns = (breadth - 1) // BLOCK + 2
    magnitude = jnp.abs(local)
    which_row = (row_start % BLOCK + jnp.arange(height, dtype=jnp.int32)) // BLOCK
    by_row = jnp.stack(
        [
            jnp.max(jnp.where((which_row == k)[:, None], magnitude, 0.0), axis=0)
            for k in range(span_rows)
        ]
    )
    which_column = (column_start % BLOCK + jnp.arange(breadth, dtype=jnp.int32)) // BLOCK
    pick = which_column[None, :] == jnp.arange(span_columns, dtype=jnp.int32)[:, None]
    part = jnp.max(jnp.where(pick[None], by_row[:, None, :], 0.0), axis=2)
    table = jnp.zeros((rows // BLOCK + span_rows, columns // BLOCK + span_columns), jnp.float32)
    return lax.dynamic_update_slice(table, part, (row_start // BLOCK, column_start // BLOCK))


def spread(scales, row_start, height, column_start, breadth):
    span_rows = (height - 1) // BLOCK + 2
    span_columns = (breadth - 1) // BLOCK + 2
    near = lax.dynamic_slice(
        scales, (row_start // BLOCK, column_start // BLOCK), (span_rows, span_columns)
    )
    which_row = (row_start % BLOCK + jnp.arange(height, dtype=jnp.int32)) // BLOCK
    which_column = (column_start % BLOCK + jnp.arange(breadth, dtype=jnp.int32)) // BLOCK
    wide = jnp.zeros((span_rows, breadth), jnp.float32)
    for k in range(span_columns):
        wide = jnp.where((which_column == k)[None, :], near[:, k : k + 1], wide)
    full = jnp.zeros((height, breadth), jnp.float32)
    for k in range(span_rows):
        full = jnp.where((which_row == k)[:, None], wide[k : k + 1, :], full)
    return full


def rollout(master, table, row_start, column_start):
    height, breadth = master.shape
    scale = spread((table + EPS) / FP8_MAX, row_start, height, column_start, breadth)
    return (snapped(master / scale) * scale).astype(jnp.bfloat16)


ORDER = ((0, 0), (1, 0), (0, -1), (0, 1), (1, -1), (1, 1), (0, 2), (1, 2))


def after(array, *others):
    return lax.optimization_barrier((array, *others))[0]


def ring(own, far, up, down, others, between):
    own_l, own_r = send(own, up), send(own, down)
    far = after(far, own_l, own_r, *others)
    far_l, far_r = send(far, up), send(far, down)
    others = between([own, far, own_l, own_r])
    own_l, far_r = after(own_l, far_l, *others), after(far_r, far_l, *others)
    own_ll, far_rr = send(own_l, up), send(far_r, down)
    return [own, far, own_l, own_r, far_l, far_r, own_ll, far_rr]


def token_kernel(count, first, has_before, last, info, *refs):
    pieces, refs = refs[:8], list(refs[8:])
    before = refs.pop(0) if has_before else None
    blocks, (out, wide, scratch, wide_sems, sems) = refs[:count], refs[count:]
    blocks = [blocks[n // 4 * 2 + n % 2].at[n // 2 % 2] for n in range(2 * count)]
    count = len(blocks)
    height = blocks[0].shape[0]

    def block_copy(n):
        rows = pl.ds(n * HALF, height)
        return pltpu.make_async_copy(blocks[n], scratch.at[rows, :], sems.at[n])

    def token_copy(n, piece=0):
        return pltpu.make_async_copy(pieces[piece], wide.at[n], wide_sems.at[n])

    def rows_of(m, n):
        start = pl.multiple_of(m * TILE, TILE)
        low, high = wide[n, pl.ds(start, TILE), :HALF], wide[n, pl.ds(start, TILE), HALF:]
        swapped = info[8] == 1
        return jnp.where(swapped, high, low), jnp.where(swapped, low, high)

    def finish(total):
        if has_before:
            total += before[...]
        if last:
            middle = total.shape[1] // 2
            gate = total[:, :middle]
            total = gate / (1.0 + jnp.exp(-gate)) * total[:, middle:]
        out[...] = total.astype(out.dtype)

    m = pl.program_id(0)

    @pl.when(m == 0)
    def _():
        for n in range(count // 2):
            for piece in range(len(pieces)):

                @pl.when(info[first + n] == piece)
                def _():
                    token_copy(n, piece).start()

            block_copy(2 * n).start()
            block_copy(2 * n + 1).start()
        for n in range(count):
            scratch[n * HALF + height : (n + 1) * HALF, :] = jnp.zeros(
                (HALF - height, scratch.shape[1]), scratch.dtype
            )
        for n in range(count // 2):
            token_copy(n).wait()
            block_copy(2 * n).wait()
            block_copy(2 * n + 1).wait()

    rows = jnp.concatenate([part for n in range(count // 2) for part in rows_of(m, n)], axis=1)
    finish(jnp.dot(rows, scratch[...], preferred_element_type=jnp.float32))


def token_sum(info, tokens, first, blocks, before=None, last=False):
    rows, columns = tokens[0].shape[0], blocks[0].shape[2]
    count = 2 * len(blocks)
    width = columns // 2 if last else columns

    def tile(width):
        return pl.BlockSpec((TILE, width), lambda m, info: (m, 0))

    return pl.pallas_call(
        functools.partial(token_kernel, len(blocks), first, before is not None, last),
        out_shape=jax.ShapeDtypeStruct((rows, width), jnp.bfloat16 if last else jnp.float32),
        grid_spec=pltpu.PrefetchScalarGridSpec(
            num_scalar_prefetch=1,
            grid=(rows // TILE,),
            in_specs=[pl.BlockSpec(memory_space=pl.ANY)] * 8
            + ([] if before is None else [tile(columns)])
            + [pl.BlockSpec(memory_space=pl.ANY)] * len(blocks),
            out_specs=tile(width),
            scratch_shapes=[
                pltpu.VMEM((count // 2, rows, 2 * HALF), jnp.bfloat16),
                pltpu.VMEM((count * HALF, columns), jnp.bfloat16),
                pltpu.SemaphoreType.DMA((count // 2,)),
                pltpu.SemaphoreType.DMA((count,)),
            ],
        ),
        compiler_params=pltpu.CompilerParams(
            vmem_limit_bytes=VMEM_LIMIT // 3 if last else VMEM_LIMIT
        ),
        cost_estimate=FREE,
    )(info, *tokens, *([] if before is None else [before]), *blocks)


def vmem(n):
    return [pl.BlockSpec(memory_space=pltpu.VMEM)] * n


def down_kernel(info, hidden, mine, theirs, *outs):
    for n, out in enumerate(outs):
        low = jnp.where(info[8] == 0, mine[n], theirs[n])
        high = jnp.where(info[8] == 0, theirs[n], mine[n])
        out[...] = lax.dot_general(
            jnp.concatenate([low, high], axis=1),
            hidden[...],
            (((1,), (1,)), ((), ())),
            preferred_element_type=jnp.float32,
        ).astype(out.dtype)


def down_terms(info, hidden, mine, theirs):
    rows, depth = hidden.shape
    count, columns, _ = mine.shape
    return pl.pallas_call(
        down_kernel,
        out_shape=[jax.ShapeDtypeStruct((columns, rows), jnp.bfloat16)] * count,
        in_specs=[pl.BlockSpec(memory_space=pltpu.SMEM)] + vmem(3),
        out_specs=vmem(count),
        compiler_params=pltpu.CompilerParams(vmem_limit_bytes=VMEM_LIMIT // 3),
        cost_estimate=pl.CostEstimate(
            flops=4 * rows * columns * depth, bytes_accessed=12 * rows * columns, transcendentals=0
        ),
    )(info, hidden, mine, theirs)


def on_device(tokens, gate_master, up_master, down_master):
    fsdp_place = lax.axis_index("fsdp")
    tp_place = lax.axis_index("tp")
    core = fsdp_place % 2
    y_hi, x = fsdp_place // 8, (fsdp_place // 2) % 4
    y_lo, z = tp_place // 4, tp_place % 4
    gate_height, gate_breadth = gate_master.shape
    down_height, down_breadth = down_master.shape
    gate_at = (fsdp_place * gate_height, tp_place * gate_breadth)
    down_at = (fsdp_place * down_height, tp_place * down_breadth)

    half = tokens.shape[1] // 2
    padded = jnp.concatenate(
        [jnp.pad(tokens[:, k * half : (k + 1) * half], ((0, 0), (0, HALF - half))) for k in range(2)],
        axis=1,
    )
    near = send(padded, y_near)
    tokens_l, tokens_r = send(padded, z_up), send(padded, z_down)
    gate_master, up_master, down_master, padded = lax.optimization_barrier(
        (gate_master, up_master, down_master, padded)
    )

    tables = [
        block_maxima(gate_master, *gate_at, D, FF),
        block_maxima(up_master, *gate_at, D, FF),
        block_maxima(down_master, *down_at, FF, D),
    ]
    rows = D // BLOCK + 12
    columns = FF // BLOCK + 56
    pad = lambda a: jnp.pad(a, ((0, rows - a.shape[0]), (0, columns - a.shape[1])))
    table = jnp.concatenate([pad(tables[0]), pad(tables[1]), pad(tables[2].T)])

    def step(table, target):
        return jnp.maximum(table, send(table, target))

    table = step(table, other_core)
    table = step(table, lambda y, x, core, z: (y, x ^ 1, core, z))
    gate_up = jnp.concatenate(
        [
            rollout(gate_master, table[:rows], *gate_at),
            rollout(up_master, table[rows : 2 * rows], *gate_at),
        ],
        axis=1,
    )
    every = step(table, lambda y, x, core, z: (y, x, core, z ^ 1))
    gate_up, every = lax.optimization_barrier((gate_up, every))
    near, tokens_l, tokens_r = lax.optimization_barrier((near, tokens_l, tokens_r))
    down_table = every
    near_l, near_r = send(near, z_up), send(near, z_down)
    tokens_l, near_r = after(tokens_l, near_l), after(near_r, near_l)
    tokens_ll, near_rr = send(tokens_l, z_up), send(near_r, z_down)
    pieces = [padded, near, tokens_l, tokens_r, near_l, near_r, tokens_ll, near_rr]
    down_weight = rollout(down_master, down_table[2 * rows : 3 * rows].T, *down_at)
    pairs = []

    def swap(blocks, *before):
        blocks = [after(block, *before) for block in blocks]
        for n in range(0, len(blocks), 2):
            pair = jnp.stack(blocks[n : n + 2])
            pairs.extend((pair, send(pair, other_core)))

    down_block = send(after(down_weight.T, near_l, near_r), to_ff_group)
    every = step(after(every, near_l, near_r), y_near)

    down_far = None

    def between(blocks):
        nonlocal down_far
        swap(blocks[:2])
        down_far = send(after(down_block, pairs[1]), y_far)
        return [pairs[1], tokens_ll, near_rr]

    far = send(gate_up, y_far)
    blocks = ring(gate_up, far, x_up, x_down, (near_l, near_r, down_block, every), between)
    swap(blocks[2:4], blocks[4], blocks[5], down_far)
    swap(blocks[4:6])

    steps = jnp.array([dy + 4 * (dx % 4) for dy, dx in ORDER] + [0] * 8, jnp.int32)
    chip_y, chip_x = (steps % 4) ^ (y_hi ^ y_lo), (steps // 4 + x - z + 4) % 4
    info = jnp.where(
        chip_x == 0,
        chip_y,
        jnp.where(chip_x == 2, 6 + chip_y, 2 + 2 * chip_y + jnp.where(chip_x == 1, 1, 0)),
    )
    info = jnp.where(jnp.arange(16) == 8, core, info)

    down_pair = jnp.stack([down_block, down_far])
    down_theirs = send(down_pair, other_core)
    pairs[0] = after(pairs[0], down_theirs)
    early = token_sum(info, pieces, 0, pairs)
    early, own_ll, far_rr = lax.optimization_barrier((early, blocks[6], blocks[7]))
    every = step(after(every, early), lambda y, x, core, z: (y, x, core, z ^ 2))
    last = jnp.stack([own_ll, far_rr])
    last = [last, send(last, other_core)]
    down_block, down_far = after(down_block, own_ll), after(down_far, own_ll)
    own_l, own_r = send(down_block, x_up), send(down_block, x_down)
    far_l, far_r = send(down_far, x_up), send(down_far, x_down)
    hidden = token_sum(info, pieces, 6, last, after(early, every), last=True)

    parts = []

    def sums(mine, *before):
        mine = jnp.stack(mine) if parts else down_pair
        theirs = send(mine, other_core) if parts else down_theirs
        terms = down_terms(info, hidden, mine, theirs)
        for term in terms:
            parts.append(send(after(term, *before), to_chunk(*ORDER[len(parts)])))
        return terms

    every = step(every, y_far)
    terms = sums((), far_l, far_r, every)
    terms = sums([after(own_l, *terms), own_r])
    own_l, far_r, *_ = lax.optimization_barrier((own_l, far_r, far_l, *parts[:2], *terms))
    own_ll, far_rr = send(own_l, x_up), send(far_r, x_down)
    terms = sums([far_l, after(far_r, *terms)])
    terms = sums([own_ll, after(far_rr, *terms, *parts[2:4])])
    every = step(after(every, *terms), lambda y, x, core, z: (y, x ^ 2, core, z))
    log_amax = jnp.log(
        jnp.stack([every[k * rows : k * rows + D // BLOCK, : FF // BLOCK] for k in range(3)]) + EPS
    )
    total = sum(part.astype(jnp.float32) for part in parts)
    return total.astype(jnp.bfloat16).T, log_amax


def solution(mesh):
    return jax.shard_map(
        on_device,
        mesh=mesh,
        in_specs=(P("fsdp", "tp"), P("fsdp", "tp"), P("fsdp", "tp"), P("fsdp", "tp")),
        out_specs=(P("fsdp", "tp"), P()),
        check_vma=False,
    )
```

```python
import functools

import jax
import jax.numpy as jnp
from jax import lax
from jax.experimental import pallas as pl
from jax.experimental.pallas import tpu as pltpu
from jax.sharding import PartitionSpec as P

D = 3584
FF = 9216
BLOCK = 128

FP8_MAX = 448.0
EPS = 1e-06
SMALLEST_NORMAL = 2.0 ** (-6)
AXES = ("fsdp", "tp")
VMEM_LIMIT = 60 * 1024 * 1024
TILE = 256
HALF = 256
FREE = pl.CostEstimate(flops=0, bytes_accessed=0, transcendentals=0)
HIDDEN_COST = pl.CostEstimate(flops=4_000_000_000, bytes_accessed=30_000_000, transcendentals=0)


def snapped(value):
    magnitude = jnp.abs(value)
    exponent = jnp.floor(jnp.log2(jnp.maximum(magnitude, SMALLEST_NORMAL)))
    step_size = jnp.exp2(exponent - 3.0)
    return jnp.sign(value) * step_size * jnp.floor(magnitude / step_size + 0.5)


def place(y, x, core, z):
    y, x, z = y % 4, x % 4, z % 4
    return (((y // 2) * 4 + x) * 2 + core) * 8 + (y % 2) * 4 + z


def send(array, target):
    pairs = [
        (place(y, x, core, z), place(*target(y, x, core, z)))
        for y in range(4)
        for x in range(4)
        for core in range(2)
        for z in range(4)
    ]
    return lax.ppermute(array, AXES, pairs)


def x_up(y, x, core, z):
    return y, x + 1, core, z


def x_down(y, x, core, z):
    return y, x - 1, core, z


def z_up(y, x, core, z):
    return y, x, core, z + 1


def z_down(y, x, core, z):
    return y, x, core, z - 1


def y_near(y, x, core, z):
    return y ^ 1, x, core, z


def y_far(y, x, core, z):
    return y + 2, x, core, z


def other_core(y, x, core, z):
    return y, x, 1 - core, z


def to_ff_group(y, x, core, z):
    y_hi, y_lo = y // 2, y % 2
    across = y_lo ^ y_hi
    return across * 2 + y_hi, z - x - 2 * across, core, x


def to_chunk(dy, dx):
    def target(y, x, core, z):
        y_hi, y_lo = y // 2, y % 2
        across = y_hi ^ dy
        return y_hi * 2 + (y_lo ^ across), x, core, z + x + dx + 2 * across

    return target


def block_maxima(local, row_start, column_start, rows, columns):
    height, breadth = local.shape
    span_rows = (height - 1) // BLOCK + 2
    span_columns = (breadth - 1) // BLOCK + 2
    magnitude = jnp.abs(local)
    which_row = (row_start % BLOCK + jnp.arange(height, dtype=jnp.int32)) // BLOCK
    by_row = jnp.stack(
        [
            jnp.max(jnp.where((which_row == k)[:, None], magnitude, 0.0), axis=0)
            for k in range(span_rows)
        ]
    )
    which_column = (column_start % BLOCK + jnp.arange(breadth, dtype=jnp.int32)) // BLOCK
    pick = which_column[None, :] == jnp.arange(span_columns, dtype=jnp.int32)[:, None]
    part = jnp.max(jnp.where(pick[None], by_row[:, None, :], 0.0), axis=2)
    table = jnp.zeros((rows // BLOCK + span_rows, columns // BLOCK + span_columns), jnp.float32)
    return lax.dynamic_update_slice(table, part, (row_start // BLOCK, column_start // BLOCK))


def spread(scales, row_start, height, column_start, breadth):
    span_rows = (height - 1) // BLOCK + 2
    span_columns = (breadth - 1) // BLOCK + 2
    near = lax.dynamic_slice(
        scales, (row_start // BLOCK, column_start // BLOCK), (span_rows, span_columns)
    )
    which_row = (row_start % BLOCK + jnp.arange(height, dtype=jnp.int32)) // BLOCK
    which_column = (column_start % BLOCK + jnp.arange(breadth, dtype=jnp.int32)) // BLOCK
    wide = jnp.zeros((span_rows, breadth), jnp.float32)
    for k in range(span_columns):
        wide = jnp.where((which_column == k)[None, :], near[:, k : k + 1], wide)
    full = jnp.zeros((height, breadth), jnp.float32)
    for k in range(span_rows):
        full = jnp.where((which_row == k)[:, None], wide[k : k + 1, :], full)
    return full


def rollout(master, table, row_start, column_start):
    height, breadth = master.shape
    scale = spread((table + EPS) / FP8_MAX, row_start, height, column_start, breadth)
    return (snapped(master / scale) * scale).astype(jnp.bfloat16)


ORDER = ((0, 0), (1, 0), (0, -1), (0, 1), (1, -1), (1, 1), (0, 2), (1, 2))


def after(array, *others):
    return lax.optimization_barrier((array, *others))[0]


def ring(own, far, up, down, others, between):
    own_l, own_r = send(own, up), send(own, down)
    far = after(far, own_l, own_r, *others)
    far_l, far_r = send(far, up), send(far, down)
    others = between([own, far, own_l, own_r])
    own_l, far_r = after(own_l, far_l, *others), after(far_r, far_l, *others)
    own_ll, far_rr = send(own_l, up), send(far_r, down)
    return [own, far, own_l, own_r, far_l, far_r, own_ll, far_rr]


def token_kernel(count, first, has_before, last, info, *refs):
    pieces, refs = refs[:8], list(refs[8:])
    before = refs.pop(0) if has_before else None
    blocks, (out, wide, scratch, wide_sems, sems) = refs[:count], refs[count:]
    blocks = [blocks[n // 4 * 2 + n % 2].at[n // 2 % 2] for n in range(2 * count)]
    count = len(blocks)
    height = blocks[0].shape[0]

    def block_copy(n):
        rows = pl.ds(n * HALF, height)
        return pltpu.make_async_copy(blocks[n], scratch.at[rows, :], sems.at[n])

    def token_copy(n, piece=0):
        return pltpu.make_async_copy(pieces[piece], wide.at[n], wide_sems.at[n])

    def rows_of(m, n):
        start = pl.multiple_of(m * TILE, TILE)
        low, high = wide[n, pl.ds(start, TILE), :HALF], wide[n, pl.ds(start, TILE), HALF:]
        swapped = info[8] == 1
        return jnp.where(swapped, high, low), jnp.where(swapped, low, high)

    def finish(total):
        if has_before:
            total += before[...]
        if last:
            middle = total.shape[1] // 2
            gate = total[:, :middle]
            total = gate / (1.0 + jnp.exp(-gate)) * total[:, middle:]
        out[...] = total.astype(out.dtype)

    m = pl.program_id(0)

    @pl.when(m == 0)
    def _():
        for n in range(count // 2):
            for piece in range(len(pieces)):

                @pl.when(info[first + n] == piece)
                def _():
                    token_copy(n, piece).start()

            block_copy(2 * n).start()
            block_copy(2 * n + 1).start()
        for n in range(count):
            scratch[n * HALF + height : (n + 1) * HALF, :] = jnp.zeros(
                (HALF - height, scratch.shape[1]), scratch.dtype
            )
        total = None
        for n in range(count // 2):
            token_copy(n).wait()
            block_copy(2 * n).wait()
            block_copy(2 * n + 1).wait()
            product = jnp.dot(
                jnp.concatenate(rows_of(0, n), axis=1),
                scratch[2 * n * HALF : 2 * (n + 1) * HALF, :],
                preferred_element_type=jnp.float32,
            )
            total = product if total is None else total + product
        finish(total)

    @pl.when(m > 0)
    def _():
        rows = jnp.concatenate([part for n in range(count // 2) for part in rows_of(m, n)], axis=1)
        finish(jnp.dot(rows, scratch[...], preferred_element_type=jnp.float32))


def token_sum(info, tokens, first, blocks, before=None, last=False):
    rows, columns = tokens[0].shape[0], blocks[0].shape[2]
    count = 2 * len(blocks)
    width = columns // 2 if last else columns

    def tile(width):
        return pl.BlockSpec((TILE, width), lambda m, info: (m, 0))

    return pl.pallas_call(
        functools.partial(token_kernel, len(blocks), first, before is not None, last),
        out_shape=jax.ShapeDtypeStruct((rows, width), jnp.bfloat16 if last else jnp.float32),
        grid_spec=pltpu.PrefetchScalarGridSpec(
            num_scalar_prefetch=1,
            grid=(rows // TILE,),
            in_specs=[pl.BlockSpec(memory_space=pl.ANY)] * 8
            + ([] if before is None else [tile(columns)])
            + [pl.BlockSpec(memory_space=pl.ANY)] * len(blocks),
            out_specs=tile(width),
            scratch_shapes=[
                pltpu.VMEM((count // 2, rows, 2 * HALF), jnp.bfloat16),
                pltpu.VMEM((count * HALF, columns), jnp.bfloat16),
                pltpu.SemaphoreType.DMA((count // 2,)),
                pltpu.SemaphoreType.DMA((count,)),
            ],
        ),
        compiler_params=pltpu.CompilerParams(
            vmem_limit_bytes=VMEM_LIMIT // 3 if last else VMEM_LIMIT
        ),
        cost_estimate=HIDDEN_COST if last else FREE,
    )(info, *tokens, *([] if before is None else [before]), *blocks)


def vmem(n):
    return [pl.BlockSpec(memory_space=pltpu.VMEM)] * n


def down_kernel(info, hidden, mine, theirs, *outs):
    for n, out in enumerate(outs):
        low = jnp.where(info[8] == 0, mine[n], theirs[n])
        high = jnp.where(info[8] == 0, theirs[n], mine[n])
        out[...] = lax.dot_general(
            jnp.concatenate([low, high], axis=1),
            hidden[...],
            (((1,), (1,)), ((), ())),
            preferred_element_type=jnp.float32,
        ).astype(out.dtype)


def down_terms(info, hidden, mine, theirs):
    rows, depth = hidden.shape
    count, columns, _ = mine.shape
    return pl.pallas_call(
        down_kernel,
        out_shape=[jax.ShapeDtypeStruct((columns, rows), jnp.bfloat16)] * count,
        in_specs=[pl.BlockSpec(memory_space=pltpu.SMEM)] + vmem(3),
        out_specs=vmem(count),
        compiler_params=pltpu.CompilerParams(vmem_limit_bytes=VMEM_LIMIT // 3),
        cost_estimate=pl.CostEstimate(
            flops=4 * rows * columns * depth, bytes_accessed=12 * rows * columns, transcendentals=0
        ),
    )(info, hidden, mine, theirs)


def on_device(tokens, gate_master, up_master, down_master):
    fsdp_place = lax.axis_index("fsdp")
    tp_place = lax.axis_index("tp")
    core = fsdp_place % 2
    y_hi, x = fsdp_place // 8, (fsdp_place // 2) % 4
    y_lo, z = tp_place // 4, tp_place % 4
    gate_height, gate_breadth = gate_master.shape
    down_height, down_breadth = down_master.shape
    gate_at = (fsdp_place * gate_height, tp_place * gate_breadth)
    down_at = (fsdp_place * down_height, tp_place * down_breadth)

    half = tokens.shape[1] // 2
    padded = jnp.concatenate(
        [jnp.pad(tokens[:, k * half : (k + 1) * half], ((0, 0), (0, HALF - half))) for k in range(2)],
        axis=1,
    )
    near = send(padded, y_near)
    tokens_l, tokens_r = send(padded, z_up), send(padded, z_down)
    gate_master, up_master, down_master, padded = lax.optimization_barrier(
        (gate_master, up_master, down_master, padded)
    )

    tables = [
        block_maxima(gate_master, *gate_at, D, FF),
        block_maxima(up_master, *gate_at, D, FF),
        block_maxima(down_master, *down_at, FF, D),
    ]
    rows = D // BLOCK + 12
    columns = FF // BLOCK + 56
    pad = lambda a: jnp.pad(a, ((0, rows - a.shape[0]), (0, columns - a.shape[1])))
    table = jnp.concatenate([pad(tables[0]), pad(tables[1]), pad(tables[2].T)])

    def step(table, target):
        return jnp.maximum(table, send(table, target))

    table = step(table, other_core)
    table = step(table, lambda y, x, core, z: (y, x ^ 1, core, z))
    gate_up = jnp.concatenate(
        [
            rollout(gate_master, table[:rows], *gate_at),
            rollout(up_master, table[rows : 2 * rows], *gate_at),
        ],
        axis=1,
    )
    every = step(table, lambda y, x, core, z: (y, x, core, z ^ 1))
    gate_up, every = lax.optimization_barrier((gate_up, every))
    near, tokens_l, tokens_r = lax.optimization_barrier((near, tokens_l, tokens_r))
    down_table = every
    near_l, near_r = send(near, z_up), send(near, z_down)
    tokens_l, near_r = after(tokens_l, near_l), after(near_r, near_l)
    tokens_ll, near_rr = send(tokens_l, z_up), send(near_r, z_down)
    pieces = [padded, near, tokens_l, tokens_r, near_l, near_r, tokens_ll, near_rr]
    down_weight = rollout(down_master, down_table[2 * rows : 3 * rows].T, *down_at)
    pairs = []

    def swap(blocks, *before):
        blocks = [after(block, *before) for block in blocks]
        for n in range(0, len(blocks), 2):
            pair = jnp.stack(blocks[n : n + 2])
            pairs.extend((pair, send(pair, other_core)))

    down_block = send(after(down_weight.T, near_l, near_r), to_ff_group)

    down_far = None

    def between(blocks):
        nonlocal down_far
        swap(blocks[:2])
        down_far = send(after(down_block, pairs[1]), y_far)
        return [pairs[1], tokens_ll, near_rr]

    far = send(gate_up, y_far)
    blocks = ring(gate_up, far, x_up, x_down, (near_l, near_r, down_block), between)
    swap(blocks[2:4], blocks[4], blocks[5], down_far)
    swap(blocks[4:6])

    steps = jnp.array([dy + 4 * (dx % 4) for dy, dx in ORDER] + [0] * 8, jnp.int32)
    chip_y, chip_x = (steps % 4) ^ (y_hi ^ y_lo), (steps // 4 + x - z + 4) % 4
    info = jnp.where(
        chip_x == 0,
        chip_y,
        jnp.where(chip_x == 2, 6 + chip_y, 2 + 2 * chip_y + jnp.where(chip_x == 1, 1, 0)),
    )
    info = jnp.where(jnp.arange(16) == 8, core, info)

    down_pair = jnp.stack([down_block, down_far])
    down_theirs = send(down_pair, other_core)
    pairs[0] = after(pairs[0], down_theirs)
    early = token_sum(info, pieces, 0, pairs)
    early, own_ll, far_rr = lax.optimization_barrier((early, blocks[6], blocks[7]))
    last = jnp.stack([own_ll, far_rr])
    last = [last, send(last, other_core)]
    down_block, down_far = after(down_block, own_ll), after(down_far, own_ll)
    own_l, own_r = send(down_block, x_up), send(down_block, x_down)
    far_l, far_r = send(down_far, x_up), send(down_far, x_down)
    hidden = token_sum(info, pieces, 6, last, early, last=True)
    every = step(after(every, early), lambda y, x, core, z: (y, x, core, z ^ 2))

    parts = []

    def sums(mine, *before):
        mine = jnp.stack(mine) if parts else down_pair
        theirs = send(mine, other_core) if parts else down_theirs
        terms = down_terms(info, hidden, mine, theirs)
        for term in terms:
            parts.append(send(after(term, *before), to_chunk(*ORDER[len(parts)])))
        return terms

    terms = sums((), far_l, far_r, every)
    terms = sums([after(own_l, *terms), own_r])
    own_l, far_r, far_l, every, *_ = lax.optimization_barrier(
        (own_l, far_r, far_l, every, *parts[:2], *terms)
    )
    own_ll, far_rr = send(own_l, x_up), send(far_r, x_down)
    terms = sums([far_l, after(far_r, *terms)])
    every = step(after(every, *terms), y_near)
    terms = sums([own_ll, after(far_rr, every, *terms, *parts[2:4])])
    every = step(after(every, *terms), y_far)
    every = step(every, lambda y, x, core, z: (y, x ^ 2, core, z))
    log_amax = jnp.log(
        jnp.stack([every[k * rows : k * rows + D // BLOCK, : FF // BLOCK] for k in range(3)]) + EPS
    )
    total = sum(part.astype(jnp.float32) for part in parts)
    return total.astype(jnp.bfloat16).T, log_amax


def solution(mesh):
    return jax.shard_map(
        on_device,
        mesh=mesh,
        in_specs=(P("fsdp", "tp"), P("fsdp", "tp"), P("fsdp", "tp"), P("fsdp", "tp")),
        out_specs=(P("fsdp", "tp"), P()),
        check_vma=False,
    )
```

```python
import functools

import jax
import jax.numpy as jnp
from jax import lax
from jax.experimental import pallas as pl
from jax.experimental.pallas import tpu as pltpu
from jax.sharding import PartitionSpec as P

D = 3584
FF = 9216
BLOCK = 128

FP8_MAX = 448.0
EPS = 1e-06
SMALLEST_NORMAL = 2.0 ** (-6)
AXES = ("fsdp", "tp")
VMEM_LIMIT = 60 * 1024 * 1024
TILE = 256
HALF = 256
FREE = pl.CostEstimate(flops=0, bytes_accessed=0, transcendentals=0)


def snapped(value):
    magnitude = jnp.abs(value)
    exponent = jnp.floor(jnp.log2(jnp.maximum(magnitude, SMALLEST_NORMAL)))
    step_size = jnp.exp2(exponent - 3.0)
    return jnp.sign(value) * step_size * jnp.floor(magnitude / step_size + 0.5)


def place(y, x, core, z):
    y, x, z = y % 4, x % 4, z % 4
    return (((y // 2) * 4 + x) * 2 + core) * 8 + (y % 2) * 4 + z


def send(array, target):
    pairs = [
        (place(y, x, core, z), place(*target(y, x, core, z)))
        for y in range(4)
        for x in range(4)
        for core in range(2)
        for z in range(4)
    ]
    return lax.ppermute(array, AXES, pairs)


def x_up(y, x, core, z):
    return y, x + 1, core, z


def x_down(y, x, core, z):
    return y, x - 1, core, z


def z_up(y, x, core, z):
    return y, x, core, z + 1


def z_down(y, x, core, z):
    return y, x, core, z - 1


def y_near(y, x, core, z):
    return y ^ 1, x, core, z


def y_far(y, x, core, z):
    return y + 2, x, core, z


def other_core(y, x, core, z):
    return y, x, 1 - core, z


def to_ff_group(y, x, core, z):
    y_hi, y_lo = y // 2, y % 2
    across = y_lo ^ y_hi
    return across * 2 + y_hi, z - x - 2 * across, core, x


def to_chunk(dy, dx):
    def target(y, x, core, z):
        y_hi, y_lo = y // 2, y % 2
        across = y_hi ^ dy
        return y_hi * 2 + (y_lo ^ across), x, core, z + x + dx + 2 * across

    return target


def block_maxima(local, row_start, column_start, rows, columns):
    height, breadth = local.shape
    span_rows = (height - 1) // BLOCK + 2
    span_columns = (breadth - 1) // BLOCK + 2
    magnitude = jnp.abs(local)
    which_row = (row_start % BLOCK + jnp.arange(height, dtype=jnp.int32)) // BLOCK
    by_row = jnp.stack(
        [
            jnp.max(jnp.where((which_row == k)[:, None], magnitude, 0.0), axis=0)
            for k in range(span_rows)
        ]
    )
    which_column = (column_start % BLOCK + jnp.arange(breadth, dtype=jnp.int32)) // BLOCK
    pick = which_column[None, :] == jnp.arange(span_columns, dtype=jnp.int32)[:, None]
    part = jnp.max(jnp.where(pick[None], by_row[:, None, :], 0.0), axis=2)
    table = jnp.zeros((rows // BLOCK + span_rows, columns // BLOCK + span_columns), jnp.float32)
    return lax.dynamic_update_slice(table, part, (row_start // BLOCK, column_start // BLOCK))


def spread(scales, row_start, height, column_start, breadth):
    span_rows = (height - 1) // BLOCK + 2
    span_columns = (breadth - 1) // BLOCK + 2
    near = lax.dynamic_slice(
        scales, (row_start // BLOCK, column_start // BLOCK), (span_rows, span_columns)
    )
    which_row = (row_start % BLOCK + jnp.arange(height, dtype=jnp.int32)) // BLOCK
    which_column = (column_start % BLOCK + jnp.arange(breadth, dtype=jnp.int32)) // BLOCK
    wide = jnp.zeros((span_rows, breadth), jnp.float32)
    for k in range(span_columns):
        wide = jnp.where((which_column == k)[None, :], near[:, k : k + 1], wide)
    full = jnp.zeros((height, breadth), jnp.float32)
    for k in range(span_rows):
        full = jnp.where((which_row == k)[:, None], wide[k : k + 1, :], full)
    return full


def rollout(master, table, row_start, column_start):
    height, breadth = master.shape
    scale = spread((table + EPS) / FP8_MAX, row_start, height, column_start, breadth)
    return (snapped(master / scale) * scale).astype(jnp.bfloat16)


ORDER = ((0, 0), (1, 0), (0, -1), (0, 1), (1, -1), (1, 1), (0, 2), (1, 2))


def after(array, *others):
    return lax.optimization_barrier((array, *others))[0]


def ring(own, far, up, down, others, between):
    own_l, own_r = send(own, up), send(own, down)
    far = after(far, own_l, own_r, *others)
    far_l, far_r = send(far, up), send(far, down)
    others = between([own, far, own_l, own_r])
    own_l, far_r = after(own_l, far_l, *others), after(far_r, far_l, *others)
    own_ll, far_rr = send(own_l, up), send(far_r, down)
    return [own, far, own_l, own_r, far_l, far_r, own_ll, far_rr]


def token_kernel(count, first, has_before, last, info, *refs):
    pieces, refs = refs[:8], list(refs[8:])
    before = refs.pop(0) if has_before else None
    blocks, (out, wide, scratch, wide_sems, sems) = refs[:count], refs[count:]
    blocks = [blocks[n // 4 * 2 + n % 2].at[n // 2 % 2] for n in range(2 * count)]
    count = len(blocks)
    height = blocks[0].shape[0]

    def block_copy(n):
        rows = pl.ds(n * HALF, height)
        return pltpu.make_async_copy(blocks[n], scratch.at[rows, :], sems.at[n])

    def token_copy(n, piece=0):
        return pltpu.make_async_copy(pieces[piece], wide.at[n], wide_sems.at[n])

    def rows_of(m, n):
        start = pl.multiple_of(m * TILE, TILE)
        low, high = wide[n, pl.ds(start, TILE), :HALF], wide[n, pl.ds(start, TILE), HALF:]
        swapped = info[8] == 1
        return jnp.where(swapped, high, low), jnp.where(swapped, low, high)

    def finish(total):
        if has_before:
            total += before[...]
        if last:
            middle = total.shape[1] // 2
            gate = total[:, :middle]
            total = gate / (1.0 + jnp.exp(-gate)) * total[:, middle:]
        out[...] = total.astype(out.dtype)

    m = pl.program_id(0)

    @pl.when(m == 0)
    def _():
        for n in range(count // 2):
            for piece in range(len(pieces)):

                @pl.when(info[first + n] == piece)
                def _():
                    token_copy(n, piece).start()

            block_copy(2 * n).start()
            block_copy(2 * n + 1).start()
        for n in range(count):
            scratch[n * HALF + height : (n + 1) * HALF, :] = jnp.zeros(
                (HALF - height, scratch.shape[1]), scratch.dtype
            )
        total = None
        for n in range(count // 2):
            token_copy(n).wait()
            block_copy(2 * n).wait()
            block_copy(2 * n + 1).wait()
            product = jnp.dot(
                jnp.concatenate(rows_of(0, n), axis=1),
                scratch[2 * n * HALF : 2 * (n + 1) * HALF, :],
                preferred_element_type=jnp.float32,
            )
            total = product if total is None else total + product
        finish(total)

    @pl.when(m > 0)
    def _():
        rows = jnp.concatenate([part for n in range(count // 2) for part in rows_of(m, n)], axis=1)
        finish(jnp.dot(rows, scratch[...], preferred_element_type=jnp.float32))


def token_sum(info, tokens, first, blocks, before=None, last=False):
    rows, columns = tokens[0].shape[0], blocks[0].shape[2]
    count = 2 * len(blocks)
    width = columns // 2 if last else columns

    def tile(width):
        return pl.BlockSpec((TILE, width), lambda m, info: (m, 0))

    return pl.pallas_call(
        functools.partial(token_kernel, len(blocks), first, before is not None, last),
        out_shape=jax.ShapeDtypeStruct((rows, width), jnp.bfloat16 if last else jnp.float32),
        grid_spec=pltpu.PrefetchScalarGridSpec(
            num_scalar_prefetch=1,
            grid=(rows // TILE,),
            in_specs=[pl.BlockSpec(memory_space=pl.ANY)] * 8
            + ([] if before is None else [tile(columns)])
            + [pl.BlockSpec(memory_space=pl.ANY)] * len(blocks),
            out_specs=tile(width),
            scratch_shapes=[
                pltpu.VMEM((count // 2, rows, 2 * HALF), jnp.bfloat16),
                pltpu.VMEM((count * HALF, columns), jnp.bfloat16),
                pltpu.SemaphoreType.DMA((count // 2,)),
                pltpu.SemaphoreType.DMA((count,)),
            ],
        ),
        compiler_params=pltpu.CompilerParams(
            vmem_limit_bytes=VMEM_LIMIT // 3 if last else VMEM_LIMIT
        ),
        cost_estimate=FREE,
    )(info, *tokens, *([] if before is None else [before]), *blocks)


def vmem(n):
    return [pl.BlockSpec(memory_space=pltpu.VMEM)] * n


def down_kernel(info, hidden, mine, theirs, *outs):
    for n, out in enumerate(outs):
        low = jnp.where(info[8] == 0, mine[n], theirs[n])
        high = jnp.where(info[8] == 0, theirs[n], mine[n])
        out[...] = lax.dot_general(
            jnp.concatenate([low, high], axis=1),
            hidden[...],
            (((1,), (1,)), ((), ())),
            preferred_element_type=jnp.float32,
        ).astype(out.dtype)


def down_terms(info, hidden, mine, theirs):
    rows, depth = hidden.shape
    count, columns, _ = mine.shape
    return pl.pallas_call(
        down_kernel,
        out_shape=[jax.ShapeDtypeStruct((columns, rows), jnp.bfloat16)] * count,
        in_specs=[pl.BlockSpec(memory_space=pltpu.SMEM)] + vmem(3),
        out_specs=vmem(count),
        compiler_params=pltpu.CompilerParams(vmem_limit_bytes=VMEM_LIMIT // 3),
        cost_estimate=pl.CostEstimate(
            flops=4 * rows * columns * depth, bytes_accessed=12 * rows * columns, transcendentals=0
        ),
    )(info, hidden, mine, theirs)


def on_device(tokens, gate_master, up_master, down_master):
    fsdp_place = lax.axis_index("fsdp")
    tp_place = lax.axis_index("tp")
    core = fsdp_place % 2
    y_hi, x = fsdp_place // 8, (fsdp_place // 2) % 4
    y_lo, z = tp_place // 4, tp_place % 4
    gate_height, gate_breadth = gate_master.shape
    down_height, down_breadth = down_master.shape
    gate_at = (fsdp_place * gate_height, tp_place * gate_breadth)
    down_at = (fsdp_place * down_height, tp_place * down_breadth)

    half = tokens.shape[1] // 2
    padded = jnp.concatenate(
        [jnp.pad(tokens[:, k * half : (k + 1) * half], ((0, 0), (0, HALF - half))) for k in range(2)],
        axis=1,
    )
    near = send(padded, y_near)
    tokens_l, tokens_r = send(padded, z_up), send(padded, z_down)
    gate_master, up_master, down_master, padded = lax.optimization_barrier(
        (gate_master, up_master, down_master, padded)
    )

    tables = [
        block_maxima(gate_master, *gate_at, D, FF),
        block_maxima(up_master, *gate_at, D, FF),
        block_maxima(down_master, *down_at, FF, D),
    ]
    rows = D // BLOCK + 12
    columns = FF // BLOCK + 56
    pad = lambda a: jnp.pad(a, ((0, rows - a.shape[0]), (0, columns - a.shape[1])))
    table = jnp.concatenate([pad(tables[0]), pad(tables[1]), pad(tables[2].T)])

    def step(table, target):
        return jnp.maximum(table, send(table, target))

    table = step(table, other_core)
    table = step(table, lambda y, x, core, z: (y, x ^ 1, core, z))
    gate_up = jnp.concatenate(
        [
            rollout(gate_master, table[:rows], *gate_at),
            rollout(up_master, table[rows : 2 * rows], *gate_at),
        ],
        axis=1,
    )
    every = step(table, lambda y, x, core, z: (y, x, core, z ^ 1))
    gate_up, every = lax.optimization_barrier((gate_up, every))
    near, tokens_l, tokens_r = lax.optimization_barrier((near, tokens_l, tokens_r))
    down_table = every
    down_weight = rollout(down_master, down_table[2 * rows : 3 * rows].T, *down_at)
    down_block = send(down_weight.T, to_ff_group)
    near, down_block = lax.optimization_barrier((near, down_block))
    near_l, near_r = send(near, z_up), send(near, z_down)
    tokens_l, near_r = after(tokens_l, near_l), after(near_r, near_l)
    tokens_ll, near_rr = send(tokens_l, z_up), send(near_r, z_down)
    pieces = [padded, near, tokens_l, tokens_r, near_l, near_r, tokens_ll, near_rr]
    pairs = []

    def swap(blocks, *before):
        blocks = [after(block, *before) for block in blocks]
        for n in range(0, len(blocks), 2):
            pair = jnp.stack(blocks[n : n + 2])
            pairs.extend((pair, send(pair, other_core)))


    down_far = None

    def between(blocks):
        nonlocal down_far
        swap(blocks[:2])
        down_far = send(after(down_block, pairs[1]), y_far)
        return [pairs[1], tokens_ll, near_rr]

    far = send(gate_up, y_far)
    blocks = ring(gate_up, far, x_up, x_down, (near_l, near_r), between)
    swap(blocks[2:4], blocks[4], blocks[5], down_far)
    swap(blocks[4:6])

    steps = jnp.array([dy + 4 * (dx % 4) for dy, dx in ORDER] + [0] * 8, jnp.int32)
    chip_y, chip_x = (steps % 4) ^ (y_hi ^ y_lo), (steps // 4 + x - z + 4) % 4
    info = jnp.where(
        chip_x == 0,
        chip_y,
        jnp.where(chip_x == 2, 6 + chip_y, 2 + 2 * chip_y + jnp.where(chip_x == 1, 1, 0)),
    )
    info = jnp.where(jnp.arange(16) == 8, core, info)

    down_pair = jnp.stack([down_block, down_far])
    down_theirs = send(down_pair, other_core)
    pairs[0] = after(pairs[0], down_theirs)
    early = token_sum(info, pieces, 0, pairs)
    early, own_ll, far_rr = lax.optimization_barrier((early, blocks[6], blocks[7]))
    every = step(after(every, early), lambda y, x, core, z: (y, x, core, z ^ 2))
    last = jnp.stack([own_ll, far_rr])
    last = [last, send(last, other_core)]
    down_block, down_far = after(down_block, own_ll), after(down_far, own_ll)
    own_l, own_r = send(down_block, x_up), send(down_block, x_down)
    far_l, far_r = send(down_far, x_up), send(down_far, x_down)
    hidden = token_sum(info, pieces, 6, last, after(early, every), last=True)

    parts = []

    def sums(mine, *before):
        mine = jnp.stack(mine) if parts else down_pair
        theirs = send(mine, other_core) if parts else down_theirs
        terms = down_terms(info, hidden, mine, theirs)
        for term in terms:
            parts.append(send(after(term, *before), to_chunk(*ORDER[len(parts)])))
        return terms

    every = step(step(every, y_far), y_near)
    terms = sums((), far_l, far_r, every)
    terms = sums([after(own_l, *terms), own_r])
    own_l, far_r, *_ = lax.optimization_barrier((own_l, far_r, far_l, *parts[:2], *terms))
    own_ll, far_rr = send(own_l, x_up), send(far_r, x_down)
    terms = sums([far_l, after(far_r, *terms)])
    terms = sums([own_ll, after(far_rr, *terms, *parts[2:4])])
    every = step(after(every, *terms), lambda y, x, core, z: (y, x ^ 2, core, z))
    log_amax = jnp.log(
        jnp.stack([every[k * rows : k * rows + D // BLOCK, : FF // BLOCK] for k in range(3)]) + EPS
    )
    total = sum(part.astype(jnp.float32) for part in parts)
    return total.astype(jnp.bfloat16).T, log_amax


def solution(mesh):
    return jax.shard_map(
        on_device,
        mesh=mesh,
        in_specs=(P("fsdp", "tp"), P("fsdp", "tp"), P("fsdp", "tp"), P("fsdp", "tp")),
        out_specs=(P("fsdp", "tp"), P()),
        check_vma=False,
    )
```

```python
import functools

import jax
import jax.numpy as jnp
from jax import lax
from jax.experimental import pallas as pl
from jax.experimental.pallas import tpu as pltpu
from jax.sharding import PartitionSpec as P

D = 3584
FF = 9216
BLOCK = 128

FP8_MAX = 448.0
EPS = 1e-06
SMALLEST_NORMAL = 2.0 ** (-6)
AXES = ("fsdp", "tp")
VMEM_LIMIT = 60 * 1024 * 1024
TILE = 256
HALF = 256
FREE = pl.CostEstimate(flops=0, bytes_accessed=0, transcendentals=0)


def snapped(value):
    magnitude = jnp.abs(value)
    exponent = jnp.floor(jnp.log2(jnp.maximum(magnitude, SMALLEST_NORMAL)))
    step_size = jnp.exp2(exponent - 3.0)
    return jnp.sign(value) * step_size * jnp.floor(magnitude / step_size + 0.5)


def place(y, x, core, z):
    y, x, z = y % 4, x % 4, z % 4
    return (((y // 2) * 4 + x) * 2 + core) * 8 + (y % 2) * 4 + z


def send(array, target):
    pairs = [
        (place(y, x, core, z), place(*target(y, x, core, z)))
        for y in range(4)
        for x in range(4)
        for core in range(2)
        for z in range(4)
    ]
    return lax.ppermute(array, AXES, pairs)


def x_up(y, x, core, z):
    return y, x + 1, core, z


def x_down(y, x, core, z):
    return y, x - 1, core, z


def z_up(y, x, core, z):
    return y, x, core, z + 1


def z_down(y, x, core, z):
    return y, x, core, z - 1


def y_near(y, x, core, z):
    return y ^ 1, x, core, z


def y_far(y, x, core, z):
    return y + 2, x, core, z


def other_core(y, x, core, z):
    return y, x, 1 - core, z


def to_ff_group(y, x, core, z):
    y_hi, y_lo = y // 2, y % 2
    across = y_lo ^ y_hi
    return across * 2 + y_hi, z - x - 2 * across, core, x


def to_chunk(dy, dx):
    def target(y, x, core, z):
        y_hi, y_lo = y // 2, y % 2
        across = y_hi ^ dy
        return y_hi * 2 + (y_lo ^ across), x, core, z + x + dx + 2 * across

    return target


def block_maxima(local, row_start, column_start, rows, columns):
    height, breadth = local.shape
    span_rows = (height - 1) // BLOCK + 2
    span_columns = (breadth - 1) // BLOCK + 2
    magnitude = jnp.abs(local)
    which_row = (row_start % BLOCK + jnp.arange(height, dtype=jnp.int32)) // BLOCK
    by_row = jnp.stack(
        [
            jnp.max(jnp.where((which_row == k)[:, None], magnitude, 0.0), axis=0)
            for k in range(span_rows)
        ]
    )
    which_column = (column_start % BLOCK + jnp.arange(breadth, dtype=jnp.int32)) // BLOCK
    pick = which_column[None, :] == jnp.arange(span_columns, dtype=jnp.int32)[:, None]
    part = jnp.max(jnp.where(pick[None], by_row[:, None, :], 0.0), axis=2)
    table = jnp.zeros((rows // BLOCK + span_rows, columns // BLOCK + span_columns), jnp.float32)
    return lax.dynamic_update_slice(table, part, (row_start // BLOCK, column_start // BLOCK))


def spread(scales, row_start, height, column_start, breadth):
    span_rows = (height - 1) // BLOCK + 2
    span_columns = (breadth - 1) // BLOCK + 2
    near = lax.dynamic_slice(
        scales, (row_start // BLOCK, column_start // BLOCK), (span_rows, span_columns)
    )
    which_row = (row_start % BLOCK + jnp.arange(height, dtype=jnp.int32)) // BLOCK
    which_column = (column_start % BLOCK + jnp.arange(breadth, dtype=jnp.int32)) // BLOCK
    wide = jnp.zeros((span_rows, breadth), jnp.float32)
    for k in range(span_columns):
        wide = jnp.where((which_column == k)[None, :], near[:, k : k + 1], wide)
    full = jnp.zeros((height, breadth), jnp.float32)
    for k in range(span_rows):
        full = jnp.where((which_row == k)[:, None], wide[k : k + 1, :], full)
    return full


def rollout(master, table, row_start, column_start):
    height, breadth = master.shape
    scale = spread((table + EPS) / FP8_MAX, row_start, height, column_start, breadth)
    return (snapped(master / scale) * scale).astype(jnp.bfloat16)


ORDER = ((0, 0), (1, 0), (0, -1), (0, 1), (1, -1), (1, 1), (0, 2), (1, 2))


def after(array, *others):
    return lax.optimization_barrier((array, *others))[0]


def ring(own, far, up, down, others, between):
    own_l, own_r = send(own, up), send(own, down)
    far = after(far, own_l, own_r, *others)
    far_l, far_r = send(far, up), send(far, down)
    others = between([own, far, own_l, own_r])
    own_l, far_r = after(own_l, far_l, *others), after(far_r, far_l, *others)
    own_ll, far_rr = send(own_l, up), send(far_r, down)
    return [own, far, own_l, own_r, far_l, far_r, own_ll, far_rr]


def token_kernel(count, first, has_before, last, info, *refs):
    pieces, refs = refs[:8], list(refs[8:])
    before = refs.pop(0) if has_before else None
    blocks, (out, wide, scratch, wide_sems, sems) = refs[:count], refs[count:]
    blocks = [blocks[n // 4 * 2 + n % 2].at[n // 2 % 2] for n in range(2 * count)]
    count = len(blocks)
    height = blocks[0].shape[0]

    def block_copy(n):
        rows = pl.ds(n * HALF, height)
        return pltpu.make_async_copy(blocks[n], scratch.at[rows, :], sems.at[n])

    def token_copy(n, piece=0):
        return pltpu.make_async_copy(pieces[piece], wide.at[n], wide_sems.at[n])

    def rows_of(m, n):
        start = pl.multiple_of(m * TILE, TILE)
        low, high = wide[n, pl.ds(start, TILE), :HALF], wide[n, pl.ds(start, TILE), HALF:]
        swapped = info[8] == 1
        return jnp.where(swapped, high, low), jnp.where(swapped, low, high)

    def finish(total):
        if has_before:
            total += before[...]
        if last:
            middle = total.shape[1] // 2
            gate = total[:, :middle]
            total = gate / (1.0 + jnp.exp(-gate)) * total[:, middle:]
        out[...] = total.astype(out.dtype)

    m = pl.program_id(0)

    @pl.when(m == 0)
    def _():
        for n in range(count // 2):
            for piece in range(len(pieces)):

                @pl.when(info[first + n] == piece)
                def _():
                    token_copy(n, piece).start()

            block_copy(2 * n).start()
            block_copy(2 * n + 1).start()
        for n in range(count):
            scratch[n * HALF + height : (n + 1) * HALF, :] = jnp.zeros(
                (HALF - height, scratch.shape[1]), scratch.dtype
            )
        total = None
        for n in range(count // 2):
            token_copy(n).wait()
            block_copy(2 * n).wait()
            block_copy(2 * n + 1).wait()
            product = jnp.dot(
                jnp.concatenate(rows_of(0, n), axis=1),
                scratch[2 * n * HALF : 2 * (n + 1) * HALF, :],
                preferred_element_type=jnp.float32,
            )
            total = product if total is None else total + product
        finish(total)

    @pl.when(m > 0)
    def _():
        rows = jnp.concatenate([part for n in range(count // 2) for part in rows_of(m, n)], axis=1)
        finish(jnp.dot(rows, scratch[...], preferred_element_type=jnp.float32))


def token_sum(info, tokens, first, blocks, before=None, last=False):
    rows, columns = tokens[0].shape[0], blocks[0].shape[2]
    count = 2 * len(blocks)
    width = columns // 2 if last else columns

    def tile(width):
        return pl.BlockSpec((TILE, width), lambda m, info: (m, 0))

    return pl.pallas_call(
        functools.partial(token_kernel, len(blocks), first, before is not None, last),
        out_shape=jax.ShapeDtypeStruct((rows, width), jnp.bfloat16 if last else jnp.float32),
        grid_spec=pltpu.PrefetchScalarGridSpec(
            num_scalar_prefetch=1,
            grid=(rows // TILE,),
            in_specs=[pl.BlockSpec(memory_space=pl.ANY)] * 8
            + ([] if before is None else [tile(columns)])
            + [pl.BlockSpec(memory_space=pl.ANY)] * len(blocks),
            out_specs=tile(width),
            scratch_shapes=[
                pltpu.VMEM((count // 2, rows, 2 * HALF), jnp.bfloat16),
                pltpu.VMEM((count * HALF, columns), jnp.bfloat16),
                pltpu.SemaphoreType.DMA((count // 2,)),
                pltpu.SemaphoreType.DMA((count,)),
            ],
        ),
        compiler_params=pltpu.CompilerParams(
            vmem_limit_bytes=VMEM_LIMIT // 3 if last else VMEM_LIMIT
        ),
        cost_estimate=FREE,
    )(info, *tokens, *([] if before is None else [before]), *blocks)


def vmem(n):
    return [pl.BlockSpec(memory_space=pltpu.VMEM)] * n


def down_kernel(info, hidden, mine, theirs, *outs):
    for n, out in enumerate(outs):
        low = jnp.where(info[8] == 0, mine[n], theirs[n])
        high = jnp.where(info[8] == 0, theirs[n], mine[n])
        out[...] = lax.dot_general(
            jnp.concatenate([low, high], axis=1),
            hidden[...],
            (((1,), (1,)), ((), ())),
            preferred_element_type=jnp.float32,
        ).astype(out.dtype)


def down_terms(info, hidden, mine, theirs):
    rows, depth = hidden.shape
    count, columns, _ = mine.shape
    return pl.pallas_call(
        down_kernel,
        out_shape=[jax.ShapeDtypeStruct((columns, rows), jnp.bfloat16)] * count,
        in_specs=[pl.BlockSpec(memory_space=pltpu.SMEM)] + vmem(3),
        out_specs=vmem(count),
        compiler_params=pltpu.CompilerParams(vmem_limit_bytes=VMEM_LIMIT // 3),
        cost_estimate=pl.CostEstimate(
            flops=4 * rows * columns * depth, bytes_accessed=12 * rows * columns, transcendentals=0
        ),
    )(info, hidden, mine, theirs)


def on_device(tokens, gate_master, up_master, down_master):
    fsdp_place = lax.axis_index("fsdp")
    tp_place = lax.axis_index("tp")
    core = fsdp_place % 2
    y_hi, x = fsdp_place // 8, (fsdp_place // 2) % 4
    y_lo, z = tp_place // 4, tp_place % 4
    gate_height, gate_breadth = gate_master.shape
    down_height, down_breadth = down_master.shape
    gate_at = (fsdp_place * gate_height, tp_place * gate_breadth)
    down_at = (fsdp_place * down_height, tp_place * down_breadth)

    half = tokens.shape[1] // 2
    padded = jnp.concatenate(
        [jnp.pad(tokens[:, k * half : (k + 1) * half], ((0, 0), (0, HALF - half))) for k in range(2)],
        axis=1,
    )
    near = send(padded, y_near)
    gate_master, up_master, down_master, padded = lax.optimization_barrier(
        (gate_master, up_master, down_master, padded)
    )

    tables = [
        block_maxima(gate_master, *gate_at, D, FF),
        block_maxima(up_master, *gate_at, D, FF),
        block_maxima(down_master, *down_at, FF, D),
    ]
    rows = D // BLOCK + 12
    columns = FF // BLOCK + 56
    pad = lambda a: jnp.pad(a, ((0, rows - a.shape[0]), (0, columns - a.shape[1])))
    table = jnp.concatenate([pad(tables[0]), pad(tables[1]), pad(tables[2].T)])

    def step(table, target):
        return jnp.maximum(table, send(table, target))

    table = step(table, other_core)
    table = step(table, lambda y, x, core, z: (y, x, core, z ^ 1))
    down_weight = rollout(down_master, table[2 * rows : 3 * rows].T, *down_at)
    own = after(padded, table)
    tokens_l, tokens_r = send(own, z_up), send(own, z_down)
    table = step(table, lambda y, x, core, z: (y, x ^ 1, core, z))
    table, down_weight = lax.optimization_barrier((table, down_weight))
    down_block = send(down_weight.T, to_ff_group)
    gate_up = jnp.concatenate(
        [
            rollout(gate_master, table[:rows], *gate_at),
            rollout(up_master, table[rows : 2 * rows], *gate_at),
        ],
        axis=1,
    )
    every = step(table, y_near)
    gate_up, every = lax.optimization_barrier((gate_up, every))
    near, tokens_l, tokens_r = lax.optimization_barrier((near, tokens_l, tokens_r))
    near, down_block = lax.optimization_barrier((near, down_block))
    near_l, near_r = send(near, z_up), send(near, z_down)
    tokens_l, near_r = after(tokens_l, near_l), after(near_r, near_l)
    tokens_ll, near_rr = send(tokens_l, z_up), send(near_r, z_down)
    pieces = [padded, near, tokens_l, tokens_r, near_l, near_r, tokens_ll, near_rr]
    pairs = []

    def swap(blocks, *before):
        blocks = [after(block, *before) for block in blocks]
        for n in range(0, len(blocks), 2):
            pair = jnp.stack(blocks[n : n + 2])
            pairs.extend((pair, send(pair, other_core)))


    down_far = None

    def between(blocks):
        nonlocal down_far
        swap(blocks[:2])
        down_far = send(after(down_block, pairs[1]), y_far)
        return [pairs[1], tokens_ll, near_rr]

    far = send(gate_up, y_far)
    blocks = ring(gate_up, far, x_up, x_down, (near_l, near_r), between)
    swap(blocks[2:4], blocks[4], blocks[5], down_far)
    swap(blocks[4:6])

    steps = jnp.array([dy + 4 * (dx % 4) for dy, dx in ORDER] + [0] * 8, jnp.int32)
    chip_y, chip_x = (steps % 4) ^ (y_hi ^ y_lo), (steps // 4 + x - z + 4) % 4
    info = jnp.where(
        chip_x == 0,
        chip_y,
        jnp.where(chip_x == 2, 6 + chip_y, 2 + 2 * chip_y + jnp.where(chip_x == 1, 1, 0)),
    )
    info = jnp.where(jnp.arange(16) == 8, core, info)

    down_pair = jnp.stack([down_block, down_far])
    down_theirs = send(down_pair, other_core)
    pairs[0] = after(pairs[0], down_theirs)
    early = token_sum(info, pieces, 0, pairs)
    early, own_ll, far_rr = lax.optimization_barrier((early, blocks[6], blocks[7]))
    every = step(after(every, early), lambda y, x, core, z: (y, x, core, z ^ 2))
    last = jnp.stack([own_ll, far_rr])
    last = [last, send(last, other_core)]
    down_block, down_far = after(down_block, own_ll), after(down_far, own_ll)
    own_l, own_r = send(down_block, x_up), send(down_block, x_down)
    far_l, far_r = send(down_far, x_up), send(down_far, x_down)
    hidden = token_sum(info, pieces, 6, last, after(early, every), last=True)

    parts = []

    def sums(mine, *before):
        mine = jnp.stack(mine) if parts else down_pair
        theirs = send(mine, other_core) if parts else down_theirs
        terms = down_terms(info, hidden, mine, theirs)
        for term in terms:
            parts.append(send(after(term, *before), to_chunk(*ORDER[len(parts)])))
        return terms

    every = step(every, y_far)
    terms = sums((), far_l, far_r, every)
    terms = sums([after(own_l, *terms), own_r])
    own_l, far_r, *_ = lax.optimization_barrier((own_l, far_r, far_l, *parts[:2], *terms))
    own_ll, far_rr = send(own_l, x_up), send(far_r, x_down)
    terms = sums([far_l, after(far_r, *terms)])
    terms = sums([own_ll, after(far_rr, *terms, *parts[2:4])])
    every = step(after(every, *terms), lambda y, x, core, z: (y, x ^ 2, core, z))
    log_amax = jnp.log(
        jnp.stack([every[k * rows : k * rows + D // BLOCK, : FF // BLOCK] for k in range(3)]) + EPS
    )
    total = sum(part.astype(jnp.float32) for part in parts)
    return total.astype(jnp.bfloat16).T, log_amax


def solution(mesh):
    return jax.shard_map(
        on_device,
        mesh=mesh,
        in_specs=(P("fsdp", "tp"), P("fsdp", "tp"), P("fsdp", "tp"), P("fsdp", "tp")),
        out_specs=(P("fsdp", "tp"), P()),
        check_vma=False,
    )
```

```python
import functools

import jax
import jax.numpy as jnp
from jax import lax
from jax.experimental import pallas as pl
from jax.experimental.pallas import tpu as pltpu
from jax.sharding import PartitionSpec as P

D = 3584
FF = 9216
BLOCK = 128

FP8_MAX = 448.0
EPS = 1e-06
SMALLEST_NORMAL = 2.0 ** (-6)
AXES = ("fsdp", "tp")
VMEM_LIMIT = 60 * 1024 * 1024
TILE = 256
HALF = 256
FREE = pl.CostEstimate(flops=0, bytes_accessed=0, transcendentals=0)


def snapped(value):
    magnitude = jnp.abs(value)
    exponent = jnp.floor(jnp.log2(jnp.maximum(magnitude, SMALLEST_NORMAL)))
    step_size = jnp.exp2(exponent - 3.0)
    return jnp.sign(value) * step_size * jnp.floor(magnitude / step_size + 0.5)


def place(y, x, core, z):
    y, x, z = y % 4, x % 4, z % 4
    return (((y // 2) * 4 + x) * 2 + core) * 8 + (y % 2) * 4 + z


def send(array, target):
    pairs = [
        (place(y, x, core, z), place(*target(y, x, core, z)))
        for y in range(4)
        for x in range(4)
        for core in range(2)
        for z in range(4)
    ]
    return lax.ppermute(array, AXES, pairs)


def x_up(y, x, core, z):
    return y, x + 1, core, z


def x_down(y, x, core, z):
    return y, x - 1, core, z


def z_up(y, x, core, z):
    return y, x, core, z + 1


def z_down(y, x, core, z):
    return y, x, core, z - 1


def y_near(y, x, core, z):
    return y ^ 1, x, core, z


def y_far(y, x, core, z):
    return y + 2, x, core, z


def other_core(y, x, core, z):
    return y, x, 1 - core, z


def to_ff_group(y, x, core, z):
    y_hi, y_lo = y // 2, y % 2
    across = y_lo ^ y_hi
    return across * 2 + y_hi, z - x - 2 * across, core, x


def to_chunk(dy, dx):
    def target(y, x, core, z):
        y_hi, y_lo = y // 2, y % 2
        across = y_hi ^ dy
        return y_hi * 2 + (y_lo ^ across), x, core, z + x + dx + 2 * across

    return target


def block_maxima(local, row_start, column_start, rows, columns):
    height, breadth = local.shape
    span_rows = (height - 1) // BLOCK + 2
    span_columns = (breadth - 1) // BLOCK + 2
    magnitude = jnp.abs(local)
    which_row = (row_start % BLOCK + jnp.arange(height, dtype=jnp.int32)) // BLOCK
    by_row = jnp.stack(
        [
            jnp.max(jnp.where((which_row == k)[:, None], magnitude, 0.0), axis=0)
            for k in range(span_rows)
        ]
    )
    which_column = (column_start % BLOCK + jnp.arange(breadth, dtype=jnp.int32)) // BLOCK
    pick = which_column[None, :] == jnp.arange(span_columns, dtype=jnp.int32)[:, None]
    part = jnp.max(jnp.where(pick[None], by_row[:, None, :], 0.0), axis=2)
    table = jnp.zeros((rows // BLOCK + span_rows, columns // BLOCK + span_columns), jnp.float32)
    return lax.dynamic_update_slice(table, part, (row_start // BLOCK, column_start // BLOCK))


def spread(scales, row_start, height, column_start, breadth):
    span_rows = (height - 1) // BLOCK + 2
    span_columns = (breadth - 1) // BLOCK + 2
    near = lax.dynamic_slice(
        scales, (row_start // BLOCK, column_start // BLOCK), (span_rows, span_columns)
    )
    which_row = (row_start % BLOCK + jnp.arange(height, dtype=jnp.int32)) // BLOCK
    which_column = (column_start % BLOCK + jnp.arange(breadth, dtype=jnp.int32)) // BLOCK
    wide = jnp.zeros((span_rows, breadth), jnp.float32)
    for k in range(span_columns):
        wide = jnp.where((which_column == k)[None, :], near[:, k : k + 1], wide)
    full = jnp.zeros((height, breadth), jnp.float32)
    for k in range(span_rows):
        full = jnp.where((which_row == k)[:, None], wide[k : k + 1, :], full)
    return full


def rollout(master, table, row_start, column_start):
    height, breadth = master.shape
    scale = spread((table + EPS) / FP8_MAX, row_start, height, column_start, breadth)
    return (snapped(master / scale) * scale).astype(jnp.bfloat16)


ORDER = ((0, 0), (1, 0), (0, -1), (0, 1), (1, -1), (1, 1), (0, 2), (1, 2))


def after(array, *others):
    return lax.optimization_barrier((array, *others))[0]


def ring(own, far, up, down, others, between):
    own_l, own_r = send(own, up), send(own, down)
    far = after(far, own_l, own_r, *others)
    far_l, far_r = send(far, up), send(far, down)
    others = between([own, far, own_l, own_r])
    own_l, far_r = after(own_l, far_l, *others), after(far_r, far_l, *others)
    own_ll, far_rr = send(own_l, up), send(far_r, down)
    return [own, far, own_l, own_r, far_l, far_r, own_ll, far_rr]


def token_kernel(count, first, has_before, last, info, *refs):
    pieces, refs = refs[:8], list(refs[8:])
    before = refs.pop(0) if has_before else None
    blocks, (out, wide, scratch, wide_sems, sems) = refs[:count], refs[count:]
    blocks = [blocks[n // 4 * 2 + n % 2].at[n // 2 % 2] for n in range(2 * count)]
    count = len(blocks)
    height = blocks[0].shape[0]

    def block_copy(n):
        rows = pl.ds(n * HALF, height)
        return pltpu.make_async_copy(blocks[n], scratch.at[rows, :], sems.at[n])

    def token_copy(n, piece=0):
        return pltpu.make_async_copy(pieces[piece], wide.at[n], wide_sems.at[n])

    def rows_of(m, n):
        start = pl.multiple_of(m * TILE, TILE)
        low, high = wide[n, pl.ds(start, TILE), :HALF], wide[n, pl.ds(start, TILE), HALF:]
        swapped = info[8] == 1
        return jnp.where(swapped, high, low), jnp.where(swapped, low, high)

    def finish(total):
        if has_before:
            total += before[...]
        if last:
            middle = total.shape[1] // 2
            gate = total[:, :middle]
            total = gate / (1.0 + jnp.exp(-gate)) * total[:, middle:]
        out[...] = total.astype(out.dtype)

    m = pl.program_id(0)

    @pl.when(m == 0)
    def _():
        for n in range(count // 2):
            for piece in range(len(pieces)):

                @pl.when(info[first + n] == piece)
                def _():
                    token_copy(n, piece).start()

            block_copy(2 * n).start()
            block_copy(2 * n + 1).start()
        for n in range(count):
            scratch[n * HALF + height : (n + 1) * HALF, :] = jnp.zeros(
                (HALF - height, scratch.shape[1]), scratch.dtype
            )
        for n in range(count // 2):
            token_copy(n).wait()
            block_copy(2 * n).wait()
            block_copy(2 * n + 1).wait()

    rows = jnp.concatenate([part for n in range(count // 2) for part in rows_of(m, n)], axis=1)
    finish(jnp.dot(rows, scratch[...], preferred_element_type=jnp.float32))


def token_sum(info, tokens, first, blocks, before=None, last=False):
    rows, columns = tokens[0].shape[0], blocks[0].shape[2]
    count = 2 * len(blocks)
    width = columns // 2 if last else columns

    def tile(width):
        return pl.BlockSpec((TILE, width), lambda m, info: (m, 0))

    return pl.pallas_call(
        functools.partial(token_kernel, len(blocks), first, before is not None, last),
        out_shape=jax.ShapeDtypeStruct((rows, width), jnp.bfloat16 if last else jnp.float32),
        grid_spec=pltpu.PrefetchScalarGridSpec(
            num_scalar_prefetch=1,
            grid=(rows // TILE,),
            in_specs=[pl.BlockSpec(memory_space=pl.ANY)] * 8
            + ([] if before is None else [tile(columns)])
            + [pl.BlockSpec(memory_space=pl.ANY)] * len(blocks),
            out_specs=tile(width),
            scratch_shapes=[
                pltpu.VMEM((count // 2, rows, 2 * HALF), jnp.bfloat16),
                pltpu.VMEM((count * HALF, columns), jnp.bfloat16),
                pltpu.SemaphoreType.DMA((count // 2,)),
                pltpu.SemaphoreType.DMA((count,)),
            ],
        ),
        compiler_params=pltpu.CompilerParams(
            vmem_limit_bytes=VMEM_LIMIT // 3 if last else VMEM_LIMIT
        ),
        cost_estimate=FREE,
    )(info, *tokens, *([] if before is None else [before]), *blocks)


def vmem(n):
    return [pl.BlockSpec(memory_space=pltpu.VMEM)] * n


def down_kernel(info, hidden, mine, theirs, *outs):
    for n, out in enumerate(outs):
        low = jnp.where(info[8] == 0, mine[n], theirs[n])
        high = jnp.where(info[8] == 0, theirs[n], mine[n])
        out[...] = lax.dot_general(
            jnp.concatenate([low, high], axis=1),
            hidden[...],
            (((1,), (1,)), ((), ())),
            preferred_element_type=jnp.float32,
        ).astype(out.dtype)


def down_terms(info, hidden, mine, theirs):
    rows, depth = hidden.shape
    count, columns, _ = mine.shape
    return pl.pallas_call(
        down_kernel,
        out_shape=[jax.ShapeDtypeStruct((columns, rows), jnp.bfloat16)] * count,
        in_specs=[pl.BlockSpec(memory_space=pltpu.SMEM)] + vmem(3),
        out_specs=vmem(count),
        compiler_params=pltpu.CompilerParams(vmem_limit_bytes=VMEM_LIMIT // 3),
        cost_estimate=pl.CostEstimate(
            flops=4 * rows * columns * depth, bytes_accessed=12 * rows * columns, transcendentals=0
        ),
    )(info, hidden, mine, theirs)


def on_device(tokens, gate_master, up_master, down_master):
    fsdp_place = lax.axis_index("fsdp")
    tp_place = lax.axis_index("tp")
    core = fsdp_place % 2
    y_hi, x = fsdp_place // 8, (fsdp_place // 2) % 4
    y_lo, z = tp_place // 4, tp_place % 4
    gate_height, gate_breadth = gate_master.shape
    down_height, down_breadth = down_master.shape
    gate_at = (fsdp_place * gate_height, tp_place * gate_breadth)
    down_at = (fsdp_place * down_height, tp_place * down_breadth)

    half = tokens.shape[1] // 2
    padded = jnp.concatenate(
        [jnp.pad(tokens[:, k * half : (k + 1) * half], ((0, 0), (0, HALF - half))) for k in range(2)],
        axis=1,
    )
    near = send(padded, y_near)
    tokens_l, tokens_r = send(padded, z_up), send(padded, z_down)
    gate_master, up_master, down_master, padded = lax.optimization_barrier(
        (gate_master, up_master, down_master, padded)
    )

    tables = [
        block_maxima(gate_master, *gate_at, D, FF),
        block_maxima(up_master, *gate_at, D, FF),
        block_maxima(down_master, *down_at, FF, D),
    ]
    rows = D // BLOCK + 12
    columns = FF // BLOCK + 56
    pad = lambda a: jnp.pad(a, ((0, rows - a.shape[0]), (0, columns - a.shape[1])))
    table = jnp.concatenate([pad(tables[0]), pad(tables[1]), pad(tables[2].T)])

    def step(table, target):
        return jnp.maximum(table, send(table, target))

    table = step(table, other_core)
    table = step(table, lambda y, x, core, z: (y, x ^ 1, core, z))
    gate_up = jnp.concatenate(
        [
            rollout(gate_master, table[:rows], *gate_at),
            rollout(up_master, table[rows : 2 * rows], *gate_at),
        ],
        axis=1,
    )
    every = step(table, lambda y, x, core, z: (y, x, core, z ^ 1))
    down_weight = rollout(down_master, every[2 * rows : 3 * rows].T, *down_at)
    down_block = send(down_weight.T, to_ff_group)
    every = step(every, y_near)
    gate_up, every, down_block = lax.optimization_barrier((gate_up, every, down_block))
    near, tokens_l, tokens_r = lax.optimization_barrier((near, tokens_l, tokens_r))
    near_l, near_r = send(near, z_up), send(near, z_down)
    tokens_l, near_r = after(tokens_l, near_l), after(near_r, near_l)
    tokens_ll, near_rr = send(tokens_l, z_up), send(near_r, z_down)
    pieces = [padded, near, tokens_l, tokens_r, near_l, near_r, tokens_ll, near_rr]
    pairs = []

    def swap(blocks, *before):
        blocks = [after(block, *before) for block in blocks]
        for n in range(0, len(blocks), 2):
            pair = jnp.stack(blocks[n : n + 2])
            pairs.extend((pair, send(pair, other_core)))


    down_far = None

    def between(blocks):
        nonlocal down_far
        swap(blocks[:2])
        down_far = send(after(down_block, pairs[1]), y_far)
        return [pairs[1], tokens_ll, near_rr]

    far = send(gate_up, y_far)
    blocks = ring(gate_up, far, x_up, x_down, (near_l, near_r), between)
    swap(blocks[2:4], blocks[4], blocks[5], down_far)
    swap(blocks[4:6])

    steps = jnp.array([dy + 4 * (dx % 4) for dy, dx in ORDER] + [0] * 8, jnp.int32)
    chip_y, chip_x = (steps % 4) ^ (y_hi ^ y_lo), (steps // 4 + x - z + 4) % 4
    info = jnp.where(
        chip_x == 0,
        chip_y,
        jnp.where(chip_x == 2, 6 + chip_y, 2 + 2 * chip_y + jnp.where(chip_x == 1, 1, 0)),
    )
    info = jnp.where(jnp.arange(16) == 8, core, info)

    down_pair = jnp.stack([down_block, down_far])
    down_theirs = send(down_pair, other_core)
    pairs[0] = after(pairs[0], down_theirs)
    early = token_sum(info, pieces, 0, pairs)
    early, own_ll, far_rr = lax.optimization_barrier((early, blocks[6], blocks[7]))
    every = step(after(every, early), lambda y, x, core, z: (y, x, core, z ^ 2))
    last = jnp.stack([own_ll, far_rr])
    last = [last, send(last, other_core)]
    down_block, down_far = after(down_block, own_ll), after(down_far, own_ll)
    own_l, own_r = send(down_block, x_up), send(down_block, x_down)
    far_l, far_r = send(down_far, x_up), send(down_far, x_down)
    hidden = token_sum(info, pieces, 6, last, after(early, every), last=True)

    parts = []

    def sums(mine, *before):
        mine = jnp.stack(mine) if parts else down_pair
        theirs = send(mine, other_core) if parts else down_theirs
        terms = down_terms(info, hidden, mine, theirs)
        for term in terms:
            parts.append(send(after(term, *before), to_chunk(*ORDER[len(parts)])))
        return terms

    every = step(every, y_far)
    terms = sums((), far_l, far_r, every)
    terms = sums([after(own_l, *terms), own_r])
    own_l, far_r, *_ = lax.optimization_barrier((own_l, far_r, far_l, *parts[:2], *terms))
    own_ll, far_rr = send(own_l, x_up), send(far_r, x_down)
    terms = sums([far_l, after(far_r, *terms)])
    terms = sums([own_ll, after(far_rr, *terms, *parts[2:4])])
    every = step(after(every, *terms), lambda y, x, core, z: (y, x ^ 2, core, z))
    log_amax = jnp.log(
        jnp.stack([every[k * rows : k * rows + D // BLOCK, : FF // BLOCK] for k in range(3)]) + EPS
    )
    total = sum(part.astype(jnp.float32) for part in parts)
    return total.astype(jnp.bfloat16).T, log_amax


def solution(mesh):
    return jax.shard_map(
        on_device,
        mesh=mesh,
        in_specs=(P("fsdp", "tp"), P("fsdp", "tp"), P("fsdp", "tp"), P("fsdp", "tp")),
        out_specs=(P("fsdp", "tp"), P()),
        check_vma=False,
    )
```

```python
import functools

import jax
import jax.numpy as jnp
from jax import lax
from jax.experimental import pallas as pl
from jax.experimental.pallas import tpu as pltpu
from jax.sharding import PartitionSpec as P

D = 3584
FF = 9216
BLOCK = 128

FP8_MAX = 448.0
EPS = 1e-06
SMALLEST_NORMAL = 2.0 ** (-6)
AXES = ("fsdp", "tp")
VMEM_LIMIT = 60 * 1024 * 1024
TILE = 256
HALF = 256
FREE = pl.CostEstimate(flops=0, bytes_accessed=0, transcendentals=0)


def snapped(value):
    magnitude = jnp.abs(value)
    exponent = jnp.floor(jnp.log2(jnp.maximum(magnitude, SMALLEST_NORMAL)))
    step_size = jnp.exp2(exponent - 3.0)
    return jnp.sign(value) * step_size * jnp.floor(magnitude / step_size + 0.5)


def place(y, x, core, z):
    y, x, z = y % 4, x % 4, z % 4
    return (((y // 2) * 4 + x) * 2 + core) * 8 + (y % 2) * 4 + z


def send(array, target):
    pairs = [
        (place(y, x, core, z), place(*target(y, x, core, z)))
        for y in range(4)
        for x in range(4)
        for core in range(2)
        for z in range(4)
    ]
    return lax.ppermute(array, AXES, pairs)


def x_up(y, x, core, z):
    return y, x + 1, core, z


def x_down(y, x, core, z):
    return y, x - 1, core, z


def z_up(y, x, core, z):
    return y, x, core, z + 1


def z_down(y, x, core, z):
    return y, x, core, z - 1


def y_near(y, x, core, z):
    return y ^ 1, x, core, z


def y_far(y, x, core, z):
    return y + 2, x, core, z


def other_core(y, x, core, z):
    return y, x, 1 - core, z


def to_ff_group(y, x, core, z):
    y_hi, y_lo = y // 2, y % 2
    across = y_lo ^ y_hi
    return across * 2 + y_hi, z - x - 2 * across, core, x


def to_chunk(dy, dx):
    def target(y, x, core, z):
        y_hi, y_lo = y // 2, y % 2
        across = y_hi ^ dy
        return y_hi * 2 + (y_lo ^ across), x, core, z + x + dx + 2 * across

    return target


def block_maxima(local, row_start, column_start, rows, columns):
    height, breadth = local.shape
    span_rows = (height - 1) // BLOCK + 2
    span_columns = (breadth - 1) // BLOCK + 2
    magnitude = jnp.abs(local)
    which_row = (row_start % BLOCK + jnp.arange(height, dtype=jnp.int32)) // BLOCK
    by_row = jnp.stack(
        [
            jnp.max(jnp.where((which_row == k)[:, None], magnitude, 0.0), axis=0)
            for k in range(span_rows)
        ]
    )
    which_column = (column_start % BLOCK + jnp.arange(breadth, dtype=jnp.int32)) // BLOCK
    pick = which_column[None, :] == jnp.arange(span_columns, dtype=jnp.int32)[:, None]
    part = jnp.max(jnp.where(pick[None], by_row[:, None, :], 0.0), axis=2)
    table = jnp.zeros((rows // BLOCK + span_rows, columns // BLOCK + span_columns), jnp.float32)
    return lax.dynamic_update_slice(table, part, (row_start // BLOCK, column_start // BLOCK))


def spread(scales, row_start, height, column_start, breadth):
    span_rows = (height - 1) // BLOCK + 2
    span_columns = (breadth - 1) // BLOCK + 2
    near = lax.dynamic_slice(
        scales, (row_start // BLOCK, column_start // BLOCK), (span_rows, span_columns)
    )
    which_row = (row_start % BLOCK + jnp.arange(height, dtype=jnp.int32)) // BLOCK
    which_column = (column_start % BLOCK + jnp.arange(breadth, dtype=jnp.int32)) // BLOCK
    wide = jnp.zeros((span_rows, breadth), jnp.float32)
    for k in range(span_columns):
        wide = jnp.where((which_column == k)[None, :], near[:, k : k + 1], wide)
    full = jnp.zeros((height, breadth), jnp.float32)
    for k in range(span_rows):
        full = jnp.where((which_row == k)[:, None], wide[k : k + 1, :], full)
    return full


def rollout(master, table, row_start, column_start):
    height, breadth = master.shape
    scale = spread((table + EPS) / FP8_MAX, row_start, height, column_start, breadth)
    return (snapped(master / scale) * scale).astype(jnp.bfloat16)


ORDER = ((0, 0), (1, 0), (0, -1), (0, 1), (1, -1), (1, 1), (0, 2), (1, 2))


def after(array, *others):
    return lax.optimization_barrier((array, *others))[0]


def ring(own, far, up, down, others, between):
    own_l, own_r = send(own, up), send(own, down)
    far = after(far, own_l, own_r, *others)
    far_l, far_r = send(far, up), send(far, down)
    others = between([own, far, own_l, own_r])
    own_l, far_r = after(own_l, far_l, *others), after(far_r, far_l, *others)
    own_ll, far_rr = send(own_l, up), send(far_r, down)
    return [own, far, own_l, own_r, far_l, far_r, own_ll, far_rr]


def token_kernel(count, first, has_before, last, info, *refs):
    pieces, refs = refs[:8], list(refs[8:])
    before = refs.pop(0) if has_before else None
    blocks, (out, wide, scratch, wide_sems, sems) = refs[:count], refs[count:]
    blocks = [blocks[n // 4 * 2 + n % 2].at[n // 2 % 2] for n in range(2 * count)]
    count = len(blocks)
    height = blocks[0].shape[0]

    def block_copy(n):
        rows = pl.ds(n * HALF, height)
        return pltpu.make_async_copy(blocks[n], scratch.at[rows, :], sems.at[n])

    def token_copy(n, piece=0):
        return pltpu.make_async_copy(pieces[piece], wide.at[n], wide_sems.at[n])

    def rows_of(m, n):
        start = pl.multiple_of(m * TILE, TILE)
        low, high = wide[n, pl.ds(start, TILE), :HALF], wide[n, pl.ds(start, TILE), HALF:]
        swapped = info[8] == 1
        return jnp.where(swapped, high, low), jnp.where(swapped, low, high)

    def finish(total):
        if has_before:
            total += before[...]
        if last:
            middle = total.shape[1] // 2
            gate = total[:, :middle]
            total = gate / (1.0 + jnp.exp(-gate)) * total[:, middle:]
        out[...] = total.astype(out.dtype)

    m = pl.program_id(0)

    @pl.when(m == 0)
    def _():
        for n in range(count // 2):
            for piece in range(len(pieces)):

                @pl.when(info[first + n] == piece)
                def _():
                    token_copy(n, piece).start()

            block_copy(2 * n).start()
            block_copy(2 * n + 1).start()
        for n in range(count):
            scratch[n * HALF + height : (n + 1) * HALF, :] = jnp.zeros(
                (HALF - height, scratch.shape[1]), scratch.dtype
            )
        for n in range(count // 2):
            token_copy(n).wait()
            block_copy(2 * n).wait()
            block_copy(2 * n + 1).wait()

    rows = jnp.concatenate([part for n in range(count // 2) for part in rows_of(m, n)], axis=1)
    finish(jnp.dot(rows, scratch[...], preferred_element_type=jnp.float32))


def token_sum(info, tokens, first, blocks, before=None, last=False):
    rows, columns = tokens[0].shape[0], blocks[0].shape[2]
    count = 2 * len(blocks)
    width = columns // 2 if last else columns

    def tile(width):
        return pl.BlockSpec((TILE, width), lambda m, info: (m, 0))

    return pl.pallas_call(
        functools.partial(token_kernel, len(blocks), first, before is not None, last),
        out_shape=jax.ShapeDtypeStruct((rows, width), jnp.bfloat16 if last else jnp.float32),
        grid_spec=pltpu.PrefetchScalarGridSpec(
            num_scalar_prefetch=1,
            grid=(rows // TILE,),
            in_specs=[pl.BlockSpec(memory_space=pl.ANY)] * 8
            + ([] if before is None else [tile(columns)])
            + [pl.BlockSpec(memory_space=pl.ANY)] * len(blocks),
            out_specs=tile(width),
            scratch_shapes=[
                pltpu.VMEM((count // 2, rows, 2 * HALF), jnp.bfloat16),
                pltpu.VMEM((count * HALF, columns), jnp.bfloat16),
                pltpu.SemaphoreType.DMA((count // 2,)),
                pltpu.SemaphoreType.DMA((count,)),
            ],
        ),
        compiler_params=pltpu.CompilerParams(
            vmem_limit_bytes=VMEM_LIMIT // 3 if last else VMEM_LIMIT
        ),
        cost_estimate=FREE,
    )(info, *tokens, *([] if before is None else [before]), *blocks)


def vmem(n):
    return [pl.BlockSpec(memory_space=pltpu.VMEM)] * n


def down_kernel(info, hidden, mine, theirs, *outs):
    for n, out in enumerate(outs):
        low = jnp.where(info[8] == 0, mine[n], theirs[n])
        high = jnp.where(info[8] == 0, theirs[n], mine[n])
        out[...] = lax.dot_general(
            jnp.concatenate([low, high], axis=1),
            hidden[...],
            (((1,), (1,)), ((), ())),
            preferred_element_type=jnp.float32,
        ).astype(out.dtype)


def down_terms(info, hidden, mine, theirs):
    rows, depth = hidden.shape
    count, columns, _ = mine.shape
    return pl.pallas_call(
        down_kernel,
        out_shape=[jax.ShapeDtypeStruct((columns, rows), jnp.bfloat16)] * count,
        in_specs=[pl.BlockSpec(memory_space=pltpu.SMEM)] + vmem(3),
        out_specs=vmem(count),
        compiler_params=pltpu.CompilerParams(vmem_limit_bytes=VMEM_LIMIT // 3),
        cost_estimate=pl.CostEstimate(
            flops=4 * rows * columns * depth, bytes_accessed=12 * rows * columns, transcendentals=0
        ),
    )(info, hidden, mine, theirs)


def on_device(tokens, gate_master, up_master, down_master):
    fsdp_place = lax.axis_index("fsdp")
    tp_place = lax.axis_index("tp")
    core = fsdp_place % 2
    y_hi, x = fsdp_place // 8, (fsdp_place // 2) % 4
    y_lo, z = tp_place // 4, tp_place % 4
    gate_height, gate_breadth = gate_master.shape
    down_height, down_breadth = down_master.shape
    gate_at = (fsdp_place * gate_height, tp_place * gate_breadth)
    down_at = (fsdp_place * down_height, tp_place * down_breadth)

    half = tokens.shape[1] // 2
    padded = jnp.concatenate(
        [jnp.pad(tokens[:, k * half : (k + 1) * half], ((0, 0), (0, HALF - half))) for k in range(2)],
        axis=1,
    )
    near = send(padded, y_near)
    tokens_l, tokens_r = send(padded, z_up), send(padded, z_down)
    gate_master, up_master, down_master, padded = lax.optimization_barrier(
        (gate_master, up_master, down_master, padded)
    )

    tables = [
        block_maxima(gate_master, *gate_at, D, FF),
        block_maxima(up_master, *gate_at, D, FF),
        block_maxima(down_master, *down_at, FF, D),
    ]
    rows = D // BLOCK + 12
    columns = FF // BLOCK + 56
    pad = lambda a: jnp.pad(a, ((0, rows - a.shape[0]), (0, columns - a.shape[1])))
    table = jnp.concatenate([pad(tables[0]), pad(tables[1]), pad(tables[2].T)])

    def step(table, target):
        return jnp.maximum(table, send(table, target))

    table = step(table, other_core)
    table = step(table, lambda y, x, core, z: (y, x ^ 1, core, z))
    gate_up = jnp.concatenate(
        [
            rollout(gate_master, table[:rows], *gate_at),
            rollout(up_master, table[rows : 2 * rows], *gate_at),
        ],
        axis=1,
    )
    every = step(table, lambda y, x, core, z: (y, x, core, z ^ 1))
    gate_up, every = lax.optimization_barrier((gate_up, every))
    near, tokens_l, tokens_r = lax.optimization_barrier((near, tokens_l, tokens_r))
    down_table = every
    near_l, near_r = send(near, z_up), send(near, z_down)
    tokens_l, near_r = after(tokens_l, near_l), after(near_r, near_l)
    tokens_ll, near_rr = send(tokens_l, z_up), send(near_r, z_down)
    pieces = [padded, near, tokens_l, tokens_r, near_l, near_r, tokens_ll, near_rr]
    down_weight = rollout(down_master, down_table[2 * rows : 3 * rows].T, *down_at)
    pairs = []

    def swap(blocks, *before):
        blocks = [after(block, *before) for block in blocks]
        for n in range(0, len(blocks), 2):
            pair = jnp.stack(blocks[n : n + 2])
            pairs.extend((pair, send(pair, other_core)))

    down_block = send(after(down_weight.T, near_l, near_r), to_ff_group)
    every = step(after(every, near_l, near_r), y_near)

    down_far = None

    def between(blocks):
        nonlocal down_far
        swap(blocks[:2])
        down_far = send(after(down_block, pairs[1]), y_far)
        return [pairs[1], tokens_ll, near_rr]

    far = send(gate_up, y_far)
    blocks = ring(gate_up, far, x_up, x_down, (near_l, near_r), between)
    swap(blocks[2:4], blocks[4], blocks[5], down_far, every)
    swap(blocks[4:6])

    steps = jnp.array([dy + 4 * (dx % 4) for dy, dx in ORDER] + [0] * 8, jnp.int32)
    chip_y, chip_x = (steps % 4) ^ (y_hi ^ y_lo), (steps // 4 + x - z + 4) % 4
    info = jnp.where(
        chip_x == 0,
        chip_y,
        jnp.where(chip_x == 2, 6 + chip_y, 2 + 2 * chip_y + jnp.where(chip_x == 1, 1, 0)),
    )
    info = jnp.where(jnp.arange(16) == 8, core, info)

    down_pair = jnp.stack([down_block, down_far])
    down_theirs = send(down_pair, other_core)
    pairs[0] = after(pairs[0], down_theirs)
    early = token_sum(info, pieces, 0, pairs)
    early, own_ll, far_rr = lax.optimization_barrier((early, blocks[6], blocks[7]))
    every = step(after(every, early), lambda y, x, core, z: (y, x, core, z ^ 2))
    last = jnp.stack([own_ll, far_rr])
    last = [last, send(last, other_core)]
    down_block, down_far = after(down_block, own_ll), after(down_far, own_ll)
    own_l, own_r = send(down_block, x_up), send(down_block, x_down)
    far_l, far_r = send(down_far, x_up), send(down_far, x_down)
    hidden = token_sum(info, pieces, 6, last, after(early, every), last=True)

    parts = []

    def sums(mine, *before):
        mine = jnp.stack(mine) if parts else down_pair
        theirs = send(mine, other_core) if parts else down_theirs
        terms = down_terms(info, hidden, mine, theirs)
        for term in terms:
            parts.append(send(after(term, *before), to_chunk(*ORDER[len(parts)])))
        return terms

    every = step(every, y_far)
    terms = sums((), far_l, far_r, every)
    terms = sums([after(own_l, *terms), own_r])
    own_l, far_r, *_ = lax.optimization_barrier((own_l, far_r, far_l, *parts[:2], *terms))
    own_ll, far_rr = send(own_l, x_up), send(far_r, x_down)
    terms = sums([far_l, after(far_r, *terms)])
    terms = sums([own_ll, after(far_rr, *terms, *parts[2:4])])
    every = step(after(every, *terms), lambda y, x, core, z: (y, x ^ 2, core, z))
    log_amax = jnp.log(
        jnp.stack([every[k * rows : k * rows + D // BLOCK, : FF // BLOCK] for k in range(3)]) + EPS
    )
    total = sum(part.astype(jnp.float32) for part in parts)
    return total.astype(jnp.bfloat16).T, log_amax


def solution(mesh):
    return jax.shard_map(
        on_device,
        mesh=mesh,
        in_specs=(P("fsdp", "tp"), P("fsdp", "tp"), P("fsdp", "tp"), P("fsdp", "tp")),
        out_specs=(P("fsdp", "tp"), P()),
        check_vma=False,
    )
```

```python
import functools

import jax
import jax.numpy as jnp
from jax import lax
from jax.experimental import pallas as pl
from jax.experimental.pallas import tpu as pltpu
from jax.sharding import PartitionSpec as P

D = 3584
FF = 9216
BLOCK = 128

FP8_MAX = 448.0
EPS = 1e-06
SMALLEST_NORMAL = 2.0 ** (-6)
AXES = ("fsdp", "tp")
VMEM_LIMIT = 60 * 1024 * 1024
TILE = 256
HALF = 256
FREE = pl.CostEstimate(flops=0, bytes_accessed=0, transcendentals=0)


def snapped(value):
    magnitude = jnp.abs(value)
    exponent = jnp.floor(jnp.log2(jnp.maximum(magnitude, SMALLEST_NORMAL)))
    step_size = jnp.exp2(exponent - 3.0)
    return jnp.sign(value) * step_size * jnp.floor(magnitude / step_size + 0.5)


def place(y, x, core, z):
    y, x, z = y % 4, x % 4, z % 4
    return (((y // 2) * 4 + x) * 2 + core) * 8 + (y % 2) * 4 + z


def send(array, target):
    pairs = [
        (place(y, x, core, z), place(*target(y, x, core, z)))
        for y in range(4)
        for x in range(4)
        for core in range(2)
        for z in range(4)
    ]
    return lax.ppermute(array, AXES, pairs)


def x_up(y, x, core, z):
    return y, x + 1, core, z


def x_down(y, x, core, z):
    return y, x - 1, core, z


def z_up(y, x, core, z):
    return y, x, core, z + 1


def z_down(y, x, core, z):
    return y, x, core, z - 1


def y_near(y, x, core, z):
    return y ^ 1, x, core, z


def y_far(y, x, core, z):
    return y + 2, x, core, z


def other_core(y, x, core, z):
    return y, x, 1 - core, z


def to_ff_group(y, x, core, z):
    y_hi, y_lo = y // 2, y % 2
    across = y_lo ^ y_hi
    return across * 2 + y_hi, z - x - 2 * across, core, x


def to_chunk(dy, dx):
    def target(y, x, core, z):
        y_hi, y_lo = y // 2, y % 2
        across = y_hi ^ dy
        return y_hi * 2 + (y_lo ^ across), x, core, z + x + dx + 2 * across

    return target


def block_maxima(local, row_start, column_start, rows, columns):
    height, breadth = local.shape
    span_rows = (height - 1) // BLOCK + 2
    span_columns = (breadth - 1) // BLOCK + 2
    magnitude = jnp.abs(local)
    which_row = (row_start % BLOCK + jnp.arange(height, dtype=jnp.int32)) // BLOCK
    by_row = jnp.stack(
        [
            jnp.max(jnp.where((which_row == k)[:, None], magnitude, 0.0), axis=0)
            for k in range(span_rows)
        ]
    )
    which_column = (column_start % BLOCK + jnp.arange(breadth, dtype=jnp.int32)) // BLOCK
    pick = which_column[None, :] == jnp.arange(span_columns, dtype=jnp.int32)[:, None]
    part = jnp.max(jnp.where(pick[None], by_row[:, None, :], 0.0), axis=2)
    table = jnp.zeros((rows // BLOCK + span_rows, columns // BLOCK + span_columns), jnp.float32)
    return lax.dynamic_update_slice(table, part, (row_start // BLOCK, column_start // BLOCK))


def spread(scales, row_start, height, column_start, breadth):
    span_rows = (height - 1) // BLOCK + 2
    span_columns = (breadth - 1) // BLOCK + 2
    near = lax.dynamic_slice(
        scales, (row_start // BLOCK, column_start // BLOCK), (span_rows, span_columns)
    )
    which_row = (row_start % BLOCK + jnp.arange(height, dtype=jnp.int32)) // BLOCK
    which_column = (column_start % BLOCK + jnp.arange(breadth, dtype=jnp.int32)) // BLOCK
    wide = jnp.zeros((span_rows, breadth), jnp.float32)
    for k in range(span_columns):
        wide = jnp.where((which_column == k)[None, :], near[:, k : k + 1], wide)
    full = jnp.zeros((height, breadth), jnp.float32)
    for k in range(span_rows):
        full = jnp.where((which_row == k)[:, None], wide[k : k + 1, :], full)
    return full


def rollout(master, table, row_start, column_start):
    height, breadth = master.shape
    scale = spread((table + EPS) / FP8_MAX, row_start, height, column_start, breadth)
    return (snapped(master / scale) * scale).astype(jnp.bfloat16)


ORDER = ((0, 0), (1, 0), (0, -1), (0, 1), (1, -1), (1, 1), (0, 2), (1, 2))


def after(array, *others):
    return lax.optimization_barrier((array, *others))[0]


def ring(own, far, up, down, others, between):
    own_l, own_r = send(own, up), send(own, down)
    far = after(far, own_l, own_r, *others)
    far_l, far_r = send(far, up), send(far, down)
    others = between([own, far, own_l, own_r])
    own_l, far_r = after(own_l, far_l, *others), after(far_r, far_l, *others)
    own_ll, far_rr = send(own_l, up), send(far_r, down)
    return [own, far, own_l, own_r, far_l, far_r, own_ll, far_rr]


def token_kernel(count, first, has_before, last, info, *refs):
    pieces, refs = refs[:8], list(refs[8:])
    before = refs.pop(0) if has_before else None
    blocks, (out, wide, scratch, wide_sems, sems) = refs[:count], refs[count:]
    blocks = [blocks[n // 4 * 2 + n % 2].at[n // 2 % 2] for n in range(2 * count)]
    count = len(blocks)
    height = blocks[0].shape[0]

    def block_copy(n):
        rows = pl.ds(n * HALF, height)
        return pltpu.make_async_copy(blocks[n], scratch.at[rows, :], sems.at[n])

    def token_copy(n, piece=0):
        return pltpu.make_async_copy(pieces[piece], wide.at[n], wide_sems.at[n])

    def rows_of(m, n):
        start = pl.multiple_of(m * TILE, TILE)
        low, high = wide[n, pl.ds(start, TILE), :HALF], wide[n, pl.ds(start, TILE), HALF:]
        swapped = info[8] == 1
        return jnp.where(swapped, high, low), jnp.where(swapped, low, high)

    def finish(total):
        if has_before:
            total += before[...]
        if last:
            middle = total.shape[1] // 2
            gate = total[:, :middle]
            total = gate / (1.0 + jnp.exp(-gate)) * total[:, middle:]
        out[...] = total.astype(out.dtype)

    m = pl.program_id(0)

    @pl.when(m == 0)
    def _():
        for n in range(count // 2):
            for piece in range(len(pieces)):

                @pl.when(info[first + n] == piece)
                def _():
                    token_copy(n, piece).start()

            block_copy(2 * n).start()
            block_copy(2 * n + 1).start()
        for n in range(count):
            scratch[n * HALF + height : (n + 1) * HALF, :] = jnp.zeros(
                (HALF - height, scratch.shape[1]), scratch.dtype
            )
        for n in range(count // 2):
            token_copy(n).wait()
            block_copy(2 * n).wait()
            block_copy(2 * n + 1).wait()

    rows = jnp.concatenate([part for n in range(count // 2) for part in rows_of(m, n)], axis=1)
    finish(jnp.dot(rows, scratch[...], preferred_element_type=jnp.float32))


def token_sum(info, tokens, first, blocks, before=None, last=False):
    rows, columns = tokens[0].shape[0], blocks[0].shape[2]
    count = 2 * len(blocks)
    width = columns // 2 if last else columns

    def tile(width):
        return pl.BlockSpec((TILE, width), lambda m, info: (m, 0))

    return pl.pallas_call(
        functools.partial(token_kernel, len(blocks), first, before is not None, last),
        out_shape=jax.ShapeDtypeStruct((rows, width), jnp.bfloat16 if last else jnp.float32),
        grid_spec=pltpu.PrefetchScalarGridSpec(
            num_scalar_prefetch=1,
            grid=(rows // TILE,),
            in_specs=[pl.BlockSpec(memory_space=pl.ANY)] * 8
            + ([] if before is None else [tile(columns)])
            + [pl.BlockSpec(memory_space=pl.ANY)] * len(blocks),
            out_specs=tile(width),
            scratch_shapes=[
                pltpu.VMEM((count // 2, rows, 2 * HALF), jnp.bfloat16),
                pltpu.VMEM((count * HALF, columns), jnp.bfloat16),
                pltpu.SemaphoreType.DMA((count // 2,)),
                pltpu.SemaphoreType.DMA((count,)),
            ],
        ),
        compiler_params=pltpu.CompilerParams(
            vmem_limit_bytes=VMEM_LIMIT // 3 if last else VMEM_LIMIT
        ),
        cost_estimate=FREE,
    )(info, *tokens, *([] if before is None else [before]), *blocks)


def vmem(n):
    return [pl.BlockSpec(memory_space=pltpu.VMEM)] * n


def down_kernel(info, hidden, mine, theirs, *outs):
    for n, out in enumerate(outs):
        low = jnp.where(info[8] == 0, mine[n], theirs[n])
        high = jnp.where(info[8] == 0, theirs[n], mine[n])
        out[...] = lax.dot_general(
            jnp.concatenate([low, high], axis=1),
            hidden[...],
            (((1,), (1,)), ((), ())),
            preferred_element_type=jnp.float32,
        ).astype(out.dtype)


def down_terms(info, hidden, mine, theirs):
    rows, depth = hidden.shape
    count, columns, _ = mine.shape
    return pl.pallas_call(
        down_kernel,
        out_shape=[jax.ShapeDtypeStruct((columns, rows), jnp.bfloat16)] * count,
        in_specs=[pl.BlockSpec(memory_space=pltpu.SMEM)] + vmem(3),
        out_specs=vmem(count),
        compiler_params=pltpu.CompilerParams(vmem_limit_bytes=VMEM_LIMIT // 3),
        cost_estimate=pl.CostEstimate(
            flops=4 * rows * columns * depth, bytes_accessed=12 * rows * columns, transcendentals=0
        ),
    )(info, hidden, mine, theirs)


def on_device(tokens, gate_master, up_master, down_master):
    fsdp_place = lax.axis_index("fsdp")
    tp_place = lax.axis_index("tp")
    core = fsdp_place % 2
    y_hi, x = fsdp_place // 8, (fsdp_place // 2) % 4
    y_lo, z = tp_place // 4, tp_place % 4
    gate_height, gate_breadth = gate_master.shape
    down_height, down_breadth = down_master.shape
    gate_at = (fsdp_place * gate_height, tp_place * gate_breadth)
    down_at = (fsdp_place * down_height, tp_place * down_breadth)

    half = tokens.shape[1] // 2
    padded = jnp.concatenate(
        [jnp.pad(tokens[:, k * half : (k + 1) * half], ((0, 0), (0, HALF - half))) for k in range(2)],
        axis=1,
    )
    near = send(padded, y_near)
    tokens_l, tokens_r = send(padded, z_up), send(padded, z_down)
    gate_master, up_master, down_master, padded = lax.optimization_barrier(
        (gate_master, up_master, down_master, padded)
    )

    tables = [
        block_maxima(gate_master, *gate_at, D, FF),
        block_maxima(up_master, *gate_at, D, FF),
        block_maxima(down_master, *down_at, FF, D),
    ]
    rows = D // BLOCK + 12
    columns = FF // BLOCK + 56
    pad = lambda a: jnp.pad(a, ((0, rows - a.shape[0]), (0, columns - a.shape[1])))
    table = jnp.concatenate([pad(tables[0]), pad(tables[1]), pad(tables[2].T)])

    def step(table, target):
        return jnp.maximum(table, send(table, target))

    table = step(table, other_core)
    table = step(table, lambda y, x, core, z: (y, x ^ 1, core, z))
    gate_up = jnp.concatenate(
        [
            rollout(gate_master, table[:rows], *gate_at),
            rollout(up_master, table[rows : 2 * rows], *gate_at),
        ],
        axis=1,
    )
    every = step(table, lambda y, x, core, z: (y, x, core, z ^ 1))
    gate_up, every = lax.optimization_barrier((gate_up, every))
    near, tokens_l, tokens_r = lax.optimization_barrier((near, tokens_l, tokens_r))
    down_table = every
    near_l, near_r = send(near, z_up), send(near, z_down)
    tokens_l, near_r = after(tokens_l, near_l), after(near_r, near_l)
    tokens_ll, near_rr = send(tokens_l, z_up), send(near_r, z_down)
    pieces = [padded, near, tokens_l, tokens_r, near_l, near_r, tokens_ll, near_rr]
    down_weight = rollout(down_master, down_table[2 * rows : 3 * rows].T, *down_at)
    pairs = []

    def swap(blocks, *before):
        blocks = [after(block, *before) for block in blocks]
        for n in range(0, len(blocks), 2):
            pair = jnp.stack(blocks[n : n + 2])
            pairs.extend((pair, send(pair, other_core)))

    down_block = send(after(down_weight.T, tokens_ll, near_rr), to_ff_group)
    every = step(after(every, near_l, near_r), y_near)

    down_far = None

    def between(blocks):
        nonlocal down_far
        swap(blocks[:2])
        down_far = send(after(down_block, pairs[1]), y_far)
        return [pairs[1], tokens_ll, near_rr]

    far = send(gate_up, y_far)
    blocks = ring(gate_up, far, x_up, x_down, (near_l, near_r), between)
    swap(blocks[2:4], blocks[4], blocks[5], down_far, every)
    swap(blocks[4:6])

    steps = jnp.array([dy + 4 * (dx % 4) for dy, dx in ORDER] + [0] * 8, jnp.int32)
    chip_y, chip_x = (steps % 4) ^ (y_hi ^ y_lo), (steps // 4 + x - z + 4) % 4
    info = jnp.where(
        chip_x == 0,
        chip_y,
        jnp.where(chip_x == 2, 6 + chip_y, 2 + 2 * chip_y + jnp.where(chip_x == 1, 1, 0)),
    )
    info = jnp.where(jnp.arange(16) == 8, core, info)

    down_pair = jnp.stack([down_block, down_far])
    down_theirs = send(down_pair, other_core)
    pairs[0] = after(pairs[0], down_theirs)
    early = token_sum(info, pieces, 0, pairs)
    early, own_ll, far_rr = lax.optimization_barrier((early, blocks[6], blocks[7]))
    every = step(after(every, early), lambda y, x, core, z: (y, x, core, z ^ 2))
    last = jnp.stack([own_ll, far_rr])
    last = [last, send(last, other_core)]
    down_block, down_far = after(down_block, own_ll), after(down_far, own_ll)
    own_l, own_r = send(down_block, x_up), send(down_block, x_down)
    far_l, far_r = send(down_far, x_up), send(down_far, x_down)
    hidden = token_sum(info, pieces, 6, last, after(early, every), last=True)

    parts = []

    def sums(mine, *before):
        mine = jnp.stack(mine) if parts else down_pair
        theirs = send(mine, other_core) if parts else down_theirs
        terms = down_terms(info, hidden, mine, theirs)
        for term in terms:
            parts.append(send(after(term, *before), to_chunk(*ORDER[len(parts)])))
        return terms

    every = step(every, y_far)
    terms = sums((), far_l, far_r, every)
    terms = sums([after(own_l, *terms), own_r])
    own_l, far_r, *_ = lax.optimization_barrier((own_l, far_r, far_l, *parts[:2], *terms))
    own_ll, far_rr = send(own_l, x_up), send(far_r, x_down)
    terms = sums([far_l, after(far_r, *terms)])
    terms = sums([own_ll, after(far_rr, *terms, *parts[2:4])])
    every = step(after(every, *terms), lambda y, x, core, z: (y, x ^ 2, core, z))
    log_amax = jnp.log(
        jnp.stack([every[k * rows : k * rows + D // BLOCK, : FF // BLOCK] for k in range(3)]) + EPS
    )
    total = sum(part.astype(jnp.float32) for part in parts)
    return total.astype(jnp.bfloat16).T, log_amax


def solution(mesh):
    return jax.shard_map(
        on_device,
        mesh=mesh,
        in_specs=(P("fsdp", "tp"), P("fsdp", "tp"), P("fsdp", "tp"), P("fsdp", "tp")),
        out_specs=(P("fsdp", "tp"), P()),
        check_vma=False,
    )
```

```python
import functools

import jax
import jax.numpy as jnp
from jax import lax
from jax.experimental import pallas as pl
from jax.experimental.pallas import tpu as pltpu
from jax.sharding import PartitionSpec as P

D = 3584
FF = 9216
BLOCK = 128

FP8_MAX = 448.0
EPS = 1e-06
SMALLEST_NORMAL = 2.0 ** (-6)
AXES = ("fsdp", "tp")
VMEM_LIMIT = 60 * 1024 * 1024
TILE = 256
HALF = 256
FREE = pl.CostEstimate(flops=0, bytes_accessed=0, transcendentals=0)


def snapped(value):
    magnitude = jnp.abs(value)
    exponent = jnp.floor(jnp.log2(jnp.maximum(magnitude, SMALLEST_NORMAL)))
    step_size = jnp.exp2(exponent - 3.0)
    return jnp.sign(value) * step_size * jnp.floor(magnitude / step_size + 0.5)


def place(y, x, core, z):
    y, x, z = y % 4, x % 4, z % 4
    return (((y // 2) * 4 + x) * 2 + core) * 8 + (y % 2) * 4 + z


def send(array, target):
    pairs = [
        (place(y, x, core, z), place(*target(y, x, core, z)))
        for y in range(4)
        for x in range(4)
        for core in range(2)
        for z in range(4)
    ]
    return lax.ppermute(array, AXES, pairs)


def x_up(y, x, core, z):
    return y, x + 1, core, z


def x_down(y, x, core, z):
    return y, x - 1, core, z


def z_up(y, x, core, z):
    return y, x, core, z + 1


def z_down(y, x, core, z):
    return y, x, core, z - 1


def y_near(y, x, core, z):
    return y ^ 1, x, core, z


def y_far(y, x, core, z):
    return y + 2, x, core, z


def other_core(y, x, core, z):
    return y, x, 1 - core, z


def to_ff_group(y, x, core, z):
    y_hi, y_lo = y // 2, y % 2
    across = y_lo ^ y_hi
    return across * 2 + y_hi, z - x - 2 * across, core, x


def to_chunk(dy, dx):
    def target(y, x, core, z):
        y_hi, y_lo = y // 2, y % 2
        across = y_hi ^ dy
        return y_hi * 2 + (y_lo ^ across), x, core, z + x + dx + 2 * across

    return target


def block_maxima(local, row_start, column_start, rows, columns):
    height, breadth = local.shape
    span_rows = (height - 1) // BLOCK + 2
    span_columns = (breadth - 1) // BLOCK + 2
    magnitude = jnp.abs(local)
    which_row = (row_start % BLOCK + jnp.arange(height, dtype=jnp.int32)) // BLOCK
    by_row = jnp.stack(
        [
            jnp.max(jnp.where((which_row == k)[:, None], magnitude, 0.0), axis=0)
            for k in range(span_rows)
        ]
    )
    which_column = (column_start % BLOCK + jnp.arange(breadth, dtype=jnp.int32)) // BLOCK
    pick = which_column[None, :] == jnp.arange(span_columns, dtype=jnp.int32)[:, None]
    part = jnp.max(jnp.where(pick[None], by_row[:, None, :], 0.0), axis=2)
    table = jnp.zeros((rows // BLOCK + span_rows, columns // BLOCK + span_columns), jnp.float32)
    return lax.dynamic_update_slice(table, part, (row_start // BLOCK, column_start // BLOCK))


def spread(scales, row_start, height, column_start, breadth):
    span_rows = (height - 1) // BLOCK + 2
    span_columns = (breadth - 1) // BLOCK + 2
    near = lax.dynamic_slice(
        scales, (row_start // BLOCK, column_start // BLOCK), (span_rows, span_columns)
    )
    which_row = (row_start % BLOCK + jnp.arange(height, dtype=jnp.int32)) // BLOCK
    which_column = (column_start % BLOCK + jnp.arange(breadth, dtype=jnp.int32)) // BLOCK
    wide = jnp.zeros((span_rows, breadth), jnp.float32)
    for k in range(span_columns):
        wide = jnp.where((which_column == k)[None, :], near[:, k : k + 1], wide)
    full = jnp.zeros((height, breadth), jnp.float32)
    for k in range(span_rows):
        full = jnp.where((which_row == k)[:, None], wide[k : k + 1, :], full)
    return full


def rollout(master, table, row_start, column_start):
    height, breadth = master.shape
    scale = spread((table + EPS) / FP8_MAX, row_start, height, column_start, breadth)
    return (snapped(master / scale) * scale).astype(jnp.bfloat16)


ORDER = ((0, 0), (1, 0), (0, -1), (0, 1), (1, -1), (1, 1), (0, 2), (1, 2))


def after(array, *others):
    return lax.optimization_barrier((array, *others))[0]


def ring(own, far, up, down, others, between):
    own_l, own_r = send(own, up), send(own, down)
    far = after(far, own_l, own_r, *others)
    far_l, far_r = send(far, up), send(far, down)
    others = between([own, far, own_l, own_r])
    own_l, far_r = after(own_l, far_l, *others), after(far_r, far_l, *others)
    own_ll, far_rr = send(own_l, up), send(far_r, down)
    return [own, far, own_l, own_r, far_l, far_r, own_ll, far_rr]


def token_kernel(count, first, has_before, last, info, *refs):
    pieces, refs = refs[:8], list(refs[8:])
    before = refs.pop(0) if has_before else None
    blocks, (out, wide, scratch, wide_sems, sems) = refs[:count], refs[count:]
    blocks = [blocks[n // 4 * 2 + n % 2].at[n // 2 % 2] for n in range(2 * count)]
    count = len(blocks)
    height = blocks[0].shape[0]

    def block_copy(n):
        rows = pl.ds(n * HALF, height)
        return pltpu.make_async_copy(blocks[n], scratch.at[rows, :], sems.at[n])

    def token_copy(n, piece=0):
        return pltpu.make_async_copy(pieces[piece], wide.at[n], wide_sems.at[n])

    def rows_of(m, n):
        start = pl.multiple_of(m * TILE, TILE)
        low, high = wide[n, pl.ds(start, TILE), :HALF], wide[n, pl.ds(start, TILE), HALF:]
        swapped = info[8] == 1
        return jnp.where(swapped, high, low), jnp.where(swapped, low, high)

    def finish(total):
        if has_before:
            total += before[...]
        if last:
            middle = total.shape[1] // 2
            gate = total[:, :middle]
            total = gate / (1.0 + jnp.exp(-gate)) * total[:, middle:]
        out[...] = total.astype(out.dtype)

    m = pl.program_id(0)

    @pl.when(m == 0)
    def _():
        for n in range(count // 2):
            for piece in range(len(pieces)):

                @pl.when(info[first + n] == piece)
                def _():
                    token_copy(n, piece).start()

            block_copy(2 * n).start()
            block_copy(2 * n + 1).start()
        for n in range(count):
            scratch[n * HALF + height : (n + 1) * HALF, :] = jnp.zeros(
                (HALF - height, scratch.shape[1]), scratch.dtype
            )
        for n in range(count // 2):
            token_copy(n).wait()
            block_copy(2 * n).wait()
            block_copy(2 * n + 1).wait()

    rows = jnp.concatenate([part for n in range(count // 2) for part in rows_of(m, n)], axis=1)
    finish(jnp.dot(rows, scratch[...], preferred_element_type=jnp.float32))


def token_sum(info, tokens, first, blocks, before=None, last=False):
    rows, columns = tokens[0].shape[0], blocks[0].shape[2]
    count = 2 * len(blocks)
    width = columns // 2 if last else columns

    def tile(width):
        return pl.BlockSpec((TILE, width), lambda m, info: (m, 0))

    return pl.pallas_call(
        functools.partial(token_kernel, len(blocks), first, before is not None, last),
        out_shape=jax.ShapeDtypeStruct((rows, width), jnp.bfloat16 if last else jnp.float32),
        grid_spec=pltpu.PrefetchScalarGridSpec(
            num_scalar_prefetch=1,
            grid=(rows // TILE,),
            in_specs=[pl.BlockSpec(memory_space=pl.ANY)] * 8
            + ([] if before is None else [tile(columns)])
            + [pl.BlockSpec(memory_space=pl.ANY)] * len(blocks),
            out_specs=tile(width),
            scratch_shapes=[
                pltpu.VMEM((count // 2, rows, 2 * HALF), jnp.bfloat16),
                pltpu.VMEM((count * HALF, columns), jnp.bfloat16),
                pltpu.SemaphoreType.DMA((count // 2,)),
                pltpu.SemaphoreType.DMA((count,)),
            ],
        ),
        compiler_params=pltpu.CompilerParams(
            vmem_limit_bytes=VMEM_LIMIT // 3 if last else VMEM_LIMIT
        ),
        cost_estimate=FREE,
    )(info, *tokens, *([] if before is None else [before]), *blocks)


def vmem(n):
    return [pl.BlockSpec(memory_space=pltpu.VMEM)] * n


def down_kernel(info, hidden, mine, theirs, *outs):
    for n, out in enumerate(outs):
        low = jnp.where(info[8] == 0, mine[n], theirs[n])
        high = jnp.where(info[8] == 0, theirs[n], mine[n])
        out[...] = lax.dot_general(
            jnp.concatenate([low, high], axis=1),
            hidden[...],
            (((1,), (1,)), ((), ())),
            preferred_element_type=jnp.float32,
        ).astype(out.dtype)


def down_terms(info, hidden, mine, theirs):
    rows, depth = hidden.shape
    count, columns, _ = mine.shape
    return pl.pallas_call(
        down_kernel,
        out_shape=[jax.ShapeDtypeStruct((columns, rows), jnp.bfloat16)] * count,
        in_specs=[pl.BlockSpec(memory_space=pltpu.SMEM)] + vmem(3),
        out_specs=vmem(count),
        compiler_params=pltpu.CompilerParams(vmem_limit_bytes=VMEM_LIMIT // 3),
        cost_estimate=pl.CostEstimate(
            flops=4 * rows * columns * depth, bytes_accessed=12 * rows * columns, transcendentals=0
        ),
    )(info, hidden, mine, theirs)


def on_device(tokens, gate_master, up_master, down_master):
    fsdp_place = lax.axis_index("fsdp")
    tp_place = lax.axis_index("tp")
    core = fsdp_place % 2
    y_hi, x = fsdp_place // 8, (fsdp_place // 2) % 4
    y_lo, z = tp_place // 4, tp_place % 4
    gate_height, gate_breadth = gate_master.shape
    down_height, down_breadth = down_master.shape
    gate_at = (fsdp_place * gate_height, tp_place * gate_breadth)
    down_at = (fsdp_place * down_height, tp_place * down_breadth)

    half = tokens.shape[1] // 2
    padded = jnp.concatenate(
        [jnp.pad(tokens[:, k * half : (k + 1) * half], ((0, 0), (0, HALF - half))) for k in range(2)],
        axis=1,
    )
    near = send(padded, y_near)
    tokens_l, tokens_r = send(padded, z_up), send(padded, z_down)
    gate_master, up_master, down_master, padded = lax.optimization_barrier(
        (gate_master, up_master, down_master, padded)
    )

    tables = [
        block_maxima(gate_master, *gate_at, D, FF),
        block_maxima(up_master, *gate_at, D, FF),
        block_maxima(down_master, *down_at, FF, D),
    ]
    rows = D // BLOCK + 12
    columns = FF // BLOCK + 56
    pad = lambda a: jnp.pad(a, ((0, rows - a.shape[0]), (0, columns - a.shape[1])))
    table = jnp.concatenate([pad(tables[0]), pad(tables[1]), pad(tables[2].T)])

    def step(table, target):
        return jnp.maximum(table, send(table, target))

    table = step(table, other_core)
    table = step(table, lambda y, x, core, z: (y, x ^ 1, core, z))
    gate_up = jnp.concatenate(
        [
            rollout(gate_master, table[:rows], *gate_at),
            rollout(up_master, table[rows : 2 * rows], *gate_at),
        ],
        axis=1,
    )
    every = step(table, lambda y, x, core, z: (y, x, core, z ^ 1))
    gate_up, every = lax.optimization_barrier((gate_up, every))
    near, tokens_l, tokens_r = lax.optimization_barrier((near, tokens_l, tokens_r))
    down_table = every
    near_l, near_r = send(near, z_up), send(near, z_down)
    tokens_l, near_r = after(tokens_l, near_l), after(near_r, near_l)
    tokens_ll, near_rr = send(tokens_l, z_up), send(near_r, z_down)
    pieces = [padded, near, tokens_l, tokens_r, near_l, near_r, tokens_ll, near_rr]
    down_weight = rollout(down_master, down_table[2 * rows : 3 * rows].T, *down_at)
    pairs = []

    def swap(blocks, *before):
        blocks = [after(block, *before) for block in blocks]
        for n in range(0, len(blocks), 2):
            pair = jnp.stack(blocks[n : n + 2])
            pairs.extend((pair, send(pair, other_core)))

    down_block = send(after(down_weight.T, near_l, near_r), to_ff_group)
    every = step(after(every, near_l, near_r), y_near)

    down_far = None

    def between(blocks):
        nonlocal down_far
        swap(blocks[:2])
        down_far = send(after(down_block, pairs[1]), y_far)
        return [pairs[1], tokens_ll, near_rr]

    far = send(gate_up, y_far)
    blocks = ring(gate_up, far, x_up, x_down, (near_l, near_r, down_block, every), between)
    swap(blocks[2:4], blocks[4], blocks[5], down_far)
    swap(blocks[4:6])

    steps = jnp.array([dy + 4 * (dx % 4) for dy, dx in ORDER] + [0] * 8, jnp.int32)
    chip_y, chip_x = (steps % 4) ^ (y_hi ^ y_lo), (steps // 4 + x - z + 4) % 4
    info = jnp.where(
        chip_x == 0,
        chip_y,
        jnp.where(chip_x == 2, 6 + chip_y, 2 + 2 * chip_y + jnp.where(chip_x == 1, 1, 0)),
    )
    info = jnp.where(jnp.arange(16) == 8, core, info)

    down_pair = jnp.stack([down_block, down_far])
    down_theirs = send(down_pair, other_core)
    pairs[0] = after(pairs[0], down_theirs)
    early = token_sum(info, pieces, 0, pairs)
    early, own_ll, far_rr = lax.optimization_barrier((early, blocks[6], blocks[7]))
    every = step(after(every, early), lambda y, x, core, z: (y, x, core, z ^ 2))
    last = jnp.stack([own_ll, far_rr])
    last = [last, send(last, other_core)]
    down_block, down_far = after(down_block, own_ll), after(down_far, own_ll)
    own_l, own_r = send(down_block, x_up), send(down_block, x_down)
    far_l, far_r = send(down_far, x_up), send(down_far, x_down)
    hidden = token_sum(info, pieces, 6, last, after(early, every), last=True)

    parts = []

    def sums(mine, *before):
        mine = jnp.stack(mine) if parts else down_pair
        theirs = send(mine, other_core) if parts else down_theirs
        terms = down_terms(info, hidden, mine, theirs)
        for term in terms:
            parts.append(send(after(term, *before), to_chunk(*ORDER[len(parts)])))
        return terms

    every = step(every, y_far)
    terms = sums((), far_l, far_r, every)
    terms = sums([after(own_l, *terms), own_r])
    own_l, far_r, *_ = lax.optimization_barrier((own_l, far_r, far_l, *parts[:2], *terms))
    own_ll, far_rr = send(own_l, x_up), send(far_r, x_down)
    terms = sums([far_l, after(far_r, *terms)])
    terms = sums([own_ll, after(far_rr, *terms)], *parts[2:4])
    every = step(after(every, *terms), lambda y, x, core, z: (y, x ^ 2, core, z))
    log_amax = jnp.log(
        jnp.stack([every[k * rows : k * rows + D // BLOCK, : FF // BLOCK] for k in range(3)]) + EPS
    )
    total = sum(part.astype(jnp.float32) for part in parts)
    return total.astype(jnp.bfloat16).T, log_amax


def solution(mesh):
    return jax.shard_map(
        on_device,
        mesh=mesh,
        in_specs=(P("fsdp", "tp"), P("fsdp", "tp"), P("fsdp", "tp"), P("fsdp", "tp")),
        out_specs=(P("fsdp", "tp"), P()),
        check_vma=False,
    )
```
